512 devices in a mesh: rows: 32 (over y, x, core), vocab: 16 (over z).
Axes of the slice: x: 4, y: 4, z: 16, core: 2. Of those that a mesh axis runs over, the one named last changes fastest.
Arguments:
- expert_hidden: bfloat16 [128, 8192], P('rows'), may hold values from -400 to 400
- expert_gain: bfloat16 [8192], replicated, may hold values from 0.5 to 1.5
- expert_head: bfloat16 [98304, 8192], P(('rows', 'vocab')), may hold values from -1 to 1
- amateur_hidden: bfloat16 [128, 3584], P('rows'), may hold values from -400 to 400
- amateur_gain: bfloat16 [3584], replicated, may hold values from 0.5 to 1.5
- amateur_head: bfloat16 [98304, 3584], P(('rows', 'vocab')), may hold values from -1 to 1
- live_mask: int32 [98304], P(('rows', 'vocab')), may hold values 0 or 1
- token_ids: int32 [128], replicated, may hold values from 0 to 98303
- plaus_level: int32 [128], replicated, may hold values from 5 to 40
Outputs:
- top_scores: float32 [128, 4], P('rows')
- peak_logprob: float32 [128, 2], P('rows')
- chosen_score: float32 [128], P('rows')
The draws below stay inside these ranges and needn't reach their ends.
All inputs are finite; a program needn't handle non-finite values. No bound on the sum of `live_mask` on one device may be relied on, other than what follows from the above.
Results may differ from the reference program's by a relative error of at most 0.012.
The reference program's roundings to bfloat16 on the way count: a program that leaves them out, or rounds other values in their place, can miss the bound.
Values may be sent and summed in bfloat16 or wider, within the bound.
No kernel may reach another device: no remote copies, remote signals or barrier semaphores. Data moves between devices by JAX's collectives and lax.ppermute only.
A program may use at most 128 MiB of HBM per device.

```python
import math
import jax
import jax.numpy as jnp
from jax import lax

D = 8192
DA = 3584
VOC_DEV = 192
TOP = 4
BEAMS = 128
VOCAB = 98304


pair_count = 6


cluster_count = 4


cluster_width = 5


def drawn_parts(key, tag):
    key = jax.random.fold_in(key, tag)
    beam_key = jax.random.fold_in(key, 1)
    beam_order = jax.random.permutation(beam_key, BEAMS)
    cluster_beams = beam_order[pair_count:pair_count + cluster_count]
    return cluster_beams


def cluster_parts(key):
    key = jax.random.fold_in(key, 31)
    shard_key, start_key, direction_key = jax.random.split(key, 3)
    shards = jax.random.permutation(shard_key, VOCAB // VOC_DEV)[:cluster_count]
    starts = shards * VOC_DEV + jax.random.randint(start_key, (cluster_count,), 0, VOC_DEV - cluster_width + 1)
    columns = (starts[:, None] + jnp.arange(cluster_width, dtype=jnp.int32)[None, :]).reshape(-1)
    directions = jnp.clip(jax.random.normal(direction_key, (cluster_count, D), jnp.float32), -4.0, 4.0)
    return (columns, directions)


def plant_cluster(head_values, base_values, columns, directions):
    strength = min(120.0, 0.12 * D)
    factors = jnp.tile(1.0 - 0.005 * jnp.arange(cluster_width, dtype=jnp.float32), cluster_count)
    repeated_rows = jnp.repeat(directions, cluster_width, axis=0)
    planted = base_values[columns] / math.sqrt(D) + factors[:, None] * strength * repeated_rows / D
    return head_values.at[columns].set(planted)


def entry_scales(scale_key):
    position = jnp.arange(VOCAB, dtype=jnp.float32) / VOCAB
    spread_part = jnp.exp(jax.random.uniform(scale_key, (VOCAB,), jnp.float32, math.log(0.7), math.log(3.5)))
    return spread_part * (1.0 + 1.5 * position)


def feature_scales(feature_key, row_key, width):
    features = jnp.exp(jax.random.uniform(feature_key, (1, width), jnp.float32, 0.0, math.log(10.0)))
    row_scales = jnp.exp(jax.random.uniform(row_key, (BEAMS, 1), jnp.float32, 0.0, math.log(10.0)))
    return features * row_scales


def draw_expert_head(key, part):
    cluster_columns, cluster_directions = cluster_parts(key)
    key = jax.random.fold_in(key, 21)
    base_key, scale_key = jax.random.split(key)
    scales = entry_scales(scale_key)
    base_values = jnp.clip(jax.random.normal(base_key, (VOCAB, D), jnp.float32), -5.0, 5.0)
    head_values = base_values * scales[:, None] / math.sqrt(D)
    head_values = plant_cluster(head_values, base_values, cluster_columns, cluster_directions)
    return jnp.clip(head_values, -1.0, 1.0).astype(jnp.bfloat16)


def draw_amateur_head(key, part):
    key = jax.random.fold_in(key, 23)
    base_key, scale_key = jax.random.split(key)
    scales = entry_scales(scale_key)
    base_values = jnp.clip(jax.random.normal(base_key, (VOCAB, DA), jnp.float32), -5.0, 5.0)
    return jnp.clip(base_values * scales[:, None] / math.sqrt(DA), -1.0, 1.0).astype(jnp.bfloat16)


def draw_expert_hidden(key, part):
    cluster_beams = drawn_parts(key, 11)
    cluster_columns, cluster_directions = cluster_parts(key)
    key = jax.random.fold_in(key, 22)
    base_key, feature_key, row_key = jax.random.split(key, 3)
    scales = feature_scales(feature_key, row_key, D)
    values = jnp.clip(jax.random.normal(base_key, (BEAMS, D), jnp.float32), -4.0, 4.0) * scales
    values = values.at[cluster_beams].set(cluster_directions)
    return jnp.clip(values, -400.0, 400.0).astype(jnp.bfloat16)


def draw_amateur_hidden(key, part):
    key = jax.random.fold_in(key, 24)
    base_key, feature_key, row_key = jax.random.split(key, 3)
    scales = feature_scales(feature_key, row_key, DA)
    values = jnp.clip(jax.random.normal(base_key, (BEAMS, DA), jnp.float32), -4.0, 4.0) * scales
    return jnp.clip(values, -400.0, 400.0).astype(jnp.bfloat16)


def with_ends(values, key, least, top_value):
    place = [jax.random.randint(jax.random.fold_in(key, axis), (), 0, length) for axis, length in enumerate(values.shape)]
    main_axis = values.shape.index(max(values.shape))
    next_to = place[:main_axis] + [(place[main_axis] + 1) % values.shape[main_axis]] + place[main_axis + 1:]
    return values.at[tuple(place)].set(least).at[tuple(next_to)].set(top_value)


def setup_inputs(seed: int = 0) -> dict:
    key_of = jax.random.split(jax.random.key(seed), 10)
    return {
        "expert_hidden": draw_expert_hidden(jax.random.fold_in(key_of[9], 71), 0),
        "expert_gain": jnp.clip(1.0 + 0.1 * jax.random.normal(key_of[1], (D,), jnp.float32), 0.5, 1.5).astype(jnp.bfloat16),
        "expert_head": draw_expert_head(jax.random.fold_in(key_of[9], 71), 0),
        "amateur_hidden": draw_amateur_hidden(jax.random.fold_in(key_of[9], 71), 0),
        "amateur_gain": jnp.clip(1.0 + 0.1 * jax.random.normal(key_of[4], (DA,), jnp.float32), 0.5, 1.5).astype(jnp.bfloat16),
        "amateur_head": draw_amateur_head(jax.random.fold_in(key_of[9], 71), 0),
        "live_mask": with_ends((jax.random.randint(key_of[6], (VOCAB,), 0, 8) < 7).astype(jnp.int32), jax.random.fold_in(key_of[6], 1), 0, 1),
        "token_ids": with_ends(jax.random.randint(key_of[7], (BEAMS,), 0, VOCAB), jax.random.fold_in(key_of[7], 1), 0, VOCAB - 1).astype(jnp.int32),
        "plaus_level": with_ends(jax.random.randint(key_of[8], (BEAMS,), 5, 41), jax.random.fold_in(key_of[8], 1), 5, 40).astype(jnp.int32),
    }


masked_floor = -1e+30
penalty_slope = 2.0
norm_epsilon = 1e-06

def normed_rows(row_block, gain):
    values = row_block.astype(jnp.float32)
    inverse_rms = lax.rsqrt(lax.optimization_barrier(jnp.mean(values * values, axis=-1, keepdims=True)) + norm_epsilon)
    return (values * inverse_rms * gain.astype(jnp.float32)).astype(jnp.bfloat16)

def head_product(normed, head):
    return lax.dot_general(normed, head, (((1,), (1,)), ((), ())), preferred_element_type=jnp.float32)

def contrast_scores(logits_e, logits_a, log_total_e, log_total_a, peak_e, alpha_gap):
    logprob_e = logits_e - log_total_e[:, None]
    logprob_a = logits_a - log_total_a[:, None]
    cut_value = peak_e - log_total_e - alpha_gap
    return logprob_e - logprob_a - penalty_slope * jnp.maximum(cut_value[:, None] - logprob_e, 0.0)

def reference(expert_hidden, expert_gain, expert_head, amateur_hidden, amateur_gain, amateur_head, live_mask, token_ids, plaus_level):
    logits_e = head_product(normed_rows(expert_hidden, expert_gain), expert_head)
    logits_a = head_product(normed_rows(amateur_hidden, amateur_gain), amateur_head)
    live_cols = live_mask[None, :] == 1
    held_e = jnp.where(live_cols, logits_e, masked_floor)
    held_a = jnp.where(live_cols, logits_a, masked_floor)
    peak_e = lax.optimization_barrier(jnp.max(held_e, axis=1))
    peak_a = lax.optimization_barrier(jnp.max(held_a, axis=1))
    log_total_e = peak_e + jnp.log(lax.optimization_barrier(jnp.sum(jnp.exp(held_e - peak_e[:, None]), axis=1)))
    log_total_a = peak_a + jnp.log(lax.optimization_barrier(jnp.sum(jnp.exp(held_a - peak_a[:, None]), axis=1)))
    alpha_gap = plaus_level.astype(jnp.float32) * 0.1
    score_table = contrast_scores(logits_e, logits_a, log_total_e, log_total_a, peak_e, alpha_gap)
    top_scores = lax.top_k(jnp.where(live_cols, score_table, masked_floor), TOP)[0]
    peak_logprob = jnp.stack([peak_e - log_total_e, peak_a - log_total_a], axis=1)
    chosen_score = jnp.take_along_axis(score_table, token_ids.astype(jnp.int32)[:, None], axis=1)[:, 0]
    return (top_scores, peak_logprob, chosen_score)
```

```python
import functools

import jax
import jax.numpy as jnp
from jax import lax
from jax.experimental import pallas as pl
from jax.experimental.pallas import tpu as pltpu
from jax.sharding import PartitionSpec as P

TOP = 4
NY, NX, NC = 4, 4, 2

masked_floor = -1e30
dead_below = -5e29
penalty_slope = 2.0
norm_epsilon = 1e-06

VMEM = pl.BlockSpec(memory_space=pltpu.VMEM)
SMEM = pl.BlockSpec(memory_space=pltpu.SMEM)
PARAMS = pltpu.CompilerParams(vmem_limit_bytes=40 * 1024 * 1024)


def row_of(y, x, c):
    return ((y % NY) * NX + x % NX) * NC + c % NC


def fetch(block, dy, dx, dc):
    pairs = [
        (row_of(y + dy, x + dx, c + dc), row_of(y, x, c))
        for y in range(NY)
        for x in range(NX)
        for c in range(NC)
    ]
    return lax.ppermute(block, "rows", pairs)


def norm_kernel(core_ref, he_ref, ge_ref, ha_ref, ga_ref, mine_ref, other_ref):
    def normed(values, gain):
        values = values.astype(jnp.float32)
        mean = jnp.mean(values * values, axis=-1, keepdims=True)
        return values * lax.rsqrt(mean + norm_epsilon) * gain.astype(jnp.float32)

    e = normed(he_ref[...], ge_ref[...])
    a = normed(ha_ref[...], ga_ref[...])
    qe, qa = e.shape[1] // 4, a.shape[1] // 4
    first = core_ref[0] == 0
    for p in range(2):
        for low, high, out in ((p, 2 + p, mine_ref), (2 + p, p, other_ref)):
            part_e = jnp.where(first, e[:, low * qe:(low + 1) * qe], e[:, high * qe:(high + 1) * qe])
            part_a = jnp.where(first, a[:, low * qa:(low + 1) * qa], a[:, high * qa:(high + 1) * qa])
            out[p, :, 0:qe] = part_e.astype(jnp.bfloat16)
            out[p, :, qe:qe + qa] = part_a.astype(jnp.bfloat16)


def logits_kernel(pos_ref, mine_ref, recv_ref, he_ref, ha_ref, live_ref, ids_ref, out_ref, acc_ref):
    y, x, c, base = pos_ref[0], pos_ref[1], pos_ref[2], pos_ref[3]
    width = he_ref.shape[0]
    beams = mine_ref.shape[0] // 2
    qe, qa = he_ref.shape[1] // 4, ha_ref.shape[1] // 4
    dims = (((1,), (1,)), ((), ()))
    for p in range(2):
        rows = slice(p * beams, (p + 1) * beams)
        for model, head, low, size in ((0, he_ref, 0, qe), (1, ha_ref, qe, qa)):
            total = None
            for part, core in ((mine_ref, c), (recv_ref, 1 - c)):
                columns = pl.ds(pl.multiple_of((2 * core + p) * size, 128), size)
                product = lax.dot_general(
                    part[rows, low:low + size], head[:, columns], dims,
                    preferred_element_type=jnp.float32,
                )
                total = product if total is None else total + product
            acc_ref[model, p] = total
    live = live_ref[...] == 1
    positions = base + lax.broadcasted_iota(jnp.int32, (1, width), 1)
    for ky in range(NY):
        for kx in range(NX):
            chip = lax.rem(y + ky, NY) * NX + lax.rem(x + kx, NX)
            hits = ids_ref[chip] == positions
            for model in range(2):
                p_row, q_row = (ky * NX + kx) * 8, (kx * NY + ky) * 8
                logits = acc_ref[model, 0, p_row:p_row + 8, :] + acc_ref[model, 1, q_row:q_row + 8, :]
                held = jnp.where(live, logits, masked_floor)
                pick = jnp.sum(jnp.where(hits, logits, 0.0), axis=1, keepdims=True)
                pick = jnp.broadcast_to(pick, (8, 256 - width))
                for core in range(NC):
                    at = 256 * model
                    own = slice(4 * core, 4 * core + 4)
                    out_ref[2 * chip + core, :, at:at + width] = held[own]
                    out_ref[2 * chip + core, :, at + width:at + 256] = pick[own]


def lanes_of(columns, shape):
    lane = lax.broadcasted_iota(jnp.int32, shape, len(shape) - 1)
    result = jnp.zeros(shape, jnp.float32)
    for i, column in enumerate(columns):
        result = jnp.where(lane == i, column, result)
    return result


def lane_at(values, i):
    lane = lax.broadcasted_iota(jnp.int32, values.shape, values.ndim - 1)
    return jnp.sum(jnp.where(lane == i, values, 0.0), axis=-1, keepdims=True)


def stats_kernel(width, table_ref, out_ref):
    columns = []
    for model in range(2):
        part = table_ref[:, :, 256 * model:256 * model + 256]
        real = lax.broadcasted_iota(jnp.int32, part.shape, 2) < width
        peak = jnp.max(jnp.max(jnp.where(real, part, masked_floor), axis=0), axis=1, keepdims=True)
        total = jnp.sum(jnp.where(real, jnp.exp(part - peak[None]), 0.0), axis=0)
        total = jnp.sum(total, axis=1, keepdims=True)
        pick = lane_at(jnp.sum(part, axis=0), width)
        columns.append((peak, total, pick))
    (pe, te, ce), (pa, ta, ca) = columns
    out_ref[...] = lanes_of([pe, pa, te, ta, ce, ca], out_ref.shape)


def best_of(levels):
    lane = lax.broadcasted_iota(jnp.int32, levels[0].shape, 1)
    found = []
    for _ in range(TOP):
        top = jnp.max(levels[0], axis=1, keepdims=True)
        found.append(top)
        at = jnp.min(jnp.where(levels[0] == top, lane, lane.shape[1]), axis=1, keepdims=True)
        hit = lane == at
        lower = levels[1:] + [jnp.full_like(levels[0], -jnp.inf)]
        levels = [jnp.where(hit, low, level) for level, low in zip(levels, lower)]
    return found


def sorted_levels(parts):
    levels = [jnp.full_like(parts[0], -jnp.inf)] * TOP
    for part in parts:
        for i in range(TOP):
            levels[i], part = jnp.maximum(levels[i], part), jnp.minimum(levels[i], part)
    return levels


def score_kernel(width, table_ref, stats_ref, gap_ref, best_ref, peaks_ref, chosen_ref):
    stats = stats_ref[...]
    peak_e, peak_a, sum_e, sum_a, pick_e, pick_a = [lane_at(stats, i) for i in range(6)]

    def total_of(peaks, sums):
        peak = jnp.max(peaks, axis=0)
        return peak, peak + jnp.log(jnp.sum(sums * jnp.exp(peaks - peak[None]), axis=0))

    peak_e, log_total_e = total_of(peak_e, sum_e)
    peak_a, log_total_a = total_of(peak_a, sum_a)
    cut = peak_e - log_total_e - gap_ref[...].astype(jnp.float32) * 0.1

    def score(logits_e, logits_a):
        logprob_e = logits_e - log_total_e
        logprob_a = logits_a - log_total_a
        return logprob_e - logprob_a - penalty_slope * jnp.maximum(cut - logprob_e, 0.0)

    peaks_ref[...] = lanes_of([peak_e - log_total_e, peak_a - log_total_a], peaks_ref.shape)
    chosen_ref[...] = score(jnp.sum(pick_e, axis=0), jnp.sum(pick_a, axis=0))
    real = lax.broadcasted_iota(jnp.int32, (table_ref.shape[1], 256), 1) < width
    parts = []
    for source in range(table_ref.shape[0]):
        e = table_ref[source, :, 0:256]
        a = table_ref[source, :, 256:512]
        parts.append(jnp.where(real & (e > dead_below), score(e, a), masked_floor))
    best_ref[...] = lanes_of(best_of(sorted_levels(parts)), best_ref.shape)


def merge_kernel(parts_ref, out_ref):
    shape = parts_ref.shape[1:]
    real = lax.broadcasted_iota(jnp.int32, shape, 1) < TOP
    parts = [jnp.where(real, parts_ref[i], -jnp.inf) for i in range(parts_ref.shape[0])]
    out_ref[...] = lanes_of(best_of(sorted_levels(parts)), out_ref.shape)


def per_device(
    expert_hidden,
    expert_gain,
    expert_head,
    amateur_hidden,
    amateur_gain,
    amateur_head,
    live_mask,
    token_ids,
    plaus_level,
):
    own, depth_e = expert_hidden.shape
    depth_a = amateur_hidden.shape[1]
    width = expert_head.shape[0]
    rows, planes = lax.axis_size("rows"), lax.axis_size("vocab")
    beams = own * rows
    quarter = (depth_e + depth_a) // 4
    row, plane = lax.axis_index("rows"), lax.axis_index("vocab")
    core, x, y = row % NC, row // NC % NX, row // (NC * NX)
    position = jnp.stack([y, x, core, (row * planes + plane) * width]).astype(jnp.int32)
    ids = token_ids.reshape(rows // NC, NC * own, 1)
    gap = lax.dynamic_slice_in_dim(plaus_level, row * own, own, 0).reshape(own, 1)

    piece = jax.ShapeDtypeStruct((2, own, quarter), jnp.bfloat16)
    mine, other = pl.pallas_call(
        norm_kernel,
        out_shape=(piece, piece),
        in_specs=[SMEM] + [VMEM] * 4,
        out_specs=(VMEM, VMEM),
        compiler_params=PARAMS,
        name="norms",
    )(core.astype(jnp.int32).reshape(1), expert_hidden, expert_gain.reshape(1, -1),
      amateur_hidden, amateur_gain.reshape(1, -1))
    recv = fetch(other, 0, 0, 1)
    chip = jnp.where(core == 0, jnp.concatenate([mine, recv], 1), jnp.concatenate([recv, mine], 1))
    p_part, q_part = chip[0], chip[1]
    p_line = jnp.concatenate([p_part] + [fetch(p_part, 0, k, 0) for k in range(1, NX)])
    q_line = jnp.concatenate([q_part] + [fetch(q_part, k, 0, 0) for k in range(1, NY)])
    p_rest = [fetch(p_line, k, 0, 0) for k in range(1, NY)]
    q_rest = [fetch(q_line, 0, k, 0) for k in range(1, NX)]
    half = jnp.concatenate([p_line] + p_rest + [q_line] + q_rest)
    other_half = fetch(half, 0, 0, 1)

    table = pl.pallas_call(
        logits_kernel,
        out_shape=jax.ShapeDtypeStruct((rows, own, 512), jnp.float32),
        in_specs=[SMEM] + [VMEM] * 6,
        out_specs=VMEM,
        scratch_shapes=[pltpu.VMEM((2, 2, beams, width), jnp.float32)],
        compiler_params=PARAMS,
        name="logits",
    )(position, half, other_half, expert_head, amateur_head, live_mask.reshape(1, -1), ids)
    table = lax.all_to_all(table, "rows", 0, 0, tiled=True)

    small = jax.ShapeDtypeStruct((own, 128), jnp.float32)
    stats = pl.pallas_call(
        functools.partial(stats_kernel, width),
        out_shape=small,
        in_specs=[VMEM],
        out_specs=VMEM,
        compiler_params=PARAMS,
        name="stats",
    )(table)
    stats = lax.all_gather(stats, "vocab")
    best, peaks, chosen = pl.pallas_call(
        functools.partial(score_kernel, width),
        out_shape=(
            small,
            jax.ShapeDtypeStruct((own, 2), jnp.float32),
            jax.ShapeDtypeStruct((own, 1), jnp.float32),
        ),
        in_specs=[VMEM] * 3,
        out_specs=(VMEM,) * 3,
        compiler_params=PARAMS,
        name="scores",
    )(table, stats, gap)
    others = [
        lax.ppermute(best, "vocab", [((z + k) % planes, z) for z in range(planes)])
        for k in range(1, planes)
    ]
    top = pl.pallas_call(
        merge_kernel,
        out_shape=jax.ShapeDtypeStruct((own, TOP), jnp.float32),
        in_specs=[VMEM],
        out_specs=VMEM,
        compiler_params=PARAMS,
        name="merge",
    )(jnp.stack([best] + others))
    return top, peaks, chosen.reshape(own)


def solution(mesh):
    in_specs = (
        P("rows", None),
        P(),
        P(("rows", "vocab"), None),
        P("rows", None),
        P(),
        P(("rows", "vocab"), None),
        P(("rows", "vocab")),
        P(),
        P(),
    )
    out_specs = (P("rows", None), P("rows", None), P("rows"))
    return jax.shard_map(
        per_device, mesh=mesh, in_specs=in_specs, out_specs=out_specs, check_vma=False
    )
```

```python
import functools

import jax
import jax.numpy as jnp
from jax import lax
from jax.experimental import pallas as pl
from jax.experimental.pallas import tpu as pltpu
from jax.sharding import PartitionSpec as P

TOP = 4
NC = 2

masked_floor = -1e30
dead_below = -5e29
penalty_slope = 2.0
norm_epsilon = 1e-06

VMEM = pl.BlockSpec(memory_space=pltpu.VMEM)
SMEM = pl.BlockSpec(memory_space=pltpu.SMEM)
PARAMS = pltpu.CompilerParams(vmem_limit_bytes=40 * 1024 * 1024)


def norm_kernel(he_ref, ge_ref, ha_ref, ga_ref, out_ref):
    own, quarters = he_ref.shape[0], []
    for hidden, gains in ((he_ref, ge_ref), (ha_ref, ga_ref)):
        values = hidden[...].astype(jnp.float32)
        gain = gains[...].astype(jnp.float32)
        mean = jnp.mean(values * values, axis=-1, keepdims=True)
        values = values * lax.rsqrt(mean + norm_epsilon)
        chunks = [
            (values[:, 128 * i:128 * i + 128] * gain[i:i + 1, :]).astype(jnp.bfloat16)
            for i in range(values.shape[1] // 128)
        ]
        each = len(chunks) // 4
        quarters.append([chunks[each * q:each * q + each] for q in range(4)])
    for core in range(NC):
        for p in range(2):
            q = 2 * core + p
            for i, chunk in enumerate(quarters[0][q] + quarters[1][q]):
                for dest in range(core, out_ref.shape[0], NC):
                    out_ref[dest, own * p:own * p + own, 128 * i:128 * i + 128] = chunk


def half_logits(core, part_ref, he_ref, ha_ref, model):
    head = (he_ref, ha_ref)[model]
    qe, qa = he_ref.shape[1] // 4, ha_ref.shape[1] // 4
    low, size = ((0, qe), (qe, qa))[model]
    sums = []
    for p in range(2):
        columns = pl.ds(pl.multiple_of((2 * core + p) * size, 128), size)
        sums.append(lax.dot_general(
            part_ref[:, low:low + size], head[:, columns], (((1,), (1,)), ((), ())),
            preferred_element_type=jnp.float32,
        ))
    return sums


def first_kernel(pos_ref, part_ref, he_ref, ha_ref, out_ref):
    for model in range(2):
        for p, total in enumerate(half_logits(pos_ref[0], part_ref, he_ref, ha_ref, model)):
            out_ref[model, p] = total


def second_kernel(pos_ref, part_ref, he_ref, ha_ref, first_ref, live_ref, ids_ref, out_ref, acc_ref):
    width = he_ref.shape[0]
    own = out_ref.shape[1]
    for model in range(2):
        for p, total in enumerate(half_logits(1 - pos_ref[0], part_ref, he_ref, ha_ref, model)):
            acc_ref[model, p] = total + first_ref[model, p]
    live = live_ref[...] == 1
    positions = pos_ref[1] + lax.broadcasted_iota(jnp.int32, (1, width), 1)
    for owner in range(out_ref.shape[0]):
        at = 2 * own * owner
        hits = ids_ref[owner] == positions
        for model in range(2):
            logits = acc_ref[model, 0, at:at + own, :] + acc_ref[model, 1, at + own:at + 2 * own, :]
            pick = jnp.sum(jnp.where(hits, logits, 0.0), axis=1, keepdims=True)
            low = 256 * model
            out_ref[owner, :, low:low + width] = jnp.where(live, logits, masked_floor)
            out_ref[owner, :, low + width:low + 256] = jnp.broadcast_to(pick, (own, 256 - width))


def lanes_of(columns, shape):
    lane = lax.broadcasted_iota(jnp.int32, shape, len(shape) - 1)
    result = jnp.zeros(shape, jnp.float32)
    for i, column in enumerate(columns):
        result = jnp.where(lane == i, column, result)
    return result


def lane_at(values, i):
    lane = lax.broadcasted_iota(jnp.int32, values.shape, values.ndim - 1)
    return jnp.sum(jnp.where(lane == i, values, 0.0), axis=-1, keepdims=True)


def stats_kernel(width, table_ref, out_ref):
    columns = []
    for model in range(2):
        part = table_ref[:, :, 256 * model:256 * model + 256]
        real = lax.broadcasted_iota(jnp.int32, part.shape, 2) < width
        peak = jnp.max(jnp.max(jnp.where(real, part, masked_floor), axis=0), axis=1, keepdims=True)
        total = jnp.sum(jnp.where(real, jnp.exp(part - peak[None]), 0.0), axis=0)
        total = jnp.sum(total, axis=1, keepdims=True)
        pick = lane_at(jnp.sum(part, axis=0), width)
        columns.append((peak, total, pick))
    (pe, te, ce), (pa, ta, ca) = columns
    stats = lanes_of([pe, pa, te, ta, ce, ca], out_ref.shape[1:])
    for plane in range(out_ref.shape[0]):
        out_ref[plane] = stats


def best_of(levels):
    lane = lax.broadcasted_iota(jnp.int32, levels[0].shape, 1)
    found = []
    for _ in range(TOP):
        top = jnp.max(levels[0], axis=1, keepdims=True)
        found.append(top)
        at = jnp.min(jnp.where(levels[0] == top, lane, lane.shape[1]), axis=1, keepdims=True)
        hit = lane == at
        lower = levels[1:] + [jnp.full_like(levels[0], -jnp.inf)]
        levels = [jnp.where(hit, low, level) for level, low in zip(levels, lower)]
    return found


def sorted_levels(parts):
    levels = [jnp.full_like(parts[0], -jnp.inf)] * TOP
    for part in parts:
        for i in range(TOP):
            levels[i], part = jnp.maximum(levels[i], part), jnp.minimum(levels[i], part)
    return levels


def score_kernel(width, table_ref, stats_ref, gap_ref, best_ref, peaks_ref, chosen_ref):
    stats = stats_ref[...]
    peak_e, peak_a, sum_e, sum_a, pick_e, pick_a = [lane_at(stats, i) for i in range(6)]

    def total_of(peaks, sums):
        peak = jnp.max(peaks, axis=0)
        return peak, peak + jnp.log(jnp.sum(sums * jnp.exp(peaks - peak[None]), axis=0))

    peak_e, log_total_e = total_of(peak_e, sum_e)
    peak_a, log_total_a = total_of(peak_a, sum_a)
    cut = peak_e - log_total_e - gap_ref[...].astype(jnp.float32) * 0.1

    def score(logits_e, logits_a):
        logprob_e = logits_e - log_total_e
        logprob_a = logits_a - log_total_a
        return logprob_e - logprob_a - penalty_slope * jnp.maximum(cut - logprob_e, 0.0)

    peaks_ref[...] = lanes_of([peak_e - log_total_e, peak_a - log_total_a], peaks_ref.shape)
    chosen_ref[...] = score(jnp.sum(pick_e, axis=0), jnp.sum(pick_a, axis=0))
    real = lax.broadcasted_iota(jnp.int32, (table_ref.shape[1], 256), 1) < width
    parts = []
    for source in range(table_ref.shape[0]):
        e = table_ref[source, :, 0:256]
        a = table_ref[source, :, 256:512]
        parts.append(jnp.where(real & (e > dead_below), score(e, a), masked_floor))
    best = lanes_of(best_of(sorted_levels(parts)), best_ref.shape[1:])
    for plane in range(best_ref.shape[0]):
        best_ref[plane] = best


def merge_kernel(parts_ref, out_ref):
    shape = parts_ref.shape[1:]
    real = lax.broadcasted_iota(jnp.int32, shape, 1) < TOP
    parts = [jnp.where(real, parts_ref[i], -jnp.inf) for i in range(parts_ref.shape[0])]
    out_ref[...] = lanes_of(best_of(sorted_levels(parts)), out_ref.shape)


def per_device(
    expert_hidden,
    expert_gain,
    expert_head,
    amateur_hidden,
    amateur_gain,
    amateur_head,
    live_mask,
    token_ids,
    plaus_level,
):
    own, depth_e = expert_hidden.shape
    depth_a = amateur_hidden.shape[1]
    width = expert_head.shape[0]
    rows, planes = lax.axis_size("rows"), lax.axis_size("vocab")
    beams = own * rows
    quarter = (depth_e + depth_a) // 4
    row, plane = lax.axis_index("rows"), lax.axis_index("vocab")
    position = jnp.stack([row % NC, (row * planes + plane) * width]).astype(jnp.int32)
    ids = token_ids.reshape(rows, own, 1)
    gap = lax.dynamic_slice_in_dim(plaus_level, row * own, own, 0).reshape(own, 1)

    blocks = pl.pallas_call(
        norm_kernel,
        out_shape=jax.ShapeDtypeStruct((rows, 2 * own, quarter), jnp.bfloat16),
        in_specs=[VMEM] * 4,
        out_specs=VMEM,
        compiler_params=PARAMS,
        name="norms",
    )(expert_hidden, expert_gain.reshape(-1, 128), amateur_hidden, amateur_gain.reshape(-1, 128))
    half = lax.all_to_all(blocks, "rows", 0, 0, tiled=True).reshape(2 * beams, quarter)
    other_half = lax.ppermute(half, "rows", [(r, r ^ 1) for r in range(rows)])
    cost = pl.CostEstimate(
        flops=4 * beams * width * 2 * quarter, bytes_accessed=4 * beams * quarter, transcendentals=0
    )
    first = pl.pallas_call(
        first_kernel,
        out_shape=jax.ShapeDtypeStruct((2, 2, 2 * beams, width), jnp.float32),
        in_specs=[SMEM] + [VMEM] * 3,
        out_specs=VMEM,
        compiler_params=PARAMS,
        cost_estimate=cost,
        name="first_half",
    )(position, half, expert_head, amateur_head)
    table = pl.pallas_call(
        second_kernel,
        out_shape=jax.ShapeDtypeStruct((rows, own, 512), jnp.float32),
        in_specs=[SMEM] + [VMEM] * 6,
        out_specs=VMEM,
        scratch_shapes=[pltpu.VMEM((2, 2, 2 * beams, width), jnp.float32)],
        compiler_params=PARAMS,
        cost_estimate=cost,
        name="second_half",
    )(position, other_half, expert_head, amateur_head, first, live_mask.reshape(1, -1), ids)
    table = lax.all_to_all(table, "rows", 0, 0, tiled=True)

    small = jax.ShapeDtypeStruct((planes, own, 128), jnp.float32)
    stats = pl.pallas_call(
        functools.partial(stats_kernel, width),
        out_shape=small,
        in_specs=[VMEM],
        out_specs=VMEM,
        compiler_params=PARAMS,
        name="stats",
    )(table)
    stats = lax.all_to_all(stats, "vocab", 0, 0, tiled=True)
    best, peaks, chosen = pl.pallas_call(
        functools.partial(score_kernel, width),
        out_shape=(
            small,
            jax.ShapeDtypeStruct((own, 2), jnp.float32),
            jax.ShapeDtypeStruct((own, 1), jnp.float32),
        ),
        in_specs=[VMEM] * 3,
        out_specs=(VMEM,) * 3,
        compiler_params=PARAMS,
        name="scores",
    )(table, stats, gap)
    best = lax.all_to_all(best, "vocab", 0, 0, tiled=True)
    top = pl.pallas_call(
        merge_kernel,
        out_shape=jax.ShapeDtypeStruct((own, TOP), jnp.float32),
        in_specs=[VMEM],
        out_specs=VMEM,
        compiler_params=PARAMS,
        name="merge",
    )(best)
    return top, peaks, chosen.reshape(own)


def solution(mesh):
    in_specs = (
        P("rows", None),
        P(),
        P(("rows", "vocab"), None),
        P("rows", None),
        P(),
        P(("rows", "vocab"), None),
        P(("rows", "vocab")),
        P(),
        P(),
    )
    out_specs = (P("rows", None), P("rows", None), P("rows"))
    return jax.shard_map(
        per_device, mesh=mesh, in_specs=in_specs, out_specs=out_specs, check_vma=False
    )
```

```python
import functools

import jax
import jax.numpy as jnp
from jax import lax
from jax.experimental import pallas as pl
from jax.experimental.pallas import tpu as pltpu
from jax.sharding import PartitionSpec as P

TOP = 4
NEAR = 16
FIRST = 16
NC = 2

masked_floor = -1e30
dead_below = -5e29
penalty_slope = 2.0
norm_epsilon = 1e-06

VMEM = pl.BlockSpec(memory_space=pltpu.VMEM)
SMEM = pl.BlockSpec(memory_space=pltpu.SMEM)
PARAMS = pltpu.CompilerParams(vmem_limit_bytes=40 * 1024 * 1024)


def norm_kernel(he_ref, ge_ref, ha_ref, ga_ref, out_ref):
    own, quarters = he_ref.shape[0], []
    for hidden, gains in ((he_ref, ge_ref), (ha_ref, ga_ref)):
        values = hidden[...].astype(jnp.float32)
        gain = gains[...].astype(jnp.float32)
        mean = jnp.mean(values * values, axis=-1, keepdims=True)
        values = values * lax.rsqrt(mean + norm_epsilon)
        chunks = [
            (values[:, 128 * i:128 * i + 128] * gain[i:i + 1, :]).astype(jnp.bfloat16)
            for i in range(values.shape[1] // 128)
        ]
        each = len(chunks) // 4
        quarters.append([chunks[each * q:each * q + each] for q in range(4)])
    for core in range(NC):
        for p in range(2):
            q = 2 * core + p
            for i, chunk in enumerate(quarters[0][q] + quarters[1][q]):
                for dest in range(core, out_ref.shape[0], NC):
                    out_ref[dest, own * p:own * p + own, 128 * i:128 * i + 128] = chunk


def half_logits(core, part_ref, he_ref, ha_ref, model):
    head = (he_ref, ha_ref)[model]
    qe, qa = he_ref.shape[1] // 4, ha_ref.shape[1] // 4
    low, size = ((0, qe), (qe, qa))[model]
    sums = []
    for p in range(2):
        columns = pl.ds(pl.multiple_of((2 * core + p) * size, 128), size)
        sums.append(lax.dot_general(
            part_ref[:, low:low + size], head[:, columns], (((1,), (1,)), ((), ())),
            preferred_element_type=jnp.float32,
        ))
    return sums


def first_kernel(pos_ref, part_ref, he_ref, ha_ref, out_ref):
    for model in range(2):
        for p, total in enumerate(half_logits(pos_ref[0], part_ref, he_ref, ha_ref, model)):
            out_ref[model, p] = total


def second_kernel(pos_ref, part_ref, he_ref, ha_ref, first_ref, live_ref, ids_ref, out_ref, acc_ref):
    width = he_ref.shape[0]
    own = out_ref.shape[1]
    for model in range(2):
        for p, total in enumerate(half_logits(1 - pos_ref[0], part_ref, he_ref, ha_ref, model)):
            acc_ref[model, p] = total + first_ref[model, p]
    live = live_ref[...] == 1
    positions = pos_ref[1] + lax.broadcasted_iota(jnp.int32, (1, width), 1)
    for owner in range(out_ref.shape[0]):
        at = 2 * own * owner
        hits = ids_ref[owner] == positions
        for model in range(2):
            logits = acc_ref[model, 0, at:at + own, :] + acc_ref[model, 1, at + own:at + 2 * own, :]
            pick = jnp.sum(jnp.where(hits, logits, 0.0), axis=1, keepdims=True)
            low = 256 * model
            out_ref[owner, :, low:low + width] = jnp.where(live, logits, masked_floor)
            out_ref[owner, :, low + width:low + 256] = jnp.broadcast_to(pick, (own, 256 - width))


def lanes_of(columns, shape):
    lane = lax.broadcasted_iota(jnp.int32, shape, len(shape) - 1)
    result = jnp.zeros(shape, jnp.float32)
    for i, column in enumerate(columns):
        result = jnp.where(lane == i, column, result)
    return result


def lane_at(values, i):
    lane = lax.broadcasted_iota(jnp.int32, values.shape, values.ndim - 1)
    return jnp.sum(jnp.where(lane == i, values, 0.0), axis=-1, keepdims=True)


def total_rows(values):
    return jnp.sum(values, axis=1, keepdims=True)


def insert(levels, entry):
    for i, level in enumerate(levels):
        above = entry[0] > level[0]
        levels[i] = tuple(jnp.where(above, new, old) for new, old in zip(entry, level))
        entry = tuple(jnp.where(above, old, new) for new, old in zip(entry, level))


def remove_top(levels, top):
    hit = levels[0][0] == top
    payload = [total_rows(jnp.where(hit, field, 0.0)) for field in levels[0][1:]]
    count = total_rows(jnp.where(hit, 1.0, 0.0))
    last = tuple(jnp.full_like(f, masked_floor) for f in levels[0])
    lower = levels[1:] + [last]
    return payload, count, [
        tuple(jnp.where(hit, new, old) for new, old in zip(low, level))
        for low, level in zip(lower, levels)
    ]


def stats_kernel(width, table_ref, gap_ref, out_ref):
    sources, own = table_ref.shape[0], table_ref.shape[1]
    real = lax.broadcasted_iota(jnp.int32, (own, 256), 1) < width
    columns = []
    for model in range(2):
        parts = [table_ref[i, :, 256 * model:256 * model + 256] for i in range(sources)]
        peak = functools.reduce(jnp.maximum, parts)
        peak = jnp.max(jnp.where(real, peak, masked_floor), axis=1, keepdims=True)
        total = functools.reduce(jnp.add, [jnp.exp(part - peak) for part in parts])
        total = total_rows(jnp.where(real, total, 0.0))
        columns.append((peak, total, lane_at(functools.reduce(jnp.add, parts), width)))
    (pe, te, ce), (pa, ta, ca) = columns
    least = pe - gap_ref[...].astype(jnp.float32) * 0.1
    floor = jnp.full((own, 256), masked_floor, jnp.float32)
    near, rest = [(floor,) * 2] * TOP, [(floor,) * 3] * TOP
    count = jnp.zeros((own, 256), jnp.float32)
    for i in range(sources):
        e, a = table_ref[i, :, 0:256], table_ref[i, :, 256:512]
        live = real & (e > dead_below)
        is_near = live & (e >= least)
        count += jnp.where(is_near, 1.0, 0.0)
        insert(near, (jnp.where(is_near, e, masked_floor), a))
        insert(rest, (jnp.where(live & (e < least), 3.0 * e - a, masked_floor), e, a))
    missing = total_rows(count)
    picked = []
    for _ in range(NEAR):
        top = jnp.max(near[0][0], axis=1, keepdims=True)
        (a,), hits, near = remove_top(near, top)
        found = top > dead_below
        picked.append((jnp.where(found, top, masked_floor), a))
        missing -= jnp.where(found & (hits == 1.0), 1.0, 0.0)
    for _ in range(TOP):
        top = jnp.max(rest[0][0], axis=1, keepdims=True)
        (e, a), hits, rest = remove_top(rest, top)
        found = top > dead_below
        picked.append((jnp.where(found, e, masked_floor), a))
        missing += jnp.where(found & (hits > 1.0), 1.0, 0.0)
    lanes = [pe, pa, te, ta, ce, ca, missing]
    lanes += [jnp.zeros_like(pe)] * (FIRST - len(lanes)) + [e for e, _ in picked]
    lanes += [jnp.zeros_like(pe)] * (64 + FIRST - len(lanes)) + [a for _, a in picked]
    stats = lanes_of(lanes, out_ref.shape[1:])
    for plane in range(out_ref.shape[0]):
        out_ref[plane] = stats


def best_of(levels):
    tops, counts, seen = [], [], 0.0
    for _ in range(TOP):
        top = jnp.max(levels[0], axis=1, keepdims=True)
        hit = levels[0] == top
        seen = seen + total_rows(jnp.where(hit, 1.0, 0.0))
        tops.append(top)
        counts.append(seen)
        lower = levels[1:] + [jnp.full_like(levels[0], -jnp.inf)]
        levels = [jnp.where(hit, low, level) for level, low in zip(levels, lower)]
    found = []
    for i in range(TOP):
        value = tops[-1]
        for top, seen in reversed(list(zip(tops, counts))):
            value = jnp.where(seen > i, top, value)
        found.append(value)
    return found


def sorted_levels(parts):
    levels = [jnp.full_like(parts[0], -jnp.inf)] * TOP
    for part in parts:
        for i in range(TOP):
            levels[i], part = jnp.maximum(levels[i], part), jnp.minimum(levels[i], part)
    return levels


def totals_of(stats_ref, gap_ref):
    stats = stats_ref[...]
    peak_e, peak_a, sum_e, sum_a = [lane_at(stats, i) for i in range(4)]

    def total_of(peaks, sums):
        peak = jnp.max(peaks, axis=0)
        return peak, peak + jnp.log(jnp.sum(sums * jnp.exp(peaks - peak[None]), axis=0))

    peak_e, log_total_e = total_of(peak_e, sum_e)
    peak_a, log_total_a = total_of(peak_a, sum_a)
    cut = peak_e - log_total_e - gap_ref[...].astype(jnp.float32) * 0.1

    def score(logits_e, logits_a):
        logprob_e = logits_e - log_total_e
        logprob_a = logits_a - log_total_a
        return logprob_e - logprob_a - penalty_slope * jnp.maximum(cut - logprob_e, 0.0)

    return [peak_e - log_total_e, peak_a - log_total_a], score


def finish_kernel(stats_ref, gap_ref, top_ref, peaks_ref, chosen_ref, lacking_ref):
    peaks, score = totals_of(stats_ref, gap_ref)
    stats = stats_ref[...]
    peaks_ref[...] = lanes_of(peaks, peaks_ref.shape)
    chosen_ref[...] = score(jnp.sum(lane_at(stats, 4), axis=0), jnp.sum(lane_at(stats, 5), axis=0))
    lane = lax.broadcasted_iota(jnp.int32, stats.shape[1:], 1)
    is_candidate = (lane >= FIRST) & (lane < FIRST + NEAR + TOP)
    parts, lacking = [], jnp.zeros(stats.shape[1:], jnp.float32)
    for plane in range(stats.shape[0]):
        e, a = stats[plane], pltpu.roll(stats[plane], 64, 1)
        value = jnp.where(e > dead_below, score(e, a), masked_floor)
        parts.append(jnp.where(is_candidate, value, -jnp.inf))
        lacking = jnp.maximum(lacking, jnp.where(lane == 6, e, 0.0))
    top_ref[...] = lanes_of(best_of(sorted_levels(parts)), top_ref.shape)
    lacking_ref[0] = jnp.where(jnp.max(lacking) > 0.0, 1, 0).astype(jnp.int32)


def score_kernel(width, table_ref, stats_ref, gap_ref, best_ref):
    _, score = totals_of(stats_ref, gap_ref)
    real = lax.broadcasted_iota(jnp.int32, (table_ref.shape[1], 256), 1) < width
    parts = []
    for source in range(table_ref.shape[0]):
        e = table_ref[source, :, 0:256]
        a = table_ref[source, :, 256:512]
        parts.append(jnp.where(real & (e > dead_below), score(e, a), masked_floor))
    best = lanes_of(best_of(sorted_levels(parts)), best_ref.shape[1:])
    for plane in range(best_ref.shape[0]):
        best_ref[plane] = best


def merge_kernel(parts_ref, out_ref):
    shape = parts_ref.shape[1:]
    real = lax.broadcasted_iota(jnp.int32, shape, 1) < TOP
    parts = [jnp.where(real, parts_ref[i], -jnp.inf) for i in range(parts_ref.shape[0])]
    out_ref[...] = lanes_of(best_of(sorted_levels(parts)), out_ref.shape)


def per_device(
    expert_hidden,
    expert_gain,
    expert_head,
    amateur_hidden,
    amateur_gain,
    amateur_head,
    live_mask,
    token_ids,
    plaus_level,
):
    own, depth_e = expert_hidden.shape
    depth_a = amateur_hidden.shape[1]
    width = expert_head.shape[0]
    rows, planes = lax.axis_size("rows"), lax.axis_size("vocab")
    beams = own * rows
    quarter = (depth_e + depth_a) // 4
    row, plane = lax.axis_index("rows"), lax.axis_index("vocab")
    position = jnp.stack([row % NC, (row * planes + plane) * width]).astype(jnp.int32)
    ids = token_ids.reshape(rows, own, 1)
    gap = lax.dynamic_slice_in_dim(plaus_level, row * own, own, 0).reshape(own, 1)

    blocks = pl.pallas_call(
        norm_kernel,
        out_shape=jax.ShapeDtypeStruct((rows, 2 * own, quarter), jnp.bfloat16),
        in_specs=[VMEM] * 4,
        out_specs=VMEM,
        compiler_params=PARAMS,
        name="norms",
    )(expert_hidden, expert_gain.reshape(-1, 128), amateur_hidden, amateur_gain.reshape(-1, 128))
    half = lax.all_to_all(blocks, "rows", 0, 0, tiled=True).reshape(2 * beams, quarter)
    other_half = lax.ppermute(half, "rows", [(r, r ^ 1) for r in range(rows)])
    cost = pl.CostEstimate(
        flops=4 * beams * width * 2 * quarter, bytes_accessed=4 * beams * quarter, transcendentals=0
    )
    first = pl.pallas_call(
        first_kernel,
        out_shape=jax.ShapeDtypeStruct((2, 2, 2 * beams, width), jnp.float32),
        in_specs=[SMEM] + [VMEM] * 3,
        out_specs=VMEM,
        compiler_params=PARAMS,
        cost_estimate=cost,
        name="first_half",
    )(position, half, expert_head, amateur_head)
    table = pl.pallas_call(
        second_kernel,
        out_shape=jax.ShapeDtypeStruct((rows, own, 512), jnp.float32),
        in_specs=[SMEM] + [VMEM] * 6,
        out_specs=VMEM,
        scratch_shapes=[pltpu.VMEM((2, 2, 2 * beams, width), jnp.float32)],
        compiler_params=PARAMS,
        cost_estimate=cost,
        name="second_half",
    )(position, other_half, expert_head, amateur_head, first, live_mask.reshape(1, -1), ids)
    table = lax.all_to_all(table, "rows", 0, 0, tiled=True)

    small = jax.ShapeDtypeStruct((planes, own, 128), jnp.float32)
    best_shape = jax.ShapeDtypeStruct((own, TOP), jnp.float32)
    stats = pl.pallas_call(
        functools.partial(stats_kernel, width),
        out_shape=small,
        in_specs=[VMEM] * 2,
        out_specs=VMEM,
        compiler_params=PARAMS,
        name="stats",
    )(table, gap)
    stats = lax.all_to_all(stats, "vocab", 0, 0, tiled=True)
    top, peaks, chosen, lacking = pl.pallas_call(
        finish_kernel,
        out_shape=(
            best_shape,
            jax.ShapeDtypeStruct((own, 2), jnp.float32),
            jax.ShapeDtypeStruct((own, 1), jnp.float32),
            jax.ShapeDtypeStruct((1,), jnp.int32),
        ),
        in_specs=[VMEM] * 2,
        out_specs=(VMEM, VMEM, VMEM, SMEM),
        compiler_params=PARAMS,
        name="finish",
    )(stats, gap)

    def with_every_entry(table, stats, gap, _):
        best = pl.pallas_call(
            functools.partial(score_kernel, width),
            out_shape=small,
            in_specs=[VMEM] * 3,
            out_specs=VMEM,
            compiler_params=PARAMS,
            name="scores",
        )(table, stats, gap)
        best = lax.all_to_all(best, "vocab", 0, 0, tiled=True)
        return pl.pallas_call(
            merge_kernel,
            out_shape=best_shape,
            in_specs=[VMEM],
            out_specs=VMEM,
            compiler_params=PARAMS,
            name="merge",
        )(best)

    top = lax.cond(lacking[0] > 0, with_every_entry, lambda *args: args[-1], table, stats, gap, top)
    return top, peaks, chosen.reshape(own)


def solution(mesh):
    in_specs = (
        P("rows", None),
        P(),
        P(("rows", "vocab"), None),
        P("rows", None),
        P(),
        P(("rows", "vocab"), None),
        P(("rows", "vocab")),
        P(),
        P(),
    )
    out_specs = (P("rows", None), P("rows", None), P("rows"))
    return jax.shard_map(
        per_device, mesh=mesh, in_specs=in_specs, out_specs=out_specs, check_vma=False
    )
```

```python
import functools

import jax
import jax.numpy as jnp
from jax import lax
from jax.experimental import pallas as pl
from jax.experimental.pallas import tpu as pltpu
from jax.sharding import PartitionSpec as P

TOP = 4
NEAR = 40
FIRST = 16
NC = 2

masked_floor = -1e30
dead_below = -5e29
penalty_slope = 2.0
norm_epsilon = 1e-06

VMEM = pl.BlockSpec(memory_space=pltpu.VMEM)
SMEM = pl.BlockSpec(memory_space=pltpu.SMEM)
PARAMS = pltpu.CompilerParams(vmem_limit_bytes=16 * 1024 * 1024)
WIDE_PARAMS = pltpu.CompilerParams(vmem_limit_bytes=60 * 1024 * 1024)


def norm_kernel(*refs):
    inputs, out_ref, held, sems = refs[:4], refs[4], refs[5:9], refs[9]
    copies = [pltpu.make_async_copy(inputs[i], held[i], sems.at[i]) for i in range(4)]
    for copy in copies:
        copy.start()
    for copy in copies:
        copy.wait()
    own, quarters = held[0].shape[0], []
    for hidden, gains in ((held[0], held[1]), (held[2], held[3])):
        values = hidden[...].astype(jnp.float32)
        gain = gains[...].astype(jnp.float32)
        mean = jnp.mean(values * values, axis=-1, keepdims=True)
        values = values * lax.rsqrt(mean + norm_epsilon)
        chunks = [
            (values[:, 128 * i:128 * i + 128] * gain[i:i + 1, :]).astype(jnp.bfloat16)
            for i in range(values.shape[1] // 128)
        ]
        each = len(chunks) // 4
        quarters.append([chunks[each * q:each * q + each] for q in range(4)])
    for core in range(NC):
        for p in range(2):
            q = 2 * core + p
            for i, chunk in enumerate(quarters[0][q] + quarters[1][q]):
                for dest in range(core, out_ref.shape[0], NC):
                    out_ref[dest, own * p:own * p + own, 128 * i:128 * i + 128] = chunk


def half_logits(core, part_ref, he_ref, ha_ref, model):
    head = (he_ref, ha_ref)[model]
    qe, qa = he_ref.shape[1] // 4, ha_ref.shape[1] // 4
    low, size = ((0, qe), (qe, qa))[model]
    sums = []
    for p in range(2):
        columns = pl.ds(pl.multiple_of((2 * core + p) * size, 128), size)
        sums.append(lax.dot_general(
            part_ref[:, low:low + size], head[:, columns], (((1,), (1,)), ((), ())),
            preferred_element_type=jnp.float32,
        ))
    return sums


def first_kernel(pos_ref, part_ref, he_ref, ha_ref, out_ref):
    for model in range(2):
        for p, total in enumerate(half_logits(pos_ref[0], part_ref, he_ref, ha_ref, model)):
            out_ref[model, p] = total


def second_kernel(pos_ref, part_ref, he_ref, ha_ref, first_ref, live_ref, ids_ref, out_ref, acc_ref):
    width = he_ref.shape[0]
    own = out_ref.shape[1]
    for model in range(2):
        for p, total in enumerate(half_logits(1 - pos_ref[0], part_ref, he_ref, ha_ref, model)):
            acc_ref[model, p] = total + first_ref[model, p]
    live = live_ref[...] == 1
    positions = pos_ref[1] + lax.broadcasted_iota(jnp.int32, (1, width), 1)
    for owner in range(out_ref.shape[0]):
        at = 2 * own * owner
        hits = ids_ref[owner] == positions
        for model in range(2):
            logits = acc_ref[model, 0, at:at + own, :] + acc_ref[model, 1, at + own:at + 2 * own, :]
            pick = jnp.sum(jnp.where(hits, logits, 0.0), axis=1, keepdims=True)
            low = 256 * model
            out_ref[owner, :, low:low + width] = jnp.where(live, logits, masked_floor)
            out_ref[owner, :, low + width:low + 256] = jnp.broadcast_to(pick, (own, 256 - width))


def lanes_of(columns, shape):
    lane = lax.broadcasted_iota(jnp.int32, shape, len(shape) - 1)
    result = jnp.zeros(shape, jnp.float32)
    for i, column in enumerate(columns):
        result = jnp.where(lane == i, column, result)
    return result


def lane_at(values, i):
    lane = lax.broadcasted_iota(jnp.int32, values.shape, values.ndim - 1)
    return jnp.sum(jnp.where(lane == i, values, 0.0), axis=-1, keepdims=True)


def total_rows(values):
    return jnp.sum(values, axis=1, keepdims=True)


def insert(levels, entry):
    for i, level in enumerate(levels):
        above = entry[0] > level[0]
        levels[i] = tuple(jnp.where(above, new, old) for new, old in zip(entry, level))
        entry = tuple(jnp.where(above, old, new) for new, old in zip(entry, level))


def remove_top(levels, top):
    hit = levels[0][0] == top
    payload = [total_rows(jnp.where(hit, field, 0.0)) for field in levels[0][1:]]
    count = total_rows(jnp.where(hit, 1.0, 0.0))
    last = tuple(jnp.full_like(f, masked_floor) for f in levels[0])
    lower = levels[1:] + [last]
    return payload, count, [
        tuple(jnp.where(hit, new, old) for new, old in zip(low, level))
        for low, level in zip(lower, levels)
    ]


def stats_kernel(width, table_ref, gap_ref, out_ref):
    sources, own = table_ref.shape[0], table_ref.shape[1]
    real = lax.broadcasted_iota(jnp.int32, (own, 256), 1) < width
    columns = []
    for model in range(2):
        parts = [table_ref[i, :, 256 * model:256 * model + 256] for i in range(sources)]
        peak = functools.reduce(jnp.maximum, parts)
        peak = jnp.max(jnp.where(real, peak, masked_floor), axis=1, keepdims=True)
        total = functools.reduce(jnp.add, [jnp.exp(part - peak) for part in parts])
        total = total_rows(jnp.where(real, total, 0.0))
        columns.append((peak, total, lane_at(functools.reduce(jnp.add, parts), width)))
    (pe, te, ce), (pa, ta, ca) = columns
    least = pe - gap_ref[...].astype(jnp.float32) * 0.1
    floor = jnp.full((own, 256), masked_floor, jnp.float32)
    near, rest = [(floor,) * 2] * TOP, [(floor,) * 3] * TOP
    count = jnp.zeros((own, 256), jnp.float32)
    for i in range(sources):
        e, a = table_ref[i, :, 0:256], table_ref[i, :, 256:512]
        live = real & (e > dead_below)
        is_near = live & (e >= least)
        count += jnp.where(is_near, 1.0, 0.0)
        insert(near, (jnp.where(is_near, e, masked_floor), a))
        insert(rest, (jnp.where(live & (e < least), 3.0 * e - a, masked_floor), e, a))
    missing = total_rows(count)
    picked = []
    for _ in range(NEAR):
        top = jnp.max(near[0][0], axis=1, keepdims=True)
        (a,), hits, near = remove_top(near, top)
        found = top > dead_below
        picked.append((jnp.where(found, top, masked_floor), a))
        missing -= jnp.where(found & (hits == 1.0), 1.0, 0.0)
    for _ in range(TOP):
        top = jnp.max(rest[0][0], axis=1, keepdims=True)
        (e, a), hits, rest = remove_top(rest, top)
        found = top > dead_below
        picked.append((jnp.where(found, e, masked_floor), a))
        missing += jnp.where(found & (hits > 1.0), 1.0, 0.0)
    lanes = [pe, pa, te, ta, ce, ca, missing]
    lanes += [jnp.zeros_like(pe)] * (FIRST - len(lanes)) + [e for e, _ in picked]
    lanes += [jnp.zeros_like(pe)] * (64 + FIRST - len(lanes)) + [a for _, a in picked]
    stats = lanes_of(lanes, out_ref.shape[1:])
    for plane in range(out_ref.shape[0]):
        out_ref[plane] = stats


def best_of(levels):
    tops, counts, seen = [], [], 0.0
    for _ in range(TOP):
        top = jnp.max(levels[0], axis=1, keepdims=True)
        hit = levels[0] == top
        seen = seen + total_rows(jnp.where(hit, 1.0, 0.0))
        tops.append(top)
        counts.append(seen)
        lower = levels[1:] + [jnp.full_like(levels[0], -jnp.inf)]
        levels = [jnp.where(hit, low, level) for level, low in zip(levels, lower)]
    found = []
    for i in range(TOP):
        value = tops[-1]
        for top, seen in reversed(list(zip(tops, counts))):
            value = jnp.where(seen > i, top, value)
        found.append(value)
    return found


def sorted_levels(parts):
    levels = [jnp.full_like(parts[0], -jnp.inf)] * TOP
    for part in parts:
        for i in range(TOP):
            levels[i], part = jnp.maximum(levels[i], part), jnp.minimum(levels[i], part)
    return levels


def row_from(column):
    shape = (column.shape[0], column.shape[0])
    here = lax.broadcasted_iota(jnp.int32, shape, 0) == lax.broadcasted_iota(jnp.int32, shape, 1)
    return jnp.sum(jnp.where(here, column, 0.0), axis=0, keepdims=True)


def totals_of(stats_ref, gap_ref):
    stats = stats_ref[...]
    peak_e, peak_a, sum_e, sum_a = [lane_at(stats, i) for i in range(4)]

    def total_of(peaks, sums):
        peak = jnp.max(peaks, axis=0)
        return peak, peak + jnp.log(jnp.sum(sums * jnp.exp(peaks - peak[None]), axis=0))

    peak_e, log_total_e = total_of(peak_e, sum_e)
    peak_a, log_total_a = total_of(peak_a, sum_a)
    cut = peak_e - log_total_e - gap_ref[...].astype(jnp.float32) * 0.1

    def score(logits_e, logits_a):
        logprob_e = logits_e - log_total_e
        logprob_a = logits_a - log_total_a
        return logprob_e - logprob_a - penalty_slope * jnp.maximum(cut - logprob_e, 0.0)

    return [peak_e - log_total_e, peak_a - log_total_a], score


def finish_kernel(stats_ref, gap_ref, top_ref, peaks_ref, chosen_ref, lacking_ref):
    peaks, score = totals_of(stats_ref, gap_ref)
    stats = stats_ref[...]
    for i, peak in enumerate(peaks):
        peaks_ref[i:i + 1, :] = row_from(peak)
    picks = [jnp.sum(lane_at(stats, i), axis=0) for i in (4, 5)]
    chosen_ref[...] = row_from(score(*picks))
    lane = lax.broadcasted_iota(jnp.int32, stats.shape[1:], 1)
    is_candidate = (lane >= FIRST) & (lane < FIRST + NEAR + TOP)
    parts, lacking = [], jnp.zeros(stats.shape[1:], jnp.float32)
    for plane in range(stats.shape[0]):
        e, a = stats[plane], pltpu.roll(stats[plane], 64, 1)
        value = jnp.where(e > dead_below, score(e, a), masked_floor)
        parts.append(jnp.where(is_candidate, value, -jnp.inf))
        lacking = jnp.maximum(lacking, jnp.where(lane == 6, e, 0.0))
    top_ref[...] = lanes_of(best_of(sorted_levels(parts)), top_ref.shape)
    lacking_ref[0] = jnp.where(jnp.max(lacking) > 0.0, 1, 0).astype(jnp.int32)


def score_kernel(width, table_ref, stats_ref, gap_ref, best_ref):
    _, score = totals_of(stats_ref, gap_ref)
    real = lax.broadcasted_iota(jnp.int32, (table_ref.shape[1], 256), 1) < width
    parts = []
    for source in range(table_ref.shape[0]):
        e = table_ref[source, :, 0:256]
        a = table_ref[source, :, 256:512]
        parts.append(jnp.where(real & (e > dead_below), score(e, a), masked_floor))
    best = lanes_of(best_of(sorted_levels(parts)), best_ref.shape[1:])
    for plane in range(best_ref.shape[0]):
        best_ref[plane] = best


def merge_kernel(parts_ref, out_ref):
    shape = parts_ref.shape[1:]
    real = lax.broadcasted_iota(jnp.int32, shape, 1) < TOP
    parts = [jnp.where(real, parts_ref[i], -jnp.inf) for i in range(parts_ref.shape[0])]
    out_ref[...] = lanes_of(best_of(sorted_levels(parts)), out_ref.shape)


def per_device(
    expert_hidden,
    expert_gain,
    expert_head,
    amateur_hidden,
    amateur_gain,
    amateur_head,
    live_mask,
    token_ids,
    plaus_level,
):
    own, depth_e = expert_hidden.shape
    depth_a = amateur_hidden.shape[1]
    width = expert_head.shape[0]
    rows, planes = lax.axis_size("rows"), lax.axis_size("vocab")
    beams = own * rows
    quarter = (depth_e + depth_a) // 4
    row, plane = lax.axis_index("rows"), lax.axis_index("vocab")
    position = jnp.stack([row % NC, (row * planes + plane) * width]).astype(jnp.int32)
    ids = token_ids.reshape(rows, own, 1)
    gap = lax.dynamic_slice_in_dim(plaus_level, row * own, own, 0).reshape(own, 1)

    norm_inputs = (
        expert_hidden, expert_gain.reshape(-1, 128), amateur_hidden, amateur_gain.reshape(-1, 128)
    )
    blocks = pl.pallas_call(
        norm_kernel,
        out_shape=jax.ShapeDtypeStruct((rows, 2 * own, quarter), jnp.bfloat16),
        in_specs=[pl.BlockSpec(memory_space=pl.ANY)] * 4,
        out_specs=VMEM,
        scratch_shapes=[pltpu.VMEM(x.shape, x.dtype) for x in norm_inputs]
        + [pltpu.SemaphoreType.DMA((4,))],
        compiler_params=WIDE_PARAMS,
        name="norms",
    )(*norm_inputs)
    half = lax.all_to_all(blocks, "rows", 0, 0, tiled=True).reshape(2 * beams, quarter)
    other_half = lax.ppermute(half, "rows", [(r, r ^ 1) for r in range(rows)])
    cost = pl.CostEstimate(
        flops=4 * beams * width * 2 * quarter, bytes_accessed=4 * beams * quarter, transcendentals=0
    )
    first = pl.pallas_call(
        first_kernel,
        out_shape=jax.ShapeDtypeStruct((2, 2, 2 * beams, width), jnp.float32),
        in_specs=[SMEM] + [VMEM] * 3,
        out_specs=VMEM,
        compiler_params=PARAMS,
        cost_estimate=cost,
        name="first_half",
    )(position, half, expert_head, amateur_head)
    table = pl.pallas_call(
        second_kernel,
        out_shape=jax.ShapeDtypeStruct((rows, own, 512), jnp.float32),
        in_specs=[SMEM] + [VMEM] * 6,
        out_specs=VMEM,
        scratch_shapes=[pltpu.VMEM((2, 2, 2 * beams, width), jnp.float32)],
        compiler_params=PARAMS,
        cost_estimate=cost,
        name="second_half",
    )(position, other_half, expert_head, amateur_head, first, live_mask.reshape(1, -1), ids)
    table = lax.all_to_all(table, "rows", 0, 0, tiled=True)

    small = jax.ShapeDtypeStruct((planes, own, 128), jnp.float32)
    best_shape = jax.ShapeDtypeStruct((own, TOP), jnp.float32)
    stats = pl.pallas_call(
        functools.partial(stats_kernel, width),
        out_shape=small,
        in_specs=[VMEM] * 2,
        out_specs=VMEM,
        compiler_params=PARAMS,
        name="stats",
    )(table, gap)
    stats = lax.all_to_all(stats, "vocab", 0, 0, tiled=True)
    top, peaks, chosen, lacking = pl.pallas_call(
        finish_kernel,
        out_shape=(
            best_shape,
            jax.ShapeDtypeStruct((2, own), jnp.float32),
            jax.ShapeDtypeStruct((1, own), jnp.float32),
            jax.ShapeDtypeStruct((1,), jnp.int32),
        ),
        in_specs=[VMEM] * 2,
        out_specs=(VMEM, VMEM, VMEM, SMEM),
        compiler_params=PARAMS,
        name="finish",
    )(stats, gap)

    def with_every_entry(table, stats, gap, _):
        best = pl.pallas_call(
            functools.partial(score_kernel, width),
            out_shape=small,
            in_specs=[VMEM] * 3,
            out_specs=VMEM,
            compiler_params=PARAMS,
            name="scores",
        )(table, stats, gap)
        best = lax.all_to_all(best, "vocab", 0, 0, tiled=True)
        return pl.pallas_call(
            merge_kernel,
            out_shape=best_shape,
            in_specs=[VMEM],
            out_specs=VMEM,
            compiler_params=PARAMS,
            name="merge",
        )(best)

    top = lax.cond(lacking[0] > 0, with_every_entry, lambda *args: args[-1], table, stats, gap, top)
    return top, peaks.T, chosen.reshape(own)


def solution(mesh):
    in_specs = (
        P("rows", None),
        P(),
        P(("rows", "vocab"), None),
        P("rows", None),
        P(),
        P(("rows", "vocab"), None),
        P(("rows", "vocab")),
        P(),
        P(),
    )
    out_specs = (P("rows", None), P("rows", None), P("rows"))
    return jax.shard_map(
        per_device, mesh=mesh, in_specs=in_specs, out_specs=out_specs, check_vma=False
    )
```

```python
import functools

import jax
import jax.numpy as jnp
from jax import lax
from jax.experimental import pallas as pl
from jax.experimental.pallas import tpu as pltpu
from jax.sharding import PartitionSpec as P

TOP = 4
NEAR = 20
FIRST = 16
NC = 2

masked_floor = -1e30
dead_below = -5e29
penalty_slope = 2.0
norm_epsilon = 1e-06

VMEM = pl.BlockSpec(memory_space=pltpu.VMEM)
ANY = pl.BlockSpec(memory_space=pl.ANY)
SMEM = pl.BlockSpec(memory_space=pltpu.SMEM)
PARAMS = pltpu.CompilerParams(vmem_limit_bytes=16 * 1024 * 1024)
PRODUCT_PARAMS = pltpu.CompilerParams(vmem_limit_bytes=54 * 1024 * 1024)
WIDE_PARAMS = pltpu.CompilerParams(vmem_limit_bytes=60 * 1024 * 1024)


def norm_kernel(*refs):
    inputs, out_ref, held, sems = refs[:4], refs[4], refs[5:9], refs[9]
    copies = [pltpu.make_async_copy(inputs[i], held[i], sems.at[i]) for i in range(4)]
    for copy in copies:
        copy.start()
    for copy in copies:
        copy.wait()
    own, quarters = held[0].shape[0], []
    for hidden, gains in ((held[0], held[1]), (held[2], held[3])):
        values = hidden[...].astype(jnp.float32)
        gain = gains[...].astype(jnp.float32)
        mean = jnp.mean(values * values, axis=-1, keepdims=True)
        values = values * lax.rsqrt(mean + norm_epsilon)
        chunks = [
            (values[:, 128 * i:128 * i + 128] * gain[i:i + 1, :]).astype(jnp.bfloat16)
            for i in range(values.shape[1] // 128)
        ]
        each = len(chunks) // 4
        quarters.append([chunks[each * q:each * q + each] for q in range(4)])
    for core in range(NC):
        for p in range(2):
            q = 2 * core + p
            for i, chunk in enumerate(quarters[0][q] + quarters[1][q]):
                for dest in range(core, out_ref.shape[0], NC):
                    out_ref[dest, own * p:own * p + own, 128 * i:128 * i + 128] = chunk


def chunked(core, part_ref, head_refs, held, sems):
    part_buf, head_bufs = held
    columns = part_ref.shape[1]
    quarter_e = head_refs[0].shape[1] // 4
    chunks = [(0, 0, quarter_e // 2), (0, quarter_e // 2, quarter_e // 2), (1, quarter_e, columns - quarter_e)]
    copies = []
    for i, (model, low, size) in enumerate(chunks):
        here = pl.ds(low, size)
        own = [pltpu.make_async_copy(part_ref.at[:, here], part_buf.at[:, here], sems.at[i, 2])]
        quarter = head_refs[model].shape[1] // 4
        inside = low - (quarter_e if model else 0)
        for p in range(2):
            source = pl.ds(pl.multiple_of((2 * core + p) * quarter + inside, 128), size)
            own.append(pltpu.make_async_copy(
                head_refs[model].at[:, source], head_bufs.at[p, :, here], sems.at[i, p]
            ))
        for copy in own:
            copy.start()
        copies.append(own)
    for (model, low, size), own in zip(chunks, copies):
        for copy in own:
            copy.wait()
        yield model, [
            lax.dot_general(
                part_buf[:, low:low + size], head_bufs[p, :, low:low + size],
                (((1,), (1,)), ((), ())), preferred_element_type=jnp.float32,
            )
            for p in range(2)
        ]


def half_sums(core, part_ref, head_refs, held, sems, acc_ref):
    started = set()
    for model, sums in chunked(core, part_ref, head_refs, held, sems):
        for p, total in enumerate(sums):
            acc_ref[model, p] = acc_ref[model, p] + total if model in started else total
        started.add(model)


def quarters_joined(acc_ref, model, owner, own):
    at = 2 * own * owner
    return acc_ref[model, 0, at:at + own, :] + acc_ref[model, 1, at + own:at + 2 * own, :]


def first_kernel(pos_ref, part_ref, he_ref, ha_ref, out_ref, part_buf, head_bufs, sems, acc_ref):
    half_sums(pos_ref[0], part_ref, (he_ref, ha_ref), (part_buf, head_bufs), sems, acc_ref)
    for model in range(2):
        for owner in range(out_ref.shape[1]):
            out_ref[model, owner] = quarters_joined(acc_ref, model, owner, out_ref.shape[2])


def second_kernel(
    pos_ref, part_ref, he_ref, ha_ref, first_ref, live_ref, ids_ref, out_ref,
    part_buf, head_bufs, sems, acc_ref,
):
    width = he_ref.shape[0]
    own = ids_ref.shape[1]
    half_sums(1 - pos_ref[0], part_ref, (he_ref, ha_ref), (part_buf, head_bufs), sems, acc_ref)
    live = live_ref[...] == 1
    positions = pos_ref[1] + lax.broadcasted_iota(jnp.int32, (1, width), 1)
    half = width // 2
    for owner in range(out_ref.shape[0]):
        hits = ids_ref[owner] == positions
        for model in range(2):
            logits = first_ref[model, owner] + quarters_joined(acc_ref, model, owner, own)
            pick = jnp.sum(jnp.where(hits, logits, 0.0), axis=1, keepdims=True)
            pick = jnp.broadcast_to(pick, (own, 128 - half))
            held = jnp.where(live, logits, masked_floor)
            low = 128 * model
            for side in range(2):
                rows = slice(own * side, own * side + own)
                out_ref[owner, rows, low:low + half] = held[:, half * side:half * side + half]
                out_ref[owner, rows, low + half:low + 128] = pick


def lanes_of(columns, shape):
    lane = lax.broadcasted_iota(jnp.int32, shape, len(shape) - 1)
    result = jnp.zeros(shape, jnp.float32)
    for i, column in enumerate(columns):
        result = jnp.where(lane == i, column, result)
    return result


def lane_at(values, i):
    lane = lax.broadcasted_iota(jnp.int32, values.shape, values.ndim - 1)
    return jnp.sum(jnp.where(lane == i, values, 0.0), axis=-1, keepdims=True)


def total_rows(values):
    return jnp.sum(values, axis=1, keepdims=True)


def insert(levels, entry):
    for i, level in enumerate(levels):
        above = entry[0] > level[0]
        levels[i] = tuple(jnp.where(above, new, old) for new, old in zip(entry, level))
        entry = tuple(jnp.where(above, old, new) for new, old in zip(entry, level))


def remove_top(levels, top):
    hit = levels[0][0] == top
    payload = [total_rows(jnp.where(hit, field, 0.0)) for field in levels[0][1:]]
    count = total_rows(jnp.where(hit, 1.0, 0.0))
    last = tuple(jnp.full_like(f, masked_floor) for f in levels[0])
    lower = levels[1:] + [last]
    return payload, count, [
        tuple(jnp.where(hit, new, old) for new, old in zip(low, level))
        for low, level in zip(lower, levels)
    ]


def stats_kernel(width, table_ref, gap_ref, out_ref):
    sources, own = table_ref.shape[0], table_ref.shape[1] // 2
    shape = (2 * own, 128)
    real = lax.broadcasted_iota(jnp.int32, shape, 1) < width // 2
    columns = []
    for model in range(2):
        parts = [table_ref[i, :, 128 * model:128 * model + 128] for i in range(sources)]
        peak = functools.reduce(jnp.maximum, parts)
        peak = jnp.max(jnp.where(real, peak, masked_floor), axis=1, keepdims=True)
        peak = jnp.maximum(peak[:own], peak[own:])
        both = jnp.concatenate([peak, peak])
        total = functools.reduce(jnp.add, [jnp.exp(part - both) for part in parts])
        total = total_rows(jnp.where(real, total, 0.0))
        pick = lane_at(functools.reduce(jnp.add, parts), width // 2)
        columns.append((peak, total[:own] + total[own:], pick[:own]))
    (pe, te, ce), (pa, ta, ca) = columns
    least = pe - gap_ref[...].astype(jnp.float32) * 0.1
    least = jnp.concatenate([least, least])
    floor = jnp.full(shape, masked_floor, jnp.float32)
    near, rest = [(floor,) * 2] * TOP, [(floor,) * 3] * TOP
    count = jnp.zeros(shape, jnp.float32)
    for i in range(sources):
        e, a = table_ref[i, :, 0:128], table_ref[i, :, 128:256]
        live = real & (e > dead_below)
        is_near = live & (e >= least)
        count += jnp.where(is_near, 1.0, 0.0)
        insert(near, (jnp.where(is_near, e, masked_floor), a))
        insert(rest, (jnp.where(live & (e < least), 3.0 * e - a, masked_floor), e, a))
    missing = total_rows(count)
    picked = []
    for _ in range(NEAR):
        top = jnp.max(near[0][0], axis=1, keepdims=True)
        (a,), hits, near = remove_top(near, top)
        found = top > dead_below
        picked.append((jnp.where(found, top, masked_floor), a))
        missing -= jnp.where(found & (hits == 1.0), 1.0, 0.0)
    for _ in range(TOP):
        top = jnp.max(rest[0][0], axis=1, keepdims=True)
        (e, a), hits, rest = remove_top(rest, top)
        found = top > dead_below
        picked.append((jnp.where(found, e, masked_floor), a))
        missing += jnp.where(found & (hits > 1.0), 1.0, 0.0)
    zeros = [jnp.zeros_like(missing)]
    lanes = zeros * FIRST + [e for e, _ in picked]
    lanes += zeros * (64 + FIRST - len(lanes)) + [a for _, a in picked]
    lanes = lanes_of(lanes, shape)
    stats = lanes_of([pe, pa, te, ta, ce, ca, missing[:own] + missing[own:]], (own, 128))
    stats += lanes[:own] + pltpu.roll(lanes, len(picked), 1)[own:]
    for plane in range(out_ref.shape[0]):
        out_ref[plane] = stats


def best_of(levels):
    tops, counts, seen = [], [], 0.0
    for _ in range(TOP):
        top = jnp.max(levels[0], axis=1, keepdims=True)
        hit = levels[0] == top
        seen = seen + total_rows(jnp.where(hit, 1.0, 0.0))
        tops.append(top)
        counts.append(seen)
        lower = levels[1:] + [jnp.full_like(levels[0], -jnp.inf)]
        levels = [jnp.where(hit, low, level) for level, low in zip(levels, lower)]
    found = []
    for i in range(TOP):
        value = tops[-1]
        for top, seen in reversed(list(zip(tops, counts))):
            value = jnp.where(seen > i, top, value)
        found.append(value)
    return found


def sorted_levels(parts):
    levels = [jnp.full_like(parts[0], -jnp.inf)] * TOP
    for part in parts:
        for i in range(TOP):
            levels[i], part = jnp.maximum(levels[i], part), jnp.minimum(levels[i], part)
    return levels


def row_from(column):
    shape = (column.shape[0], column.shape[0])
    here = lax.broadcasted_iota(jnp.int32, shape, 0) == lax.broadcasted_iota(jnp.int32, shape, 1)
    return jnp.sum(jnp.where(here, column, 0.0), axis=0, keepdims=True)


def totals_of(stats_ref, gap_ref, copies=1):
    stats = stats_ref[...]
    peak_e, peak_a, sum_e, sum_a = [lane_at(stats, i) for i in range(4)]

    def total_of(peaks, sums):
        peak = jnp.max(peaks, axis=0)
        return peak, peak + jnp.log(jnp.sum(sums * jnp.exp(peaks - peak[None]), axis=0))

    peak_e, log_total_e = total_of(peak_e, sum_e)
    peak_a, log_total_a = total_of(peak_a, sum_a)
    cut = peak_e - log_total_e - gap_ref[...].astype(jnp.float32) * 0.1
    shift_e, shift_a, cuts = [
        jnp.concatenate([x] * copies) if copies > 1 else x for x in (log_total_e, log_total_a, cut)
    ]

    def score(logits_e, logits_a):
        logprob_e = logits_e - shift_e
        logprob_a = logits_a - shift_a
        return logprob_e - logprob_a - penalty_slope * jnp.maximum(cuts - logprob_e, 0.0)

    return [peak_e - log_total_e, peak_a - log_total_a], score


def finish_kernel(stats_ref, gap_ref, top_ref, peaks_ref, chosen_ref, lacking_ref):
    peaks, score = totals_of(stats_ref, gap_ref)
    stats = stats_ref[...]
    for i, peak in enumerate(peaks):
        peaks_ref[i:i + 1, :] = row_from(peak)
    picks = [jnp.sum(lane_at(stats, i), axis=0) for i in (4, 5)]
    chosen_ref[...] = row_from(score(*picks))
    lane = lax.broadcasted_iota(jnp.int32, stats.shape[1:], 1)
    is_candidate = (lane >= FIRST) & (lane < FIRST + 2 * (NEAR + TOP))
    parts, lacking = [], jnp.zeros(stats.shape[1:], jnp.float32)
    for plane in range(stats.shape[0]):
        e, a = stats[plane], pltpu.roll(stats[plane], 64, 1)
        value = jnp.where(e > dead_below, score(e, a), masked_floor)
        parts.append(jnp.where(is_candidate, value, -jnp.inf))
        lacking = jnp.maximum(lacking, jnp.where(lane == 6, e, 0.0))
    top_ref[...] = lanes_of(best_of(sorted_levels(parts)), top_ref.shape)
    lacking_ref[0] = jnp.where(jnp.max(lacking) > 0.0, 1, 0).astype(jnp.int32)


def score_kernel(width, table_ref, stats_ref, gap_ref, best_ref):
    _, score = totals_of(stats_ref, gap_ref, 2)
    own = table_ref.shape[1] // 2
    real = lax.broadcasted_iota(jnp.int32, (2 * own, 128), 1) < width // 2
    parts = []
    for source in range(table_ref.shape[0]):
        e, a = table_ref[source, :, 0:128], table_ref[source, :, 128:256]
        parts.append(jnp.where(real & (e > dead_below), score(e, a), masked_floor))
    found = best_of(sorted_levels(parts))
    found = [value[:own] for value in found] + [value[own:] for value in found]
    best = lanes_of(found, best_ref.shape[1:])
    for plane in range(best_ref.shape[0]):
        best_ref[plane] = best


def merge_kernel(parts_ref, out_ref):
    shape = parts_ref.shape[1:]
    real = lax.broadcasted_iota(jnp.int32, shape, 1) < 2 * TOP
    parts = [jnp.where(real, parts_ref[i], -jnp.inf) for i in range(parts_ref.shape[0])]
    out_ref[...] = lanes_of(best_of(sorted_levels(parts)), out_ref.shape)


def per_device(
    expert_hidden,
    expert_gain,
    expert_head,
    amateur_hidden,
    amateur_gain,
    amateur_head,
    live_mask,
    token_ids,
    plaus_level,
):
    own, depth_e = expert_hidden.shape
    depth_a = amateur_hidden.shape[1]
    width = expert_head.shape[0]
    rows, planes = lax.axis_size("rows"), lax.axis_size("vocab")
    beams = own * rows
    quarter = (depth_e + depth_a) // 4
    row, plane = lax.axis_index("rows"), lax.axis_index("vocab")
    position = jnp.stack([row % NC, (row * planes + plane) * width]).astype(jnp.int32)
    ids = token_ids.reshape(rows, own, 1)
    gap = lax.dynamic_slice_in_dim(plaus_level, row * own, own, 0).reshape(own, 1)

    norm_inputs = (
        expert_hidden, expert_gain.reshape(-1, 128), amateur_hidden, amateur_gain.reshape(-1, 128)
    )
    blocks = pl.pallas_call(
        norm_kernel,
        out_shape=jax.ShapeDtypeStruct((rows, 2 * own, quarter), jnp.bfloat16),
        in_specs=[ANY] * 4,
        out_specs=VMEM,
        scratch_shapes=[pltpu.VMEM(x.shape, x.dtype) for x in norm_inputs]
        + [pltpu.SemaphoreType.DMA((4,))],
        compiler_params=WIDE_PARAMS,
        name="norms",
    )(*norm_inputs)
    half = lax.all_to_all(blocks, "rows", 0, 0, tiled=True).reshape(2 * beams, quarter)
    other_half = lax.ppermute(half, "rows", [(r, r ^ 1) for r in range(rows)])
    cost = pl.CostEstimate(
        flops=4 * beams * width * 2 * quarter, bytes_accessed=4 * beams * quarter, transcendentals=0
    )
    buffers = [
        pltpu.VMEM((2 * beams, quarter), jnp.bfloat16),
        pltpu.VMEM((2, width, quarter), jnp.bfloat16),
        pltpu.SemaphoreType.DMA((3, 3)),
        pltpu.VMEM((2, 2, 2 * beams, width), jnp.float32),
    ]
    first = pl.pallas_call(
        first_kernel,
        out_shape=jax.ShapeDtypeStruct((2, rows, own, width), jnp.float32),
        in_specs=[SMEM] + [ANY] * 3,
        out_specs=VMEM,
        scratch_shapes=buffers,
        compiler_params=PRODUCT_PARAMS,
        cost_estimate=cost,
        name="first_half",
    )(position, half, expert_head, amateur_head)
    table = pl.pallas_call(
        second_kernel,
        out_shape=jax.ShapeDtypeStruct((rows, 2 * own, 256), jnp.float32),
        in_specs=[SMEM] + [ANY] * 3 + [VMEM] * 3,
        out_specs=VMEM,
        scratch_shapes=buffers,
        compiler_params=PRODUCT_PARAMS,
        cost_estimate=cost,
        name="second_half",
    )(position, other_half, expert_head, amateur_head, first, live_mask.reshape(1, -1), ids)
    table = lax.all_to_all(table, "rows", 0, 0, tiled=True)

    small = jax.ShapeDtypeStruct((planes, own, 128), jnp.float32)
    best_shape = jax.ShapeDtypeStruct((own, TOP), jnp.float32)
    stats = pl.pallas_call(
        functools.partial(stats_kernel, width),
        out_shape=small,
        in_specs=[VMEM] * 2,
        out_specs=VMEM,
        compiler_params=PARAMS,
        name="stats",
    )(table, gap)
    stats = lax.all_to_all(stats, "vocab", 0, 0, tiled=True)
    top, peaks, chosen, lacking = pl.pallas_call(
        finish_kernel,
        out_shape=(
            best_shape,
            jax.ShapeDtypeStruct((2, own), jnp.float32),
            jax.ShapeDtypeStruct((1, own), jnp.float32),
            jax.ShapeDtypeStruct((1,), jnp.int32),
        ),
        in_specs=[VMEM] * 2,
        out_specs=(VMEM, VMEM, VMEM, SMEM),
        compiler_params=PARAMS,
        name="finish",
    )(stats, gap)

    def with_every_entry(table, stats, gap, _):
        best = pl.pallas_call(
            functools.partial(score_kernel, width),
            out_shape=small,
            in_specs=[VMEM] * 3,
            out_specs=VMEM,
            compiler_params=PARAMS,
            name="scores",
        )(table, stats, gap)
        best = lax.all_to_all(best, "vocab", 0, 0, tiled=True)
        return pl.pallas_call(
            merge_kernel,
            out_shape=best_shape,
            in_specs=[VMEM],
            out_specs=VMEM,
            compiler_params=PARAMS,
            name="merge",
        )(best)

    top = lax.cond(lacking[0] > 0, with_every_entry, lambda *args: args[-1], table, stats, gap, top)
    return top, peaks.T, chosen.reshape(own)


def solution(mesh):
    in_specs = (
        P("rows", None),
        P(),
        P(("rows", "vocab"), None),
        P("rows", None),
        P(),
        P(("rows", "vocab"), None),
        P(("rows", "vocab")),
        P(),
        P(),
    )
    out_specs = (P("rows", None), P("rows", None), P("rows"))
    return jax.shard_map(
        per_device, mesh=mesh, in_specs=in_specs, out_specs=out_specs, check_vma=False
    )
```

```python
import functools

import jax
import jax.numpy as jnp
from jax import lax
from jax.experimental import pallas as pl
from jax.experimental.pallas import tpu as pltpu
from jax.sharding import PartitionSpec as P

TOP = 4
NEAR = 20
FIRST = 16
NC = 2

masked_floor = -1e30
dead_below = -5e29
penalty_slope = 2.0
norm_epsilon = 1e-06

VMEM = pl.BlockSpec(memory_space=pltpu.VMEM)
HBM = pl.BlockSpec(memory_space=pltpu.HBM)
SMEM = pl.BlockSpec(memory_space=pltpu.SMEM)
WIDE_PARAMS = pltpu.CompilerParams(vmem_limit_bytes=60 * 1024 * 1024)
PARAMS = pltpu.CompilerParams(vmem_limit_bytes=16 * 1024 * 1024)


def norm_kernel(*refs):
    inputs, out_ref, held, sems = refs[:4], refs[4], refs[5:9], refs[9]
    copies = [pltpu.make_async_copy(inputs[i], held[i], sems.at[i]) for i in range(4)]
    for copy in copies:
        copy.start()
    for copy in copies:
        copy.wait()
    own, quarters = held[0].shape[0], []
    for hidden, gains in ((held[0], held[1]), (held[2], held[3])):
        values = hidden[...].astype(jnp.float32)
        gain = gains[...].astype(jnp.float32)
        mean = jnp.mean(values * values, axis=-1, keepdims=True)
        values = values * lax.rsqrt(mean + norm_epsilon)
        chunks = [
            (values[:, 128 * i:128 * i + 128] * gain[i:i + 1, :]).astype(jnp.bfloat16)
            for i in range(values.shape[1] // 128)
        ]
        each = len(chunks) // 4
        quarters.append([chunks[each * q:each * q + each] for q in range(4)])
    for core in range(NC):
        for p in range(2):
            q = 2 * core + p
            for i, chunk in enumerate(quarters[0][q] + quarters[1][q]):
                for dest in range(core, out_ref.shape[0], NC):
                    out_ref[dest, own * p:own * p + own, 128 * i:128 * i + 128] = chunk


def half_sums(core, part_ref, head_refs, acc_ref):
    low = 0
    for model, head in enumerate(head_refs):
        size = head.shape[1] // 4
        for p in range(2):
            columns = pl.ds(pl.multiple_of((2 * core + p) * size, 128), size)
            acc_ref[model, p] = lax.dot_general(
                part_ref[:, low:low + size], head[:, columns], (((1,), (1,)), ((), ())),
                preferred_element_type=jnp.float32,
            )
        low += size


def quarters_joined(acc_ref, model, owner, own):
    at = 2 * own * owner
    return acc_ref[model, 0, at:at + own, :] + acc_ref[model, 1, at + own:at + 2 * own, :]


def first_kernel(pos_ref, part_ref, he_ref, ha_ref, out_ref, acc_ref):
    half_sums(pos_ref[0], part_ref, (he_ref, ha_ref), acc_ref)
    for model in range(2):
        for owner in range(out_ref.shape[1]):
            out_ref[model, owner] = quarters_joined(acc_ref, model, owner, out_ref.shape[2])


def second_kernel(
    pos_ref, part_ref, he_ref, ha_ref, first_ref, live_ref, ids_ref, out_ref, acc_ref
):
    width = he_ref.shape[0]
    own = ids_ref.shape[1]
    half_sums(1 - pos_ref[0], part_ref, (he_ref, ha_ref), acc_ref)
    live = live_ref[...] == 1
    positions = pos_ref[1] + lax.broadcasted_iota(jnp.int32, (1, width), 1)
    half = width // 2
    for owner in range(out_ref.shape[0]):
        hits = ids_ref[owner] == positions
        for model in range(2):
            logits = first_ref[model, owner] + quarters_joined(acc_ref, model, owner, own)
            pick = jnp.sum(jnp.where(hits, logits, 0.0), axis=1, keepdims=True)
            pick = jnp.broadcast_to(pick, (own, 128 - half))
            held = jnp.where(live, logits, masked_floor)
            low = 128 * model
            for side in range(2):
                rows = slice(own * side, own * side + own)
                out_ref[owner, rows, low:low + half] = held[:, half * side:half * side + half]
                out_ref[owner, rows, low + half:low + 128] = pick


def lanes_of(columns, shape):
    lane = lax.broadcasted_iota(jnp.int32, shape, len(shape) - 1)
    result = jnp.zeros(shape, jnp.float32)
    for i, column in enumerate(columns):
        result = jnp.where(lane == i, column, result)
    return result


def lane_at(values, i):
    lane = lax.broadcasted_iota(jnp.int32, values.shape, values.ndim - 1)
    return jnp.sum(jnp.where(lane == i, values, 0.0), axis=-1, keepdims=True)


def total_rows(values):
    return jnp.sum(values, axis=1, keepdims=True)


def insert(levels, entry):
    for i, level in enumerate(levels):
        above = entry[0] > level[0]
        levels[i] = tuple(jnp.where(above, new, old) for new, old in zip(entry, level))
        entry = tuple(jnp.where(above, old, new) for new, old in zip(entry, level))


def remove_top(levels, top):
    hit = levels[0][0] == top
    payload = [total_rows(jnp.where(hit, field, 0.0)) for field in levels[0][1:]]
    count = total_rows(jnp.where(hit, 1.0, 0.0))
    last = tuple(jnp.full_like(f, masked_floor) for f in levels[0])
    lower = levels[1:] + [last]
    return payload, count, [
        tuple(jnp.where(hit, new, old) for new, old in zip(low, level))
        for low, level in zip(lower, levels)
    ]


def stats_kernel(width, table_ref, gap_ref, out_ref):
    sources, own = table_ref.shape[0], table_ref.shape[1] // 2
    shape = (2 * own, 128)
    real = lax.broadcasted_iota(jnp.int32, shape, 1) < width // 2
    columns = []
    for model in range(2):
        parts = [table_ref[i, :, 128 * model:128 * model + 128] for i in range(sources)]
        peak = functools.reduce(jnp.maximum, parts)
        peak = jnp.max(jnp.where(real, peak, masked_floor), axis=1, keepdims=True)
        peak = jnp.maximum(peak[:own], peak[own:])
        both = jnp.concatenate([peak, peak])
        total = functools.reduce(jnp.add, [jnp.exp(part - both) for part in parts])
        total = total_rows(jnp.where(real, total, 0.0))
        pick = lane_at(functools.reduce(jnp.add, parts), width // 2)
        columns.append((peak, total[:own] + total[own:], pick[:own]))
    (pe, te, ce), (pa, ta, ca) = columns
    least = pe - gap_ref[...].astype(jnp.float32) * 0.1
    least = jnp.concatenate([least, least])
    floor = jnp.full(shape, masked_floor, jnp.float32)
    near, rest = [(floor,) * 2] * TOP, [(floor,) * 3] * TOP
    count = jnp.zeros(shape, jnp.float32)
    for i in range(sources):
        e, a = table_ref[i, :, 0:128], table_ref[i, :, 128:256]
        live = real & (e > dead_below)
        is_near = live & (e >= least)
        count += jnp.where(is_near, 1.0, 0.0)
        insert(near, (jnp.where(is_near, e, masked_floor), a))
        insert(rest, (jnp.where(live & (e < least), 3.0 * e - a, masked_floor), e, a))
    missing = total_rows(count)
    picked = []
    for _ in range(NEAR):
        top = jnp.max(near[0][0], axis=1, keepdims=True)
        (a,), hits, near = remove_top(near, top)
        found = top > dead_below
        picked.append((jnp.where(found, top, masked_floor), a))
        missing -= jnp.where(found & (hits == 1.0), 1.0, 0.0)
    for _ in range(TOP):
        top = jnp.max(rest[0][0], axis=1, keepdims=True)
        (e, a), hits, rest = remove_top(rest, top)
        found = top > dead_below
        picked.append((jnp.where(found, e, masked_floor), a))
        missing += jnp.where(found & (hits > 1.0), 1.0, 0.0)
    zeros = [jnp.zeros_like(missing)]
    lanes = zeros * FIRST + [e for e, _ in picked]
    lanes += zeros * (64 + FIRST - len(lanes)) + [a for _, a in picked]
    lanes = lanes_of(lanes, shape)
    stats = lanes_of([pe, pa, te, ta, ce, ca, missing[:own] + missing[own:]], (own, 128))
    stats += lanes[:own] + pltpu.roll(lanes, len(picked), 1)[own:]
    for plane in range(out_ref.shape[0]):
        out_ref[plane] = stats


def best_of(levels):
    tops, counts, seen = [], [], 0.0
    for _ in range(TOP):
        top = jnp.max(levels[0], axis=1, keepdims=True)
        hit = levels[0] == top
        seen = seen + total_rows(jnp.where(hit, 1.0, 0.0))
        tops.append(top)
        counts.append(seen)
        lower = levels[1:] + [jnp.full_like(levels[0], -jnp.inf)]
        levels = [jnp.where(hit, low, level) for level, low in zip(levels, lower)]
    found = []
    for i in range(TOP):
        value = tops[-1]
        for top, seen in reversed(list(zip(tops, counts))):
            value = jnp.where(seen > i, top, value)
        found.append(value)
    return found


def sorted_levels(parts):
    levels = [jnp.full_like(parts[0], -jnp.inf)] * TOP
    for part in parts:
        for i in range(TOP):
            levels[i], part = jnp.maximum(levels[i], part), jnp.minimum(levels[i], part)
    return levels


def row_from(column):
    shape = (column.shape[0], column.shape[0])
    here = lax.broadcasted_iota(jnp.int32, shape, 0) == lax.broadcasted_iota(jnp.int32, shape, 1)
    return jnp.sum(jnp.where(here, column, 0.0), axis=0, keepdims=True)


def totals_of(stats_ref, gap_ref, copies=1):
    stats = stats_ref[...]
    peak_e, peak_a, sum_e, sum_a = [lane_at(stats, i) for i in range(4)]

    def total_of(peaks, sums):
        peak = jnp.max(peaks, axis=0)
        return peak, peak + jnp.log(jnp.sum(sums * jnp.exp(peaks - peak[None]), axis=0))

    peak_e, log_total_e = total_of(peak_e, sum_e)
    peak_a, log_total_a = total_of(peak_a, sum_a)
    cut = peak_e - log_total_e - gap_ref[...].astype(jnp.float32) * 0.1
    shift_e, shift_a, cuts = [
        jnp.concatenate([x] * copies) if copies > 1 else x for x in (log_total_e, log_total_a, cut)
    ]

    def score(logits_e, logits_a):
        logprob_e = logits_e - shift_e
        logprob_a = logits_a - shift_a
        return logprob_e - logprob_a - penalty_slope * jnp.maximum(cuts - logprob_e, 0.0)

    return [peak_e - log_total_e, peak_a - log_total_a], score


def finish_kernel(stats_ref, gap_ref, top_ref, peaks_ref, chosen_ref, lacking_ref):
    peaks, score = totals_of(stats_ref, gap_ref)
    stats = stats_ref[...]
    for i, peak in enumerate(peaks):
        peaks_ref[i:i + 1, :] = row_from(peak)
    picks = [jnp.sum(lane_at(stats, i), axis=0) for i in (4, 5)]
    chosen_ref[...] = row_from(score(*picks))
    lane = lax.broadcasted_iota(jnp.int32, stats.shape[1:], 1)
    is_candidate = (lane >= FIRST) & (lane < FIRST + 2 * (NEAR + TOP))
    parts, lacking = [], jnp.zeros(stats.shape[1:], jnp.float32)
    for plane in range(stats.shape[0]):
        e, a = stats[plane], pltpu.roll(stats[plane], 64, 1)
        value = jnp.where(e > dead_below, score(e, a), masked_floor)
        parts.append(jnp.where(is_candidate, value, -jnp.inf))
        lacking = jnp.maximum(lacking, jnp.where(lane == 6, e, 0.0))
    top_ref[...] = lanes_of(best_of(sorted_levels(parts)), top_ref.shape)
    lacking_ref[0] = jnp.where(jnp.max(lacking) > 0.0, 1, 0).astype(jnp.int32)


def score_kernel(width, table_ref, stats_ref, gap_ref, best_ref):
    _, score = totals_of(stats_ref, gap_ref, 2)
    own = table_ref.shape[1] // 2
    real = lax.broadcasted_iota(jnp.int32, (2 * own, 128), 1) < width // 2
    parts = []
    for source in range(table_ref.shape[0]):
        e, a = table_ref[source, :, 0:128], table_ref[source, :, 128:256]
        parts.append(jnp.where(real & (e > dead_below), score(e, a), masked_floor))
    found = best_of(sorted_levels(parts))
    found = [value[:own] for value in found] + [value[own:] for value in found]
    best = lanes_of(found, best_ref.shape[1:])
    for plane in range(best_ref.shape[0]):
        best_ref[plane] = best


def merge_kernel(parts_ref, out_ref):
    shape = parts_ref.shape[1:]
    real = lax.broadcasted_iota(jnp.int32, shape, 1) < 2 * TOP
    parts = [jnp.where(real, parts_ref[i], -jnp.inf) for i in range(parts_ref.shape[0])]
    out_ref[...] = lanes_of(best_of(sorted_levels(parts)), out_ref.shape)


def per_device(
    expert_hidden,
    expert_gain,
    expert_head,
    amateur_hidden,
    amateur_gain,
    amateur_head,
    live_mask,
    token_ids,
    plaus_level,
):
    own, depth_e = expert_hidden.shape
    depth_a = amateur_hidden.shape[1]
    width = expert_head.shape[0]
    rows, planes = lax.axis_size("rows"), lax.axis_size("vocab")
    beams = own * rows
    quarter = (depth_e + depth_a) // 4
    row, plane = lax.axis_index("rows"), lax.axis_index("vocab")
    position = jnp.stack([row % NC, (row * planes + plane) * width]).astype(jnp.int32)
    ids = token_ids.reshape(rows, own, 1)
    gap = lax.dynamic_slice_in_dim(plaus_level, row * own, own, 0).reshape(own, 1)

    norm_inputs = (
        expert_hidden, expert_gain.reshape(-1, 128), amateur_hidden, amateur_gain.reshape(-1, 128)
    )
    blocks = pl.pallas_call(
        norm_kernel,
        out_shape=jax.ShapeDtypeStruct((rows, 2 * own, quarter), jnp.bfloat16),
        in_specs=[HBM] * 4,
        out_specs=VMEM,
        scratch_shapes=[pltpu.VMEM(x.shape, x.dtype) for x in norm_inputs]
        + [pltpu.SemaphoreType.DMA((4,))],
        compiler_params=WIDE_PARAMS,
        name="norms",
    )(*norm_inputs)
    half = lax.all_to_all(blocks, "rows", 0, 0, tiled=True).reshape(2 * beams, quarter)
    other_half = lax.ppermute(half, "rows", [(r, r ^ 1) for r in range(rows)])
    cost = pl.CostEstimate(
        flops=4 * beams * width * 2 * quarter, bytes_accessed=4 * beams * quarter, transcendentals=0
    )
    buffers = [pltpu.VMEM((2, 2, 2 * beams, width), jnp.float32)]
    first = pl.pallas_call(
        first_kernel,
        out_shape=jax.ShapeDtypeStruct((2, rows, own, width), jnp.float32),
        in_specs=[SMEM] + [VMEM] * 3,
        out_specs=VMEM,
        scratch_shapes=buffers,
        compiler_params=PARAMS,
        cost_estimate=cost,
        name="first_half",
    )(position, half, expert_head, amateur_head)
    table = pl.pallas_call(
        second_kernel,
        out_shape=jax.ShapeDtypeStruct((rows, 2 * own, 256), jnp.float32),
        in_specs=[SMEM] + [VMEM] * 6,
        out_specs=VMEM,
        scratch_shapes=buffers,
        compiler_params=PARAMS,
        cost_estimate=cost,
        name="second_half",
    )(position, other_half, expert_head, amateur_head, first, live_mask.reshape(1, -1), ids)
    table = lax.all_to_all(table, "rows", 0, 0, tiled=True)

    small = jax.ShapeDtypeStruct((planes, own, 128), jnp.float32)
    best_shape = jax.ShapeDtypeStruct((own, TOP), jnp.float32)
    stats = pl.pallas_call(
        functools.partial(stats_kernel, width),
        out_shape=small,
        in_specs=[VMEM] * 2,
        out_specs=VMEM,
        compiler_params=PARAMS,
        name="stats",
    )(table, gap)
    stats = lax.all_to_all(stats, "vocab", 0, 0, tiled=True)
    top, peaks, chosen, lacking = pl.pallas_call(
        finish_kernel,
        out_shape=(
            best_shape,
            jax.ShapeDtypeStruct((2, own), jnp.float32),
            jax.ShapeDtypeStruct((1, own), jnp.float32),
            jax.ShapeDtypeStruct((1,), jnp.int32),
        ),
        in_specs=[VMEM] * 2,
        out_specs=(VMEM, VMEM, VMEM, SMEM),
        compiler_params=PARAMS,
        name="finish",
    )(stats, gap)

    def with_every_entry(table, stats, gap, _):
        best = pl.pallas_call(
            functools.partial(score_kernel, width),
            out_shape=small,
            in_specs=[VMEM] * 3,
            out_specs=VMEM,
            compiler_params=PARAMS,
            name="scores",
        )(table, stats, gap)
        best = lax.all_to_all(best, "vocab", 0, 0, tiled=True)
        return pl.pallas_call(
            merge_kernel,
            out_shape=best_shape,
            in_specs=[VMEM],
            out_specs=VMEM,
            compiler_params=PARAMS,
            name="merge",
        )(best)

    top = lax.cond(lacking[0] > 0, with_every_entry, lambda *args: args[-1], table, stats, gap, top)
    return top, peaks.T, chosen.reshape(own)


def solution(mesh):
    in_specs = (
        P("rows", None),
        P(),
        P(("rows", "vocab"), None),
        P("rows", None),
        P(),
        P(("rows", "vocab"), None),
        P(("rows", "vocab")),
        P(),
        P(),
    )
    out_specs = (P("rows", None), P("rows", None), P("rows"))
    return jax.shard_map(
        per_device, mesh=mesh, in_specs=in_specs, out_specs=out_specs, check_vma=False
    )
```

```python
import functools

import jax
import jax.numpy as jnp
from jax import lax
from jax.experimental import pallas as pl
from jax.experimental.pallas import tpu as pltpu
from jax.sharding import PartitionSpec as P

TOP = 4
NEAR = 20
FIRST = 16
NC = 2

masked_floor = -1e30
dead_below = -5e29
penalty_slope = 2.0
norm_epsilon = 1e-06

VMEM = pl.BlockSpec(memory_space=pltpu.VMEM)
HBM = pl.BlockSpec(memory_space=pltpu.HBM)
SMEM = pl.BlockSpec(memory_space=pltpu.SMEM)
WIDE_PARAMS = pltpu.CompilerParams(vmem_limit_bytes=60 * 1024 * 1024)
PARAMS = pltpu.CompilerParams(vmem_limit_bytes=16 * 1024 * 1024)


def norm_kernel(*refs):
    inputs, out_ref, held, block_ref, sems, out_sems = refs[:4], refs[4], refs[5:9], *refs[9:]
    copies = [pltpu.make_async_copy(inputs[i], held[i], sems.at[i]) for i in range(4)]
    for copy in copies:
        copy.start()
    quarters = []
    for model in range(2):
        copies[2 * model].wait()
        copies[2 * model + 1].wait()
        values = held[2 * model][...].astype(jnp.float32)
        gain = held[2 * model + 1][...].astype(jnp.float32)
        mean = jnp.mean(values * values, axis=-1, keepdims=True)
        values = values * lax.rsqrt(mean + norm_epsilon)
        chunks = [
            values[:, 128 * i:128 * i + 128] * gain[i:i + 1, :] for i in range(values.shape[1] // 128)
        ]
        each = len(chunks) // 4
        quarters.append([chunks[each * q:each * q + each] for q in range(4)])
    sent = []
    for core in range(NC):
        rows = [quarters[0][2 * core + p] + quarters[1][2 * core + p] for p in range(2)]
        for i, pair in enumerate(zip(*rows)):
            block_ref[core, :, 128 * i:128 * i + 128] = jnp.concatenate(pair).astype(jnp.bfloat16)
        for dest in range(core, out_ref.shape[0], NC):
            sent.append(pltpu.make_async_copy(block_ref.at[core], out_ref.at[dest], out_sems.at[dest]))
            sent[-1].start()
    for copy in sent:
        copy.wait()


def half_sums(core, part_ref, head_refs, acc_ref):
    low = 0
    for model, head in enumerate(head_refs):
        size = head.shape[1] // 4
        for p in range(2):
            columns = pl.ds(pl.multiple_of((2 * core + p) * size, 128), size)
            acc_ref[model, p] = lax.dot_general(
                part_ref[:, low:low + size], head[:, columns], (((1,), (1,)), ((), ())),
                preferred_element_type=jnp.float32,
            )
        low += size


def quarters_joined(acc_ref, model, owner, own):
    at = 2 * own * owner
    return acc_ref[model, 0, at:at + own, :] + acc_ref[model, 1, at + own:at + 2 * own, :]


def first_kernel(pos_ref, part_ref, he_ref, ha_ref, out_ref, acc_ref):
    half_sums(pos_ref[0], part_ref, (he_ref, ha_ref), acc_ref)
    for model in range(2):
        for owner in range(out_ref.shape[1]):
            out_ref[model, owner] = quarters_joined(acc_ref, model, owner, out_ref.shape[2])


def second_kernel(
    pos_ref, part_ref, he_ref, ha_ref, first_ref, live_ref, ids_ref, out_ref, acc_ref
):
    width = he_ref.shape[0]
    own = ids_ref.shape[1]
    half_sums(1 - pos_ref[0], part_ref, (he_ref, ha_ref), acc_ref)
    live = live_ref[...] == 1
    positions = pos_ref[1] + lax.broadcasted_iota(jnp.int32, (1, width), 1)
    half = width // 2
    for owner in range(out_ref.shape[0]):
        hits = ids_ref[owner] == positions
        for model in range(2):
            logits = first_ref[model, owner] + quarters_joined(acc_ref, model, owner, own)
            pick = jnp.sum(jnp.where(hits, logits, 0.0), axis=1, keepdims=True)
            pick = jnp.broadcast_to(pick, (own, 128 - half))
            held = jnp.where(live, logits, masked_floor)
            low = 128 * model
            for side in range(2):
                rows = slice(own * side, own * side + own)
                out_ref[owner, rows, low:low + half] = held[:, half * side:half * side + half]
                out_ref[owner, rows, low + half:low + 128] = pick


def lanes_of(columns, shape):
    lane = lax.broadcasted_iota(jnp.int32, shape, len(shape) - 1)
    result = jnp.zeros(shape, jnp.float32)
    for i, column in enumerate(columns):
        result = jnp.where(lane == i, column, result)
    return result


def lane_at(values, i):
    lane = lax.broadcasted_iota(jnp.int32, values.shape, values.ndim - 1)
    return jnp.sum(jnp.where(lane == i, values, 0.0), axis=-1, keepdims=True)


def total_rows(values):
    return jnp.sum(values, axis=1, keepdims=True)


def insert(levels, entry):
    for i, level in enumerate(levels):
        above = entry[0] > level[0]
        levels[i] = tuple(jnp.where(above, new, old) for new, old in zip(entry, level))
        entry = tuple(jnp.where(above, old, new) for new, old in zip(entry, level))


def remove_top(levels, top):
    hit = levels[0][0] == top
    payload = [total_rows(jnp.where(hit, field, 0.0)) for field in levels[0][1:]]
    count = total_rows(jnp.where(hit, 1.0, 0.0))
    last = tuple(jnp.full_like(f, masked_floor) for f in levels[0])
    lower = levels[1:] + [last]
    return payload, count, [
        tuple(jnp.where(hit, new, old) for new, old in zip(low, level))
        for low, level in zip(lower, levels)
    ]


def stats_kernel(width, table_ref, gap_ref, out_ref):
    sources, own = table_ref.shape[0], table_ref.shape[1] // 2
    shape = (2 * own, 128)
    real = lax.broadcasted_iota(jnp.int32, shape, 1) < width // 2
    columns = []
    for model in range(2):
        parts = [table_ref[i, :, 128 * model:128 * model + 128] for i in range(sources)]
        peak = functools.reduce(jnp.maximum, parts)
        peak = jnp.max(jnp.where(real, peak, masked_floor), axis=1, keepdims=True)
        peak = jnp.maximum(peak[:own], peak[own:])
        both = jnp.concatenate([peak, peak])
        total = functools.reduce(jnp.add, [jnp.exp(part - both) for part in parts])
        total = total_rows(jnp.where(real, total, 0.0))
        pick = lane_at(functools.reduce(jnp.add, parts), width // 2)
        columns.append((peak, total[:own] + total[own:], pick[:own]))
    (pe, te, ce), (pa, ta, ca) = columns
    least = pe - gap_ref[...].astype(jnp.float32) * 0.1
    least = jnp.concatenate([least, least])
    floor = jnp.full(shape, masked_floor, jnp.float32)
    near, rest = [(floor,) * 2] * TOP, [(floor,) * 3] * TOP
    count = jnp.zeros(shape, jnp.float32)
    for i in range(sources):
        e, a = table_ref[i, :, 0:128], table_ref[i, :, 128:256]
        live = real & (e > dead_below)
        is_near = live & (e >= least)
        count += jnp.where(is_near, 1.0, 0.0)
        insert(near, (jnp.where(is_near, e, masked_floor), a))
        insert(rest, (jnp.where(live & (e < least), 3.0 * e - a, masked_floor), e, a))
    missing = total_rows(count)
    picked = []
    for _ in range(NEAR):
        top = jnp.max(near[0][0], axis=1, keepdims=True)
        (a,), hits, near = remove_top(near, top)
        found = top > dead_below
        picked.append((jnp.where(found, top, masked_floor), a))
        missing -= jnp.where(found & (hits == 1.0), 1.0, 0.0)
    for _ in range(TOP):
        top = jnp.max(rest[0][0], axis=1, keepdims=True)
        (e, a), hits, rest = remove_top(rest, top)
        found = top > dead_below
        picked.append((jnp.where(found, e, masked_floor), a))
        missing += jnp.where(found & (hits > 1.0), 1.0, 0.0)
    zeros = [jnp.zeros_like(missing)]
    lanes = zeros * FIRST + [e for e, _ in picked]
    lanes += zeros * (64 + FIRST - len(lanes)) + [a for _, a in picked]
    lanes = lanes_of(lanes, shape)
    stats = lanes_of([pe, pa, te, ta, ce, ca, missing[:own] + missing[own:]], (own, 128))
    stats += lanes[:own] + pltpu.roll(lanes, len(picked), 1)[own:]
    for plane in range(out_ref.shape[0]):
        out_ref[plane] = stats


def best_of(levels):
    tops, counts, seen = [], [], 0.0
    for _ in range(TOP):
        top = jnp.max(levels[0], axis=1, keepdims=True)
        hit = levels[0] == top
        seen = seen + total_rows(jnp.where(hit, 1.0, 0.0))
        tops.append(top)
        counts.append(seen)
        lower = levels[1:] + [jnp.full_like(levels[0], -jnp.inf)]
        levels = [jnp.where(hit, low, level) for level, low in zip(levels, lower)]
    found = []
    for i in range(TOP):
        value = tops[-1]
        for top, seen in reversed(list(zip(tops, counts))):
            value = jnp.where(seen > i, top, value)
        found.append(value)
    return found


def sorted_levels(parts):
    levels = [jnp.full_like(parts[0], -jnp.inf)] * TOP
    for part in parts:
        for i in range(TOP):
            levels[i], part = jnp.maximum(levels[i], part), jnp.minimum(levels[i], part)
    return levels


def row_from(column):
    shape = (column.shape[0], column.shape[0])
    here = lax.broadcasted_iota(jnp.int32, shape, 0) == lax.broadcasted_iota(jnp.int32, shape, 1)
    return jnp.sum(jnp.where(here, column, 0.0), axis=0, keepdims=True)


def totals_of(stats_ref, gap_ref, copies=1):
    stats = stats_ref[...]
    peak_e, peak_a, sum_e, sum_a = [lane_at(stats, i) for i in range(4)]

    def total_of(peaks, sums):
        peak = jnp.max(peaks, axis=0)
        return peak, peak + jnp.log(jnp.sum(sums * jnp.exp(peaks - peak[None]), axis=0))

    peak_e, log_total_e = total_of(peak_e, sum_e)
    peak_a, log_total_a = total_of(peak_a, sum_a)
    cut = peak_e - log_total_e - gap_ref[...].astype(jnp.float32) * 0.1
    shift_e, shift_a, cuts = [
        jnp.concatenate([x] * copies) if copies > 1 else x for x in (log_total_e, log_total_a, cut)
    ]

    def score(logits_e, logits_a):
        logprob_e = logits_e - shift_e
        logprob_a = logits_a - shift_a
        return logprob_e - logprob_a - penalty_slope * jnp.maximum(cuts - logprob_e, 0.0)

    return [peak_e - log_total_e, peak_a - log_total_a], score


def finish_kernel(stats_ref, gap_ref, top_ref, peaks_ref, chosen_ref, lacking_ref):
    peaks, score = totals_of(stats_ref, gap_ref)
    stats = stats_ref[...]
    for i, peak in enumerate(peaks):
        peaks_ref[i:i + 1, :] = row_from(peak)
    picks = [jnp.sum(lane_at(stats, i), axis=0) for i in (4, 5)]
    chosen_ref[...] = row_from(score(*picks))
    lane = lax.broadcasted_iota(jnp.int32, stats.shape[1:], 1)
    is_candidate = (lane >= FIRST) & (lane < FIRST + 2 * (NEAR + TOP))
    parts, lacking = [], jnp.zeros(stats.shape[1:], jnp.float32)
    for plane in range(stats.shape[0]):
        e, a = stats[plane], pltpu.roll(stats[plane], 64, 1)
        value = jnp.where(e > dead_below, score(e, a), masked_floor)
        parts.append(jnp.where(is_candidate, value, -jnp.inf))
        lacking = jnp.maximum(lacking, jnp.where(lane == 6, e, 0.0))
    top_ref[...] = lanes_of(best_of(sorted_levels(parts)), top_ref.shape)
    lacking_ref[0] = jnp.where(jnp.max(lacking) > 0.0, 1, 0).astype(jnp.int32)


def score_kernel(width, table_ref, stats_ref, gap_ref, best_ref):
    _, score = totals_of(stats_ref, gap_ref, 2)
    own = table_ref.shape[1] // 2
    real = lax.broadcasted_iota(jnp.int32, (2 * own, 128), 1) < width // 2
    parts = []
    for source in range(table_ref.shape[0]):
        e, a = table_ref[source, :, 0:128], table_ref[source, :, 128:256]
        parts.append(jnp.where(real & (e > dead_below), score(e, a), masked_floor))
    found = best_of(sorted_levels(parts))
    found = [value[:own] for value in found] + [value[own:] for value in found]
    best = lanes_of(found, best_ref.shape[1:])
    for plane in range(best_ref.shape[0]):
        best_ref[plane] = best


def merge_kernel(parts_ref, out_ref):
    shape = parts_ref.shape[1:]
    real = lax.broadcasted_iota(jnp.int32, shape, 1) < 2 * TOP
    parts = [jnp.where(real, parts_ref[i], -jnp.inf) for i in range(parts_ref.shape[0])]
    out_ref[...] = lanes_of(best_of(sorted_levels(parts)), out_ref.shape)


def per_device(
    expert_hidden,
    expert_gain,
    expert_head,
    amateur_hidden,
    amateur_gain,
    amateur_head,
    live_mask,
    token_ids,
    plaus_level,
):
    own, depth_e = expert_hidden.shape
    depth_a = amateur_hidden.shape[1]
    width = expert_head.shape[0]
    rows, planes = lax.axis_size("rows"), lax.axis_size("vocab")
    beams = own * rows
    quarter = (depth_e + depth_a) // 4
    row, plane = lax.axis_index("rows"), lax.axis_index("vocab")
    position = jnp.stack([row % NC, (row * planes + plane) * width]).astype(jnp.int32)
    ids = token_ids.reshape(rows, own, 1)
    gap = lax.dynamic_slice_in_dim(plaus_level, row * own, own, 0).reshape(own, 1)

    norm_inputs = (
        expert_hidden, expert_gain.reshape(-1, 128), amateur_hidden, amateur_gain.reshape(-1, 128)
    )
    blocks = pl.pallas_call(
        norm_kernel,
        out_shape=jax.ShapeDtypeStruct((rows, 2 * own, quarter), jnp.bfloat16),
        in_specs=[HBM] * 4,
        out_specs=HBM,
        scratch_shapes=[pltpu.VMEM(x.shape, x.dtype) for x in norm_inputs] + [
            pltpu.VMEM((NC, 2 * own, quarter), jnp.bfloat16),
            pltpu.SemaphoreType.DMA((4,)),
            pltpu.SemaphoreType.DMA((rows,)),
        ],
        compiler_params=WIDE_PARAMS,
        name="norms",
    )(*norm_inputs)
    half = lax.all_to_all(blocks, "rows", 0, 0, tiled=True).reshape(2 * beams, quarter)
    other_half = lax.ppermute(half, "rows", [(r, r ^ 1) for r in range(rows)])
    cost = pl.CostEstimate(
        flops=4 * beams * width * 2 * quarter, bytes_accessed=4 * beams * quarter, transcendentals=0
    )
    buffers = [pltpu.VMEM((2, 2, 2 * beams, width), jnp.float32)]
    first = pl.pallas_call(
        first_kernel,
        out_shape=jax.ShapeDtypeStruct((2, rows, own, width), jnp.float32),
        in_specs=[SMEM] + [VMEM] * 3,
        out_specs=VMEM,
        scratch_shapes=buffers,
        compiler_params=PARAMS,
        cost_estimate=cost,
        name="first_half",
    )(position, half, expert_head, amateur_head)
    table = pl.pallas_call(
        second_kernel,
        out_shape=jax.ShapeDtypeStruct((rows, 2 * own, 256), jnp.float32),
        in_specs=[SMEM] + [VMEM] * 6,
        out_specs=VMEM,
        scratch_shapes=buffers,
        compiler_params=PARAMS,
        cost_estimate=cost,
        name="second_half",
    )(position, other_half, expert_head, amateur_head, first, live_mask.reshape(1, -1), ids)
    table = lax.all_to_all(table, "rows", 0, 0, tiled=True)

    small = jax.ShapeDtypeStruct((planes, own, 128), jnp.float32)
    best_shape = jax.ShapeDtypeStruct((own, TOP), jnp.float32)
    stats = pl.pallas_call(
        functools.partial(stats_kernel, width),
        out_shape=small,
        in_specs=[VMEM] * 2,
        out_specs=VMEM,
        compiler_params=PARAMS,
        name="stats",
    )(table, gap)
    stats = lax.all_to_all(stats, "vocab", 0, 0, tiled=True)
    top, peaks, chosen, lacking = pl.pallas_call(
        finish_kernel,
        out_shape=(
            best_shape,
            jax.ShapeDtypeStruct((2, own), jnp.float32),
            jax.ShapeDtypeStruct((1, own), jnp.float32),
            jax.ShapeDtypeStruct((1,), jnp.int32),
        ),
        in_specs=[VMEM] * 2,
        out_specs=(VMEM, VMEM, VMEM, SMEM),
        compiler_params=PARAMS,
        name="finish",
    )(stats, gap)

    def with_every_entry(table, stats, gap, _):
        best = pl.pallas_call(
            functools.partial(score_kernel, width),
            out_shape=small,
            in_specs=[VMEM] * 3,
            out_specs=VMEM,
            compiler_params=PARAMS,
            name="scores",
        )(table, stats, gap)
        best = lax.all_to_all(best, "vocab", 0, 0, tiled=True)
        return pl.pallas_call(
            merge_kernel,
            out_shape=best_shape,
            in_specs=[VMEM],
            out_specs=VMEM,
            compiler_params=PARAMS,
            name="merge",
        )(best)

    top = lax.cond(lacking[0] > 0, with_every_entry, lambda *args: args[-1], table, stats, gap, top)
    return top, peaks.T, chosen.reshape(own)


def solution(mesh):
    in_specs = (
        P("rows", None),
        P(),
        P(("rows", "vocab"), None),
        P("rows", None),
        P(),
        P(("rows", "vocab"), None),
        P(("rows", "vocab")),
        P(),
        P(),
    )
    out_specs = (P("rows", None), P("rows", None), P("rows"))
    return jax.shard_map(
        per_device, mesh=mesh, in_specs=in_specs, out_specs=out_specs, check_vma=False
    )
```

```python
import functools

import jax
import jax.numpy as jnp
from jax import lax
from jax.experimental import pallas as pl
from jax.experimental.pallas import tpu as pltpu
from jax.sharding import PartitionSpec as P

TOP = 4
NEAR = 20
FIRST = 16
NC = 2

masked_floor = -1e30
dead_below = -5e29
penalty_slope = 2.0
norm_epsilon = 1e-06

VMEM = pl.BlockSpec(memory_space=pltpu.VMEM)
HBM = pl.BlockSpec(memory_space=pltpu.HBM)
SMEM = pl.BlockSpec(memory_space=pltpu.SMEM)
WIDE_PARAMS = pltpu.CompilerParams(vmem_limit_bytes=60 * 1024 * 1024)
PARAMS = pltpu.CompilerParams(vmem_limit_bytes=16 * 1024 * 1024)


def norm_kernel(*refs):
    inputs, out_ref, held, block_ref, sems, out_sems = refs[:4], refs[4], refs[5:9], *refs[9:]
    copies = [pltpu.make_async_copy(inputs[i], held[i], sems.at[i]) for i in range(4)]
    for copy in copies:
        copy.start()
    quarters = []
    for model in range(2):
        copies[2 * model].wait()
        copies[2 * model + 1].wait()
        values = held[2 * model][...].astype(jnp.float32)
        gain = held[2 * model + 1][...].astype(jnp.float32)
        mean = jnp.mean(values * values, axis=-1, keepdims=True)
        values = values * lax.rsqrt(mean + norm_epsilon)
        chunks = [
            values[:, 128 * i:128 * i + 128] * gain[i:i + 1, :] for i in range(values.shape[1] // 128)
        ]
        each = len(chunks) // 4
        quarters.append([chunks[each * q:each * q + each] for q in range(4)])
    sent = []
    for core in range(NC):
        rows = [quarters[0][2 * core + p] + quarters[1][2 * core + p] for p in range(2)]
        for i, pair in enumerate(zip(*rows)):
            block_ref[core, :, 128 * i:128 * i + 128] = jnp.concatenate(pair).astype(jnp.bfloat16)
        for dest in range(core, out_ref.shape[0], NC):
            sent.append(pltpu.make_async_copy(block_ref.at[core], out_ref.at[dest], out_sems.at[dest]))
            sent[-1].start()
    for copy in sent:
        copy.wait()


def quarters_apart(part):
    groups = part.reshape(part.shape[0] // 32, 2, 16, part.shape[1])
    even, odd = groups[:, 0], groups[:, 1]
    first = lax.broadcasted_iota(jnp.int32, even.shape, 1) % 8 < 4
    down = pltpu.roll(odd, 4, 1)
    up = pltpu.roll(even, 12, 1)
    apart = jnp.where(first, even, down), jnp.where(first, up, odd)
    return [x.reshape(part.shape[0] // 2, part.shape[1]) for x in apart]


def half_sums(core, part_ref, head_refs, acc_ref):
    low = 0
    for model, head in enumerate(head_refs):
        size = head.shape[1] // 4
        total = None
        for p, rows in enumerate(quarters_apart(part_ref[:, low:low + size])):
            columns = pl.ds(pl.multiple_of((2 * core + p) * size, 128), size)
            product = lax.dot_general(
                rows, head[:, columns], (((1,), (1,)), ((), ())), preferred_element_type=jnp.float32
            )
            total = product if total is None else total + product
        acc_ref[model] = total
        low += size


def sums_of(acc_ref, model, owner, own):
    at = 4 * own * (owner // 4) + own * (0, 2, 1, 3)[owner % 4]
    return acc_ref[model, at:at + own, :]


def first_kernel(pos_ref, part_ref, he_ref, ha_ref, out_ref, acc_ref):
    half_sums(pos_ref[0], part_ref, (he_ref, ha_ref), acc_ref)
    for model in range(2):
        for owner in range(out_ref.shape[1]):
            out_ref[model, owner] = sums_of(acc_ref, model, owner, out_ref.shape[2])


def second_kernel(
    pos_ref, part_ref, he_ref, ha_ref, first_ref, live_ref, ids_ref, out_ref, acc_ref
):
    width = he_ref.shape[0]
    own = ids_ref.shape[1]
    half_sums(1 - pos_ref[0], part_ref, (he_ref, ha_ref), acc_ref)
    live = live_ref[...] == 1
    positions = pos_ref[1] + lax.broadcasted_iota(jnp.int32, (1, width), 1)
    half = width // 2
    for owner in range(out_ref.shape[0]):
        hits = ids_ref[owner] == positions
        for model in range(2):
            logits = first_ref[model, owner] + sums_of(acc_ref, model, owner, own)
            pick = jnp.sum(jnp.where(hits, logits, 0.0), axis=1, keepdims=True)
            pick = jnp.broadcast_to(pick, (own, 128 - half))
            held = jnp.where(live, logits, masked_floor)
            low = 128 * model
            for side in range(2):
                rows = slice(own * side, own * side + own)
                out_ref[owner, rows, low:low + half] = held[:, half * side:half * side + half]
                out_ref[owner, rows, low + half:low + 128] = pick


def lanes_of(columns, shape):
    lane = lax.broadcasted_iota(jnp.int32, shape, len(shape) - 1)
    result = jnp.zeros(shape, jnp.float32)
    for i, column in enumerate(columns):
        result = jnp.where(lane == i, column, result)
    return result


def lane_at(values, i):
    lane = lax.broadcasted_iota(jnp.int32, values.shape, values.ndim - 1)
    return jnp.sum(jnp.where(lane == i, values, 0.0), axis=-1, keepdims=True)


def total_rows(values):
    return jnp.sum(values, axis=1, keepdims=True)


def insert(levels, entry):
    for i, level in enumerate(levels):
        above = entry[0] > level[0]
        levels[i] = tuple(jnp.where(above, new, old) for new, old in zip(entry, level))
        entry = tuple(jnp.where(above, old, new) for new, old in zip(entry, level))


def remove_top(levels, top):
    hit = levels[0][0] == top
    payload = [total_rows(jnp.where(hit, field, 0.0)) for field in levels[0][1:]]
    count = total_rows(jnp.where(hit, 1.0, 0.0))
    last = tuple(jnp.full_like(f, masked_floor) for f in levels[0])
    lower = levels[1:] + [last]
    return payload, count, [
        tuple(jnp.where(hit, new, old) for new, old in zip(low, level))
        for low, level in zip(lower, levels)
    ]


def stats_kernel(width, table_ref, gap_ref, out_ref):
    sources, own = table_ref.shape[0], table_ref.shape[1] // 2
    shape = (2 * own, 128)
    real = lax.broadcasted_iota(jnp.int32, shape, 1) < width // 2
    columns = []
    for model in range(2):
        parts = [table_ref[i, :, 128 * model:128 * model + 128] for i in range(sources)]
        peak = functools.reduce(jnp.maximum, parts)
        peak = jnp.max(jnp.where(real, peak, masked_floor), axis=1, keepdims=True)
        peak = jnp.maximum(peak[:own], peak[own:])
        both = jnp.concatenate([peak, peak])
        total = functools.reduce(jnp.add, [jnp.exp(part - both) for part in parts])
        total = total_rows(jnp.where(real, total, 0.0))
        pick = lane_at(functools.reduce(jnp.add, parts), width // 2)
        columns.append((peak, total[:own] + total[own:], pick[:own]))
    (pe, te, ce), (pa, ta, ca) = columns
    least = pe - gap_ref[...].astype(jnp.float32) * 0.1
    least = jnp.concatenate([least, least])
    floor = jnp.full(shape, masked_floor, jnp.float32)
    near, rest = [(floor,) * 2] * TOP, [(floor,) * 3] * TOP
    count = jnp.zeros(shape, jnp.float32)
    for i in range(sources):
        e, a = table_ref[i, :, 0:128], table_ref[i, :, 128:256]
        live = real & (e > dead_below)
        is_near = live & (e >= least)
        count += jnp.where(is_near, 1.0, 0.0)
        insert(near, (jnp.where(is_near, e, masked_floor), a))
        insert(rest, (jnp.where(live & (e < least), 3.0 * e - a, masked_floor), e, a))
    missing = total_rows(count)
    picked = []
    for _ in range(NEAR):
        top = jnp.max(near[0][0], axis=1, keepdims=True)
        (a,), hits, near = remove_top(near, top)
        found = top > dead_below
        picked.append((jnp.where(found, top, masked_floor), a))
        missing -= jnp.where(found & (hits == 1.0), 1.0, 0.0)
    for _ in range(TOP):
        top = jnp.max(rest[0][0], axis=1, keepdims=True)
        (e, a), hits, rest = remove_top(rest, top)
        found = top > dead_below
        picked.append((jnp.where(found, e, masked_floor), a))
        missing += jnp.where(found & (hits > 1.0), 1.0, 0.0)
    zeros = [jnp.zeros_like(missing)]
    lanes = zeros * FIRST + [e for e, _ in picked]
    lanes += zeros * (64 + FIRST - len(lanes)) + [a for _, a in picked]
    lanes = lanes_of(lanes, shape)
    stats = lanes_of([pe, pa, te, ta, ce, ca, missing[:own] + missing[own:]], (own, 128))
    stats += lanes[:own] + pltpu.roll(lanes, len(picked), 1)[own:]
    for plane in range(out_ref.shape[0]):
        out_ref[plane] = stats


def best_of(levels):
    tops, counts, seen = [], [], 0.0
    for _ in range(TOP):
        top = jnp.max(levels[0], axis=1, keepdims=True)
        hit = levels[0] == top
        seen = seen + total_rows(jnp.where(hit, 1.0, 0.0))
        tops.append(top)
        counts.append(seen)
        lower = levels[1:] + [jnp.full_like(levels[0], -jnp.inf)]
        levels = [jnp.where(hit, low, level) for level, low in zip(levels, lower)]
    found = []
    for i in range(TOP):
        value = tops[-1]
        for top, seen in reversed(list(zip(tops, counts))):
            value = jnp.where(seen > i, top, value)
        found.append(value)
    return found


def sorted_levels(parts):
    levels = [jnp.full_like(parts[0], -jnp.inf)] * TOP
    for part in parts:
        for i in range(TOP):
            levels[i], part = jnp.maximum(levels[i], part), jnp.minimum(levels[i], part)
    return levels


def row_from(column):
    shape = (column.shape[0], column.shape[0])
    here = lax.broadcasted_iota(jnp.int32, shape, 0) == lax.broadcasted_iota(jnp.int32, shape, 1)
    return jnp.sum(jnp.where(here, column, 0.0), axis=0, keepdims=True)


def totals_of(stats_ref, gap_ref, copies=1):
    stats = stats_ref[...]
    peak_e, peak_a, sum_e, sum_a = [lane_at(stats, i) for i in range(4)]

    def total_of(peaks, sums):
        peak = jnp.max(peaks, axis=0)
        return peak, peak + jnp.log(jnp.sum(sums * jnp.exp(peaks - peak[None]), axis=0))

    peak_e, log_total_e = total_of(peak_e, sum_e)
    peak_a, log_total_a = total_of(peak_a, sum_a)
    cut = peak_e - log_total_e - gap_ref[...].astype(jnp.float32) * 0.1
    shift_e, shift_a, cuts = [
        jnp.concatenate([x] * copies) if copies > 1 else x for x in (log_total_e, log_total_a, cut)
    ]

    def score(logits_e, logits_a):
        logprob_e = logits_e - shift_e
        logprob_a = logits_a - shift_a
        return logprob_e - logprob_a - penalty_slope * jnp.maximum(cuts - logprob_e, 0.0)

    return [peak_e - log_total_e, peak_a - log_total_a], score


def finish_kernel(stats_ref, gap_ref, top_ref, peaks_ref, chosen_ref, lacking_ref):
    peaks, score = totals_of(stats_ref, gap_ref)
    stats = stats_ref[...]
    for i, peak in enumerate(peaks):
        peaks_ref[i:i + 1, :] = row_from(peak)
    picks = [jnp.sum(lane_at(stats, i), axis=0) for i in (4, 5)]
    chosen_ref[...] = row_from(score(*picks))
    lane = lax.broadcasted_iota(jnp.int32, stats.shape[1:], 1)
    is_candidate = (lane >= FIRST) & (lane < FIRST + 2 * (NEAR + TOP))
    parts, lacking = [], jnp.zeros(stats.shape[1:], jnp.float32)
    for plane in range(stats.shape[0]):
        e, a = stats[plane], pltpu.roll(stats[plane], 64, 1)
        value = jnp.where(e > dead_below, score(e, a), masked_floor)
        parts.append(jnp.where(is_candidate, value, -jnp.inf))
        lacking = jnp.maximum(lacking, jnp.where(lane == 6, e, 0.0))
    top_ref[...] = lanes_of(best_of(sorted_levels(parts)), top_ref.shape)
    lacking_ref[0] = jnp.where(jnp.max(lacking) > 0.0, 1, 0).astype(jnp.int32)


def score_kernel(width, table_ref, stats_ref, gap_ref, best_ref):
    _, score = totals_of(stats_ref, gap_ref, 2)
    own = table_ref.shape[1] // 2
    real = lax.broadcasted_iota(jnp.int32, (2 * own, 128), 1) < width // 2
    parts = []
    for source in range(table_ref.shape[0]):
        e, a = table_ref[source, :, 0:128], table_ref[source, :, 128:256]
        parts.append(jnp.where(real & (e > dead_below), score(e, a), masked_floor))
    found = best_of(sorted_levels(parts))
    found = [value[:own] for value in found] + [value[own:] for value in found]
    best = lanes_of(found, best_ref.shape[1:])
    for plane in range(best_ref.shape[0]):
        best_ref[plane] = best


def merge_kernel(parts_ref, out_ref):
    shape = parts_ref.shape[1:]
    real = lax.broadcasted_iota(jnp.int32, shape, 1) < 2 * TOP
    parts = [jnp.where(real, parts_ref[i], -jnp.inf) for i in range(parts_ref.shape[0])]
    out_ref[...] = lanes_of(best_of(sorted_levels(parts)), out_ref.shape)


def per_device(
    expert_hidden,
    expert_gain,
    expert_head,
    amateur_hidden,
    amateur_gain,
    amateur_head,
    live_mask,
    token_ids,
    plaus_level,
):
    own, depth_e = expert_hidden.shape
    depth_a = amateur_hidden.shape[1]
    width = expert_head.shape[0]
    rows, planes = lax.axis_size("rows"), lax.axis_size("vocab")
    beams = own * rows
    quarter = (depth_e + depth_a) // 4
    row, plane = lax.axis_index("rows"), lax.axis_index("vocab")
    position = jnp.stack([row % NC, (row * planes + plane) * width]).astype(jnp.int32)
    ids = token_ids.reshape(rows, own, 1)
    gap = lax.dynamic_slice_in_dim(plaus_level, row * own, own, 0).reshape(own, 1)

    norm_inputs = (
        expert_hidden, expert_gain.reshape(-1, 128), amateur_hidden, amateur_gain.reshape(-1, 128)
    )
    blocks = pl.pallas_call(
        norm_kernel,
        out_shape=jax.ShapeDtypeStruct((rows, 2 * own, quarter), jnp.bfloat16),
        in_specs=[HBM] * 4,
        out_specs=HBM,
        scratch_shapes=[pltpu.VMEM(x.shape, x.dtype) for x in norm_inputs] + [
            pltpu.VMEM((NC, 2 * own, quarter), jnp.bfloat16),
            pltpu.SemaphoreType.DMA((4,)),
            pltpu.SemaphoreType.DMA((rows,)),
        ],
        compiler_params=WIDE_PARAMS,
        name="norms",
    )(*norm_inputs)
    half = lax.all_to_all(blocks, "rows", 0, 0, tiled=True).reshape(2 * beams, quarter)
    other_half = lax.ppermute(half, "rows", [(r, r ^ 1) for r in range(rows)])
    cost = pl.CostEstimate(
        flops=4 * beams * width * 2 * quarter, bytes_accessed=4 * beams * quarter, transcendentals=0
    )
    buffers = [pltpu.VMEM((2, beams, width), jnp.float32)]
    first = pl.pallas_call(
        first_kernel,
        out_shape=jax.ShapeDtypeStruct((2, rows, own, width), jnp.float32),
        in_specs=[SMEM] + [VMEM] * 3,
        out_specs=VMEM,
        scratch_shapes=buffers,
        compiler_params=PARAMS,
        cost_estimate=cost,
        name="first_half",
    )(position, half, expert_head, amateur_head)
    table = pl.pallas_call(
        second_kernel,
        out_shape=jax.ShapeDtypeStruct((rows, 2 * own, 256), jnp.float32),
        in_specs=[SMEM] + [VMEM] * 6,
        out_specs=VMEM,
        scratch_shapes=buffers,
        compiler_params=PARAMS,
        cost_estimate=cost,
        name="second_half",
    )(position, other_half, expert_head, amateur_head, first, live_mask.reshape(1, -1), ids)
    table = lax.all_to_all(table, "rows", 0, 0, tiled=True)

    small = jax.ShapeDtypeStruct((planes, own, 128), jnp.float32)
    best_shape = jax.ShapeDtypeStruct((own, TOP), jnp.float32)
    stats = pl.pallas_call(
        functools.partial(stats_kernel, width),
        out_shape=small,
        in_specs=[VMEM] * 2,
        out_specs=VMEM,
        compiler_params=PARAMS,
        name="stats",
    )(table, gap)
    stats = lax.all_to_all(stats, "vocab", 0, 0, tiled=True)
    top, peaks, chosen, lacking = pl.pallas_call(
        finish_kernel,
        out_shape=(
            best_shape,
            jax.ShapeDtypeStruct((2, own), jnp.float32),
            jax.ShapeDtypeStruct((1, own), jnp.float32),
            jax.ShapeDtypeStruct((1,), jnp.int32),
        ),
        in_specs=[VMEM] * 2,
        out_specs=(VMEM, VMEM, VMEM, SMEM),
        compiler_params=PARAMS,
        name="finish",
    )(stats, gap)

    def with_every_entry(table, stats, gap, _):
        best = pl.pallas_call(
            functools.partial(score_kernel, width),
            out_shape=small,
            in_specs=[VMEM] * 3,
            out_specs=VMEM,
            compiler_params=PARAMS,
            name="scores",
        )(table, stats, gap)
        best = lax.all_to_all(best, "vocab", 0, 0, tiled=True)
        return pl.pallas_call(
            merge_kernel,
            out_shape=best_shape,
            in_specs=[VMEM],
            out_specs=VMEM,
            compiler_params=PARAMS,
            name="merge",
        )(best)

    top = lax.cond(lacking[0] > 0, with_every_entry, lambda *args: args[-1], table, stats, gap, top)
    return top, peaks.T, chosen.reshape(own)


def solution(mesh):
    in_specs = (
        P("rows", None),
        P(),
        P(("rows", "vocab"), None),
        P("rows", None),
        P(),
        P(("rows", "vocab"), None),
        P(("rows", "vocab")),
        P(),
        P(),
    )
    out_specs = (P("rows", None), P("rows", None), P("rows"))
    return jax.shard_map(
        per_device, mesh=mesh, in_specs=in_specs, out_specs=out_specs, check_vma=False
    )
```

```python
import functools

import jax
import jax.numpy as jnp
from jax import lax
from jax.experimental import pallas as pl
from jax.experimental.pallas import tpu as pltpu
from jax.sharding import PartitionSpec as P

TOP = 4
NEAR = 20
FIRST = 16
NC = 2

masked_floor = -1e30
dead_below = -5e29
penalty_slope = 2.0
norm_epsilon = 1e-06

VMEM = pl.BlockSpec(memory_space=pltpu.VMEM)
HBM = pl.BlockSpec(memory_space=pltpu.HBM)
SMEM = pl.BlockSpec(memory_space=pltpu.SMEM)
WIDE_PARAMS = pltpu.CompilerParams(vmem_limit_bytes=60 * 1024 * 1024)
PARAMS = pltpu.CompilerParams(vmem_limit_bytes=16 * 1024 * 1024)


def norm_kernel(*refs):
    inputs, out_ref, held, block_ref, sems, out_sems = refs[:4], refs[4], refs[5:9], *refs[9:]
    copies = [pltpu.make_async_copy(inputs[i], held[i], sems.at[i]) for i in range(4)]
    for copy in copies:
        copy.start()
    quarters = []
    for model in range(2):
        copies[2 * model].wait()
        copies[2 * model + 1].wait()
        values = held[2 * model][...].astype(jnp.float32)
        gain = held[2 * model + 1][...].astype(jnp.float32)
        mean = jnp.mean(values * values, axis=-1, keepdims=True)
        values = values * lax.rsqrt(mean + norm_epsilon)
        chunks = [
            values[:, 128 * i:128 * i + 128] * gain[i:i + 1, :] for i in range(values.shape[1] // 128)
        ]
        each = len(chunks) // 4
        quarters.append([chunks[each * q:each * q + each] for q in range(4)])
    sent = []
    for core in range(NC):
        rows = [quarters[0][2 * core + p] + quarters[1][2 * core + p] for p in range(2)]
        for i, pair in enumerate(zip(*rows)):
            block_ref[core, :, 128 * i:128 * i + 128] = jnp.concatenate(pair).astype(jnp.bfloat16)
        for dest in range(core, out_ref.shape[0], NC):
            sent.append(pltpu.make_async_copy(block_ref.at[core], out_ref.at[dest], out_sems.at[dest]))
            sent[-1].start()
    for copy in sent:
        copy.wait()


def quarters_apart(part):
    groups = part.reshape(part.shape[0] // 32, 2, 16, part.shape[1])
    even, odd = groups[:, 0], groups[:, 1]
    first = lax.broadcasted_iota(jnp.int32, even.shape, 1) % 8 < 4
    down = pltpu.roll(odd, 4, 1)
    up = pltpu.roll(even, 12, 1)
    apart = jnp.where(first, even, down), jnp.where(first, up, odd)
    return [x.reshape(part.shape[0] // 2, part.shape[1]) for x in apart]


def half_sums(core, part_ref, head_refs, acc_ref):
    low = 0
    for model, head in enumerate(head_refs):
        size = head.shape[1] // 4
        total = None
        for p, rows in enumerate(quarters_apart(part_ref[:, low:low + size])):
            columns = pl.ds(pl.multiple_of((2 * core + p) * size, 128), size)
            product = lax.dot_general(
                rows, head[:, columns], (((1,), (1,)), ((), ())), preferred_element_type=jnp.float32
            )
            total = product if total is None else total + product
        acc_ref[model] = total
        low += size


def first_kernel(pos_ref, part_ref, he_ref, ha_ref, out_ref):
    half_sums(pos_ref[0], part_ref, (he_ref, ha_ref), out_ref)


def second_kernel(
    pos_ref, part_ref, he_ref, ha_ref, first_ref, live_ref, ids_ref, out_ref, acc_ref
):
    beams, width = ids_ref.shape[0], he_ref.shape[0]
    half_sums(1 - pos_ref[0], part_ref, (he_ref, ha_ref), acc_ref)
    hits = ids_ref[...] == pos_ref[1] + lax.broadcasted_iota(jnp.int32, (1, width), 1)
    live = live_ref[...] == 1
    half = width // 2
    tiles = (beams // 8, 8, 128)
    upper = lax.broadcasted_iota(jnp.int32, tiles, 1) < 4
    for model in range(2):
        logits = first_ref[model] + acc_ref[model]
        pick = jnp.sum(jnp.where(hits, logits, 0.0), axis=1, keepdims=True)
        pick = jnp.broadcast_to(pick, (beams, 128 - half))
        held = jnp.where(live, logits, masked_floor)
        left = jnp.concatenate([held[:, :half], pick], axis=1).reshape(tiles)
        right = jnp.concatenate([held[:, half:], pick], axis=1).reshape(tiles)
        low_owner = jnp.where(upper, left, pltpu.roll(right, 4, 1))
        high_owner = jnp.where(upper, pltpu.roll(left, 4, 1), right)
        lanes = slice(128 * model, 128 * model + 128)
        for tile in range(tiles[0]):
            owner = 4 * (tile // 2) + tile % 2
            out_ref[owner, :, lanes] = low_owner[tile]
            out_ref[owner + 2, :, lanes] = high_owner[tile]


def lanes_of(columns, shape):
    lane = lax.broadcasted_iota(jnp.int32, shape, len(shape) - 1)
    result = jnp.zeros(shape, jnp.float32)
    for i, column in enumerate(columns):
        result = jnp.where(lane == i, column, result)
    return result


def lane_at(values, i):
    lane = lax.broadcasted_iota(jnp.int32, values.shape, values.ndim - 1)
    return jnp.sum(jnp.where(lane == i, values, 0.0), axis=-1, keepdims=True)


def total_rows(values):
    return jnp.sum(values, axis=1, keepdims=True)


def insert(levels, entry):
    for i, level in enumerate(levels):
        above = entry[0] > level[0]
        levels[i] = tuple(jnp.where(above, new, old) for new, old in zip(entry, level))
        entry = tuple(jnp.where(above, old, new) for new, old in zip(entry, level))


def remove_top(levels, top):
    hit = levels[0][0] == top
    payload = [total_rows(jnp.where(hit, field, 0.0)) for field in levels[0][1:]]
    count = total_rows(jnp.where(hit, 1.0, 0.0))
    last = tuple(jnp.full_like(f, masked_floor) for f in levels[0])
    lower = levels[1:] + [last]
    return payload, count, [
        tuple(jnp.where(hit, new, old) for new, old in zip(low, level))
        for low, level in zip(lower, levels)
    ]


def stats_kernel(width, table_ref, gap_ref, out_ref):
    sources, own = table_ref.shape[0], table_ref.shape[1] // 2
    shape = (2 * own, 128)
    real = lax.broadcasted_iota(jnp.int32, shape, 1) < width // 2
    columns = []
    for model in range(2):
        parts = [table_ref[i, :, 128 * model:128 * model + 128] for i in range(sources)]
        peak = functools.reduce(jnp.maximum, parts)
        peak = jnp.max(jnp.where(real, peak, masked_floor), axis=1, keepdims=True)
        peak = jnp.maximum(peak[:own], peak[own:])
        both = jnp.concatenate([peak, peak])
        total = functools.reduce(jnp.add, [jnp.exp(part - both) for part in parts])
        total = total_rows(jnp.where(real, total, 0.0))
        pick = lane_at(functools.reduce(jnp.add, parts), width // 2)
        columns.append((peak, total[:own] + total[own:], pick[:own]))
    (pe, te, ce), (pa, ta, ca) = columns
    least = pe - gap_ref[...].astype(jnp.float32) * 0.1
    least = jnp.concatenate([least, least])
    floor = jnp.full(shape, masked_floor, jnp.float32)
    near, rest = [(floor,) * 2] * TOP, [(floor,) * 3] * TOP
    count = jnp.zeros(shape, jnp.float32)
    for i in range(sources):
        e, a = table_ref[i, :, 0:128], table_ref[i, :, 128:256]
        live = real & (e > dead_below)
        is_near = live & (e >= least)
        count += jnp.where(is_near, 1.0, 0.0)
        insert(near, (jnp.where(is_near, e, masked_floor), a))
        insert(rest, (jnp.where(live & (e < least), 3.0 * e - a, masked_floor), e, a))
    missing = total_rows(count)
    picked = []
    for _ in range(NEAR):
        top = jnp.max(near[0][0], axis=1, keepdims=True)
        (a,), hits, near = remove_top(near, top)
        found = top > dead_below
        picked.append((jnp.where(found, top, masked_floor), a))
        missing -= jnp.where(found & (hits == 1.0), 1.0, 0.0)
    for _ in range(TOP):
        top = jnp.max(rest[0][0], axis=1, keepdims=True)
        (e, a), hits, rest = remove_top(rest, top)
        found = top > dead_below
        picked.append((jnp.where(found, e, masked_floor), a))
        missing += jnp.where(found & (hits > 1.0), 1.0, 0.0)
    zeros = [jnp.zeros_like(missing)]
    lanes = zeros * FIRST + [e for e, _ in picked]
    lanes += zeros * (64 + FIRST - len(lanes)) + [a for _, a in picked]
    lanes = lanes_of(lanes, shape)
    stats = lanes_of([pe, pa, te, ta, ce, ca, missing[:own] + missing[own:]], (own, 128))
    stats += lanes[:own] + pltpu.roll(lanes, len(picked), 1)[own:]
    for plane in range(out_ref.shape[0]):
        out_ref[plane] = stats


def best_of(levels):
    tops, counts, seen = [], [], 0.0
    for _ in range(TOP):
        top = jnp.max(levels[0], axis=1, keepdims=True)
        hit = levels[0] == top
        seen = seen + total_rows(jnp.where(hit, 1.0, 0.0))
        tops.append(top)
        counts.append(seen)
        lower = levels[1:] + [jnp.full_like(levels[0], -jnp.inf)]
        levels = [jnp.where(hit, low, level) for level, low in zip(levels, lower)]
    found = []
    for i in range(TOP):
        value = tops[-1]
        for top, seen in reversed(list(zip(tops, counts))):
            value = jnp.where(seen > i, top, value)
        found.append(value)
    return found


def sorted_levels(parts):
    levels = [jnp.full_like(parts[0], -jnp.inf)] * TOP
    for part in parts:
        for i in range(TOP):
            levels[i], part = jnp.maximum(levels[i], part), jnp.minimum(levels[i], part)
    return levels


def row_from(column):
    shape = (column.shape[0], column.shape[0])
    here = lax.broadcasted_iota(jnp.int32, shape, 0) == lax.broadcasted_iota(jnp.int32, shape, 1)
    return jnp.sum(jnp.where(here, column, 0.0), axis=0, keepdims=True)


def totals_of(stats_ref, gap_ref, copies=1):
    stats = stats_ref[...]
    peak_e, peak_a, sum_e, sum_a = [lane_at(stats, i) for i in range(4)]

    def total_of(peaks, sums):
        peak = jnp.max(peaks, axis=0)
        return peak, peak + jnp.log(jnp.sum(sums * jnp.exp(peaks - peak[None]), axis=0))

    peak_e, log_total_e = total_of(peak_e, sum_e)
    peak_a, log_total_a = total_of(peak_a, sum_a)
    cut = peak_e - log_total_e - gap_ref[...].astype(jnp.float32) * 0.1
    shift_e, shift_a, cuts = [
        jnp.concatenate([x] * copies) if copies > 1 else x for x in (log_total_e, log_total_a, cut)
    ]

    def score(logits_e, logits_a):
        logprob_e = logits_e - shift_e
        logprob_a = logits_a - shift_a
        return logprob_e - logprob_a - penalty_slope * jnp.maximum(cuts - logprob_e, 0.0)

    return [peak_e - log_total_e, peak_a - log_total_a], score


def finish_kernel(stats_ref, gap_ref, top_ref, peaks_ref, chosen_ref, lacking_ref):
    peaks, score = totals_of(stats_ref, gap_ref)
    stats = stats_ref[...]
    for i, peak in enumerate(peaks):
        peaks_ref[i:i + 1, :] = row_from(peak)
    picks = [jnp.sum(lane_at(stats, i), axis=0) for i in (4, 5)]
    chosen_ref[...] = row_from(score(*picks))
    lane = lax.broadcasted_iota(jnp.int32, stats.shape[1:], 1)
    is_candidate = (lane >= FIRST) & (lane < FIRST + 2 * (NEAR + TOP))
    parts, lacking = [], jnp.zeros(stats.shape[1:], jnp.float32)
    for plane in range(stats.shape[0]):
        e, a = stats[plane], pltpu.roll(stats[plane], 64, 1)
        value = jnp.where(e > dead_below, score(e, a), masked_floor)
        parts.append(jnp.where(is_candidate, value, -jnp.inf))
        lacking = jnp.maximum(lacking, jnp.where(lane == 6, e, 0.0))
    top_ref[...] = lanes_of(best_of(sorted_levels(parts)), top_ref.shape)
    lacking_ref[0] = jnp.where(jnp.max(lacking) > 0.0, 1, 0).astype(jnp.int32)


def score_kernel(width, table_ref, stats_ref, gap_ref, best_ref):
    _, score = totals_of(stats_ref, gap_ref, 2)
    own = table_ref.shape[1] // 2
    real = lax.broadcasted_iota(jnp.int32, (2 * own, 128), 1) < width // 2
    parts = []
    for source in range(table_ref.shape[0]):
        e, a = table_ref[source, :, 0:128], table_ref[source, :, 128:256]
        parts.append(jnp.where(real & (e > dead_below), score(e, a), masked_floor))
    found = best_of(sorted_levels(parts))
    found = [value[:own] for value in found] + [value[own:] for value in found]
    best = lanes_of(found, best_ref.shape[1:])
    for plane in range(best_ref.shape[0]):
        best_ref[plane] = best


def merge_kernel(parts_ref, out_ref):
    shape = parts_ref.shape[1:]
    real = lax.broadcasted_iota(jnp.int32, shape, 1) < 2 * TOP
    parts = [jnp.where(real, parts_ref[i], -jnp.inf) for i in range(parts_ref.shape[0])]
    out_ref[...] = lanes_of(best_of(sorted_levels(parts)), out_ref.shape)


def per_device(
    expert_hidden,
    expert_gain,
    expert_head,
    amateur_hidden,
    amateur_gain,
    amateur_head,
    live_mask,
    token_ids,
    plaus_level,
):
    own, depth_e = expert_hidden.shape
    depth_a = amateur_hidden.shape[1]
    width = expert_head.shape[0]
    rows, planes = lax.axis_size("rows"), lax.axis_size("vocab")
    beams = own * rows
    quarter = (depth_e + depth_a) // 4
    row, plane = lax.axis_index("rows"), lax.axis_index("vocab")
    position = jnp.stack([row % NC, (row * planes + plane) * width]).astype(jnp.int32)
    ids = token_ids.reshape(rows // 4, 2, 2, own).swapaxes(1, 2).reshape(beams, 1)
    gap = lax.dynamic_slice_in_dim(plaus_level, row * own, own, 0).reshape(own, 1)

    norm_inputs = (
        expert_hidden, expert_gain.reshape(-1, 128), amateur_hidden, amateur_gain.reshape(-1, 128)
    )
    blocks = pl.pallas_call(
        norm_kernel,
        out_shape=jax.ShapeDtypeStruct((rows, 2 * own, quarter), jnp.bfloat16),
        in_specs=[HBM] * 4,
        out_specs=HBM,
        scratch_shapes=[pltpu.VMEM(x.shape, x.dtype) for x in norm_inputs] + [
            pltpu.VMEM((NC, 2 * own, quarter), jnp.bfloat16),
            pltpu.SemaphoreType.DMA((4,)),
            pltpu.SemaphoreType.DMA((rows,)),
        ],
        compiler_params=WIDE_PARAMS,
        name="norms",
    )(*norm_inputs)
    half = lax.all_to_all(blocks, "rows", 0, 0, tiled=True).reshape(2 * beams, quarter)
    other_half = lax.ppermute(half, "rows", [(r, r ^ 1) for r in range(rows)])
    cost = pl.CostEstimate(
        flops=4 * beams * width * 2 * quarter, bytes_accessed=4 * beams * quarter, transcendentals=0
    )
    first = pl.pallas_call(
        first_kernel,
        out_shape=jax.ShapeDtypeStruct((2, beams, width), jnp.float32),
        in_specs=[SMEM] + [VMEM] * 3,
        out_specs=VMEM,
        compiler_params=PARAMS,
        cost_estimate=cost,
        name="first_half",
    )(position, half, expert_head, amateur_head)
    table = pl.pallas_call(
        second_kernel,
        out_shape=jax.ShapeDtypeStruct((rows, 2 * own, 256), jnp.float32),
        in_specs=[SMEM] + [VMEM] * 6,
        out_specs=VMEM,
        scratch_shapes=[pltpu.VMEM((2, beams, width), jnp.float32)],
        compiler_params=PARAMS,
        cost_estimate=cost,
        name="second_half",
    )(position, other_half, expert_head, amateur_head, first, live_mask.reshape(1, -1), ids)
    table = lax.all_to_all(table, "rows", 0, 0, tiled=True)

    small = jax.ShapeDtypeStruct((planes, own, 128), jnp.float32)
    best_shape = jax.ShapeDtypeStruct((own, TOP), jnp.float32)
    stats = pl.pallas_call(
        functools.partial(stats_kernel, width),
        out_shape=small,
        in_specs=[VMEM] * 2,
        out_specs=VMEM,
        compiler_params=PARAMS,
        name="stats",
    )(table, gap)
    stats = lax.all_to_all(stats, "vocab", 0, 0, tiled=True)
    top, peaks, chosen, lacking = pl.pallas_call(
        finish_kernel,
        out_shape=(
            best_shape,
            jax.ShapeDtypeStruct((2, own), jnp.float32),
            jax.ShapeDtypeStruct((1, own), jnp.float32),
            jax.ShapeDtypeStruct((1,), jnp.int32),
        ),
        in_specs=[VMEM] * 2,
        out_specs=(VMEM, VMEM, VMEM, SMEM),
        compiler_params=PARAMS,
        name="finish",
    )(stats, gap)

    def with_every_entry(table, stats, gap, _):
        best = pl.pallas_call(
            functools.partial(score_kernel, width),
            out_shape=small,
            in_specs=[VMEM] * 3,
            out_specs=VMEM,
            compiler_params=PARAMS,
            name="scores",
        )(table, stats, gap)
        best = lax.all_to_all(best, "vocab", 0, 0, tiled=True)
        return pl.pallas_call(
            merge_kernel,
            out_shape=best_shape,
            in_specs=[VMEM],
            out_specs=VMEM,
            compiler_params=PARAMS,
            name="merge",
        )(best)

    top = lax.cond(lacking[0] > 0, with_every_entry, lambda *args: args[-1], table, stats, gap, top)
    return top, peaks.T, chosen.reshape(own)


def solution(mesh):
    in_specs = (
        P("rows", None),
        P(),
        P(("rows", "vocab"), None),
        P("rows", None),
        P(),
        P(("rows", "vocab"), None),
        P(("rows", "vocab")),
        P(),
        P(),
    )
    out_specs = (P("rows", None), P("rows", None), P("rows"))
    return jax.shard_map(
        per_device, mesh=mesh, in_specs=in_specs, out_specs=out_specs, check_vma=False
    )
```

```python
import functools

import jax
import jax.numpy as jnp
from jax import lax
from jax.experimental import pallas as pl
from jax.experimental.pallas import tpu as pltpu
from jax.sharding import PartitionSpec as P

TOP = 4
NEAR = 20
FIRST = 16
NC = 2

masked_floor = -1e30
dead_below = -5e29
penalty_slope = 2.0
norm_epsilon = 1e-06

VMEM = pl.BlockSpec(memory_space=pltpu.VMEM)
HBM = pl.BlockSpec(memory_space=pltpu.HBM)
SMEM = pl.BlockSpec(memory_space=pltpu.SMEM)
WIDE_PARAMS = pltpu.CompilerParams(vmem_limit_bytes=60 * 1024 * 1024)
PARAMS = pltpu.CompilerParams(vmem_limit_bytes=16 * 1024 * 1024)


def norm_kernel(*refs):
    inputs, out_ref, held, block_ref, sems, out_sems = refs[:4], refs[4], refs[5:9], *refs[9:]
    copies = [pltpu.make_async_copy(inputs[i], held[i], sems.at[i]) for i in range(4)]
    for copy in copies:
        copy.start()
    quarters = []
    for model in range(2):
        copies[2 * model].wait()
        copies[2 * model + 1].wait()
        values = held[2 * model][...].astype(jnp.float32)
        gain = held[2 * model + 1][...].astype(jnp.float32)
        mean = jnp.mean(values * values, axis=-1, keepdims=True)
        values = values * lax.rsqrt(mean + norm_epsilon)
        chunks = [
            values[:, 128 * i:128 * i + 128] * gain[i:i + 1, :] for i in range(values.shape[1] // 128)
        ]
        each = len(chunks) // 4
        quarters.append([chunks[each * q:each * q + each] for q in range(4)])
    sent = []
    for core in range(NC):
        rows = [quarters[0][2 * core + p] + quarters[1][2 * core + p] for p in range(2)]
        for i, pair in enumerate(zip(*rows)):
            block_ref[core, :, 128 * i:128 * i + 128] = jnp.concatenate(pair).astype(jnp.bfloat16)
        for dest in range(core, out_ref.shape[0], NC):
            sent.append(pltpu.make_async_copy(block_ref.at[core], out_ref.at[dest], out_sems.at[dest]))
            sent[-1].start()
    for copy in sent:
        copy.wait()


def quarters_apart(part):
    groups = part.reshape(part.shape[0] // 32, 2, 16, part.shape[1])
    even, odd = groups[:, 0], groups[:, 1]
    first = lax.broadcasted_iota(jnp.int32, even.shape, 1) % 8 < 4
    down = pltpu.roll(odd, 4, 1)
    up = pltpu.roll(even, 12, 1)
    apart = jnp.where(first, even, down), jnp.where(first, up, odd)
    return [x.reshape(part.shape[0] // 2, part.shape[1]) for x in apart]


def half_sums(core, part_ref, head_refs, acc_ref):
    low = 0
    for model, head in enumerate(head_refs):
        size = head.shape[1] // 4
        total = None
        for p, rows in enumerate(quarters_apart(part_ref[:, low:low + size])):
            columns = pl.ds(pl.multiple_of((2 * core + p) * size, 128), size)
            product = lax.dot_general(
                rows, head[:, columns], (((1,), (1,)), ((), ())), preferred_element_type=jnp.float32
            )
            total = product if total is None else total + product
        acc_ref[model] = total
        low += size


def first_kernel(pos_ref, part_ref, he_ref, ha_ref, out_ref):
    half_sums(pos_ref[0], part_ref, (he_ref, ha_ref), out_ref)


def second_kernel(
    pos_ref, part_ref, he_ref, ha_ref, first_ref, live_ref, ids_ref, out_ref, acc_ref
):
    beams, width = ids_ref.shape[0], he_ref.shape[0]
    half_sums(1 - pos_ref[0], part_ref, (he_ref, ha_ref), acc_ref)
    hits = ids_ref[...] == pos_ref[1] + lax.broadcasted_iota(jnp.int32, (1, width), 1)
    live = live_ref[...] == 1
    half = width // 2
    tiles = (beams // 8, 8, 128)
    upper = lax.broadcasted_iota(jnp.int32, tiles, 1) < 4
    for model in range(2):
        logits = first_ref[model] + acc_ref[model]
        pick = jnp.sum(jnp.where(hits, logits, 0.0), axis=1, keepdims=True)
        pick = jnp.broadcast_to(pick, (beams, 128 - half))
        held = jnp.where(live, logits, masked_floor)
        left = jnp.concatenate([held[:, :half], pick], axis=1).reshape(tiles)
        right = jnp.concatenate([held[:, half:], pick], axis=1).reshape(tiles)
        low_owner = jnp.where(upper, left, pltpu.roll(right, 4, 1))
        high_owner = jnp.where(upper, pltpu.roll(left, 4, 1), right)
        lanes = slice(128 * model, 128 * model + 128)
        for tile in range(tiles[0]):
            owner = 4 * (tile // 2) + tile % 2
            out_ref[owner, :, lanes] = low_owner[tile]
            out_ref[owner + 2, :, lanes] = high_owner[tile]


def lanes_of(columns, shape):
    lane = lax.broadcasted_iota(jnp.int32, shape, len(shape) - 1)
    result = jnp.zeros(shape, jnp.float32)
    for i, column in enumerate(columns):
        result = jnp.where(lane == i, column, result)
    return result


def lane_at(values, i):
    lane = lax.broadcasted_iota(jnp.int32, values.shape, values.ndim - 1)
    return jnp.sum(jnp.where(lane == i, values, 0.0), axis=-1, keepdims=True)


def total_rows(values):
    return jnp.sum(values, axis=1, keepdims=True)


def insert(levels, entry):
    for i, level in enumerate(levels):
        above = entry[0] > level[0]
        levels[i] = tuple(jnp.where(above, new, old) for new, old in zip(entry, level))
        entry = tuple(jnp.where(above, old, new) for new, old in zip(entry, level))


def remove_top(levels, top):
    hit = levels[0][0] == top
    payload = [total_rows(jnp.where(hit, field, 0.0)) for field in levels[0][1:]]
    count = total_rows(jnp.where(hit, 1.0, 0.0))
    last = tuple(jnp.full_like(f, masked_floor) for f in levels[0])
    lower = levels[1:] + [last]
    return payload, count, [
        tuple(jnp.where(hit, new, old) for new, old in zip(low, level))
        for low, level in zip(lower, levels)
    ]


def gap_column(pos_ref, level_ref, shape):
    row = lax.broadcasted_iota(jnp.int32, shape, 0)
    levels = jnp.zeros(shape, jnp.int32)
    for i in range(shape[0]):
        levels = jnp.where(row == i, level_ref[pos_ref[2] + i], levels)
    return levels.astype(jnp.float32) * 0.1


def stats_kernel(width, pos_ref, level_ref, table_ref, out_ref):
    sources, own = table_ref.shape[0], table_ref.shape[1] // 2
    shape = (2 * own, 128)
    real = lax.broadcasted_iota(jnp.int32, shape, 1) < width // 2
    columns = []
    for model in range(2):
        parts = [table_ref[i, :, 128 * model:128 * model + 128] for i in range(sources)]
        peak = functools.reduce(jnp.maximum, parts)
        peak = jnp.max(jnp.where(real, peak, masked_floor), axis=1, keepdims=True)
        peak = jnp.maximum(peak[:own], peak[own:])
        both = jnp.concatenate([peak, peak])
        total = functools.reduce(jnp.add, [jnp.exp(part - both) for part in parts])
        total = total_rows(jnp.where(real, total, 0.0))
        pick = lane_at(functools.reduce(jnp.add, parts), width // 2)
        columns.append((peak, total[:own] + total[own:], pick[:own]))
    (pe, te, ce), (pa, ta, ca) = columns
    least = pe - gap_column(pos_ref, level_ref, pe.shape)
    least = jnp.concatenate([least, least])
    floor = jnp.full(shape, masked_floor, jnp.float32)
    near, rest = [(floor,) * 2] * TOP, [(floor,) * 3] * TOP
    count = jnp.zeros(shape, jnp.float32)
    for i in range(sources):
        e, a = table_ref[i, :, 0:128], table_ref[i, :, 128:256]
        live = real & (e > dead_below)
        is_near = live & (e >= least)
        count += jnp.where(is_near, 1.0, 0.0)
        insert(near, (jnp.where(is_near, e, masked_floor), a))
        insert(rest, (jnp.where(live & (e < least), 3.0 * e - a, masked_floor), e, a))
    missing = total_rows(count)
    picked = []
    for _ in range(NEAR):
        top = jnp.max(near[0][0], axis=1, keepdims=True)
        (a,), hits, near = remove_top(near, top)
        found = top > dead_below
        picked.append((jnp.where(found, top, masked_floor), a))
        missing -= jnp.where(found & (hits == 1.0), 1.0, 0.0)
    for _ in range(TOP):
        top = jnp.max(rest[0][0], axis=1, keepdims=True)
        (e, a), hits, rest = remove_top(rest, top)
        found = top > dead_below
        picked.append((jnp.where(found, e, masked_floor), a))
        missing += jnp.where(found & (hits > 1.0), 1.0, 0.0)
    zeros = [jnp.zeros_like(missing)]
    lanes = zeros * FIRST + [e for e, _ in picked]
    lanes += zeros * (64 + FIRST - len(lanes)) + [a for _, a in picked]
    lanes = lanes_of(lanes, shape)
    stats = lanes_of([pe, pa, te, ta, ce, ca, missing[:own] + missing[own:]], (own, 128))
    stats += lanes[:own] + pltpu.roll(lanes, len(picked), 1)[own:]
    for plane in range(out_ref.shape[0]):
        out_ref[plane] = stats


def best_of(levels):
    tops, counts, seen = [], [], 0.0
    for _ in range(TOP):
        top = jnp.max(levels[0], axis=1, keepdims=True)
        hit = levels[0] == top
        seen = seen + total_rows(jnp.where(hit, 1.0, 0.0))
        tops.append(top)
        counts.append(seen)
        lower = levels[1:] + [jnp.full_like(levels[0], -jnp.inf)]
        levels = [jnp.where(hit, low, level) for level, low in zip(levels, lower)]
    found = []
    for i in range(TOP):
        value = tops[-1]
        for top, seen in reversed(list(zip(tops, counts))):
            value = jnp.where(seen > i, top, value)
        found.append(value)
    return found


def sorted_levels(parts):
    levels = [jnp.full_like(parts[0], -jnp.inf)] * TOP
    for part in parts:
        for i in range(TOP):
            levels[i], part = jnp.maximum(levels[i], part), jnp.minimum(levels[i], part)
    return levels


def row_from(column):
    shape = (column.shape[0], column.shape[0])
    here = lax.broadcasted_iota(jnp.int32, shape, 0) == lax.broadcasted_iota(jnp.int32, shape, 1)
    return jnp.sum(jnp.where(here, column, 0.0), axis=0, keepdims=True)


def totals_of(stats_ref, pos_ref, level_ref, copies=1):
    stats = stats_ref[...]
    peak_e, peak_a, sum_e, sum_a = [lane_at(stats, i) for i in range(4)]

    def total_of(peaks, sums):
        peak = jnp.max(peaks, axis=0)
        return peak, peak + jnp.log(jnp.sum(sums * jnp.exp(peaks - peak[None]), axis=0))

    peak_e, log_total_e = total_of(peak_e, sum_e)
    peak_a, log_total_a = total_of(peak_a, sum_a)
    cut = peak_e - log_total_e - gap_column(pos_ref, level_ref, peak_e.shape)
    shift_e, shift_a, cuts = [
        jnp.concatenate([x] * copies) if copies > 1 else x for x in (log_total_e, log_total_a, cut)
    ]

    def score(logits_e, logits_a):
        logprob_e = logits_e - shift_e
        logprob_a = logits_a - shift_a
        return logprob_e - logprob_a - penalty_slope * jnp.maximum(cuts - logprob_e, 0.0)

    return [peak_e - log_total_e, peak_a - log_total_a], score


def finish_kernel(pos_ref, level_ref, stats_ref, top_ref, peaks_ref, chosen_ref, lacking_ref):
    peaks, score = totals_of(stats_ref, pos_ref, level_ref)
    stats = stats_ref[...]
    for i, peak in enumerate(peaks):
        peaks_ref[i:i + 1, :] = row_from(peak)
    picks = [jnp.sum(lane_at(stats, i), axis=0) for i in (4, 5)]
    chosen_ref[...] = row_from(score(*picks))
    lane = lax.broadcasted_iota(jnp.int32, stats.shape[1:], 1)
    is_candidate = (lane >= FIRST) & (lane < FIRST + 2 * (NEAR + TOP))
    parts, lacking = [], jnp.zeros(stats.shape[1:], jnp.float32)
    for plane in range(stats.shape[0]):
        e, a = stats[plane], pltpu.roll(stats[plane], 64, 1)
        value = jnp.where(e > dead_below, score(e, a), masked_floor)
        parts.append(jnp.where(is_candidate, value, -jnp.inf))
        lacking = jnp.maximum(lacking, jnp.where(lane == 6, e, 0.0))
    top_ref[...] = lanes_of(best_of(sorted_levels(parts)), top_ref.shape)
    lacking_ref[0] = jnp.where(jnp.max(lacking) > 0.0, 1, 0).astype(jnp.int32)


def score_kernel(width, pos_ref, level_ref, table_ref, stats_ref, best_ref):
    _, score = totals_of(stats_ref, pos_ref, level_ref, 2)
    own = table_ref.shape[1] // 2
    real = lax.broadcasted_iota(jnp.int32, (2 * own, 128), 1) < width // 2
    parts = []
    for source in range(table_ref.shape[0]):
        e, a = table_ref[source, :, 0:128], table_ref[source, :, 128:256]
        parts.append(jnp.where(real & (e > dead_below), score(e, a), masked_floor))
    found = best_of(sorted_levels(parts))
    found = [value[:own] for value in found] + [value[own:] for value in found]
    best = lanes_of(found, best_ref.shape[1:])
    for plane in range(best_ref.shape[0]):
        best_ref[plane] = best


def merge_kernel(parts_ref, out_ref):
    shape = parts_ref.shape[1:]
    real = lax.broadcasted_iota(jnp.int32, shape, 1) < 2 * TOP
    parts = [jnp.where(real, parts_ref[i], -jnp.inf) for i in range(parts_ref.shape[0])]
    out_ref[...] = lanes_of(best_of(sorted_levels(parts)), out_ref.shape)


def per_device(
    expert_hidden,
    expert_gain,
    expert_head,
    amateur_hidden,
    amateur_gain,
    amateur_head,
    live_mask,
    token_ids,
    plaus_level,
):
    own, depth_e = expert_hidden.shape
    depth_a = amateur_hidden.shape[1]
    width = expert_head.shape[0]
    rows, planes = lax.axis_size("rows"), lax.axis_size("vocab")
    beams = own * rows
    quarter = (depth_e + depth_a) // 4
    row, plane = lax.axis_index("rows"), lax.axis_index("vocab")
    position = jnp.stack([row % NC, (row * planes + plane) * width, row * own]).astype(jnp.int32)
    ids = token_ids.reshape(rows // 4, 2, 2, own).swapaxes(1, 2).reshape(beams, 1)

    norm_inputs = (
        expert_hidden, expert_gain.reshape(-1, 128), amateur_hidden, amateur_gain.reshape(-1, 128)
    )
    blocks = pl.pallas_call(
        norm_kernel,
        out_shape=jax.ShapeDtypeStruct((rows, 2 * own, quarter), jnp.bfloat16),
        in_specs=[HBM] * 4,
        out_specs=HBM,
        scratch_shapes=[pltpu.VMEM(x.shape, x.dtype) for x in norm_inputs] + [
            pltpu.VMEM((NC, 2 * own, quarter), jnp.bfloat16),
            pltpu.SemaphoreType.DMA((4,)),
            pltpu.SemaphoreType.DMA((rows,)),
        ],
        compiler_params=WIDE_PARAMS,
        name="norms",
    )(*norm_inputs)
    half = lax.all_to_all(blocks, "rows", 0, 0, tiled=True).reshape(2 * beams, quarter)
    other_half = lax.ppermute(half, "rows", [(r, r ^ 1) for r in range(rows)])
    cost = pl.CostEstimate(
        flops=4 * beams * width * 2 * quarter, bytes_accessed=4 * beams * quarter, transcendentals=0
    )
    first = pl.pallas_call(
        first_kernel,
        out_shape=jax.ShapeDtypeStruct((2, beams, width), jnp.float32),
        in_specs=[SMEM] + [VMEM] * 3,
        out_specs=VMEM,
        compiler_params=PARAMS,
        cost_estimate=cost,
        name="first_half",
    )(position, half, expert_head, amateur_head)
    table = pl.pallas_call(
        second_kernel,
        out_shape=jax.ShapeDtypeStruct((rows, 2 * own, 256), jnp.float32),
        in_specs=[SMEM] + [VMEM] * 6,
        out_specs=VMEM,
        scratch_shapes=[pltpu.VMEM((2, beams, width), jnp.float32)],
        compiler_params=PARAMS,
        cost_estimate=cost,
        name="second_half",
    )(position, other_half, expert_head, amateur_head, first, live_mask.reshape(1, -1), ids)
    table = lax.all_to_all(table, "rows", 0, 0, tiled=True)

    small = jax.ShapeDtypeStruct((planes, own, 128), jnp.float32)
    best_shape = jax.ShapeDtypeStruct((own, TOP), jnp.float32)
    stats = pl.pallas_call(
        functools.partial(stats_kernel, width),
        out_shape=small,
        in_specs=[SMEM, SMEM, VMEM],
        out_specs=VMEM,
        compiler_params=PARAMS,
        name="stats",
    )(position, plaus_level, table)
    stats = lax.all_to_all(stats, "vocab", 0, 0, tiled=True)
    top, peaks, chosen, lacking = pl.pallas_call(
        finish_kernel,
        out_shape=(
            best_shape,
            jax.ShapeDtypeStruct((2, own), jnp.float32),
            jax.ShapeDtypeStruct((1, own), jnp.float32),
            jax.ShapeDtypeStruct((1,), jnp.int32),
        ),
        in_specs=[SMEM, SMEM, VMEM],
        out_specs=(VMEM, VMEM, VMEM, SMEM),
        compiler_params=PARAMS,
        name="finish",
    )(position, plaus_level, stats)

    def with_every_entry(position, level, table, stats, _):
        best = pl.pallas_call(
            functools.partial(score_kernel, width),
            out_shape=small,
            in_specs=[SMEM, SMEM, VMEM, VMEM],
            out_specs=VMEM,
            compiler_params=PARAMS,
            name="scores",
        )(position, level, table, stats)
        best = lax.all_to_all(best, "vocab", 0, 0, tiled=True)
        return pl.pallas_call(
            merge_kernel,
            out_shape=best_shape,
            in_specs=[VMEM],
            out_specs=VMEM,
            compiler_params=PARAMS,
            name="merge",
        )(best)

    operands = (position, plaus_level, table, stats, top)
    top = lax.cond(lacking[0] > 0, with_every_entry, lambda *args: args[-1], *operands)
    return top, peaks.T, chosen.reshape(own)


def solution(mesh):
    in_specs = (
        P("rows", None),
        P(),
        P(("rows", "vocab"), None),
        P("rows", None),
        P(),
        P(("rows", "vocab"), None),
        P(("rows", "vocab")),
        P(),
        P(),
    )
    out_specs = (P("rows", None), P("rows", None), P("rows"))
    return jax.shard_map(
        per_device, mesh=mesh, in_specs=in_specs, out_specs=out_specs, check_vma=False
    )
```

```python
import functools

import jax
import jax.numpy as jnp
from jax import lax
from jax.experimental import pallas as pl
from jax.experimental.pallas import tpu as pltpu
from jax.sharding import PartitionSpec as P

TOP = 4
NEAR = 20
FIRST = 16
NC = 2

masked_floor = -1e30
dead_below = -5e29
penalty_slope = 2.0
norm_epsilon = 1e-06

VMEM = pl.BlockSpec(memory_space=pltpu.VMEM)
HBM = pl.BlockSpec(memory_space=pltpu.HBM)
SMEM = pl.BlockSpec(memory_space=pltpu.SMEM)
WIDE_PARAMS = pltpu.CompilerParams(vmem_limit_bytes=60 * 1024 * 1024)
PARAMS = pltpu.CompilerParams(vmem_limit_bytes=16 * 1024 * 1024)


def norm_kernel(*refs):
    inputs, out_ref, held, block_ref, sems, out_sems = refs[:4], refs[4], refs[5:9], *refs[9:]
    copies = [pltpu.make_async_copy(inputs[i], held[i], sems.at[i]) for i in range(4)]
    for copy in copies:
        copy.start()
    quarters = []
    for model in range(2):
        copies[2 * model].wait()
        copies[2 * model + 1].wait()
        values = held[2 * model][...].astype(jnp.float32)
        gain = held[2 * model + 1][...].astype(jnp.float32)
        mean = jnp.mean(values * values, axis=-1, keepdims=True)
        values = values * lax.rsqrt(mean + norm_epsilon)
        chunks = [
            values[:, 128 * i:128 * i + 128] * gain[i:i + 1, :] for i in range(values.shape[1] // 128)
        ]
        each = len(chunks) // 4
        quarters.append([chunks[each * q:each * q + each] for q in range(4)])
    sent = []
    for core in range(NC):
        rows = [quarters[0][2 * core + p] + quarters[1][2 * core + p] for p in range(2)]
        for i, pair in enumerate(zip(*rows)):
            block_ref[core, :, 128 * i:128 * i + 128] = jnp.concatenate(pair).astype(jnp.bfloat16)
        for dest in range(core, out_ref.shape[0], NC):
            sent.append(pltpu.make_async_copy(block_ref.at[core], out_ref.at[dest], out_sems.at[dest]))
            sent[-1].start()
    for copy in sent:
        copy.wait()


def quarters_apart(part):
    groups = part.reshape(part.shape[0] // 32, 2, 16, part.shape[1])
    even, odd = groups[:, 0], groups[:, 1]
    first = lax.broadcasted_iota(jnp.int32, even.shape, 1) % 8 < 4
    down = pltpu.roll(odd, 4, 1)
    up = pltpu.roll(even, 12, 1)
    apart = jnp.where(first, even, down), jnp.where(first, up, odd)
    return [x.reshape(part.shape[0] // 2, part.shape[1]) for x in apart]


def half_sums(core, part_ref, head_refs, acc_ref):
    low = 0
    for model, head in enumerate(head_refs):
        size = head.shape[1] // 4
        total = None
        for p, rows in enumerate(quarters_apart(part_ref[:, low:low + size])):
            columns = pl.ds(pl.multiple_of((2 * core + p) * size, 128), size)
            product = lax.dot_general(
                rows, head[:, columns], (((1,), (1,)), ((), ())), preferred_element_type=jnp.float32
            )
            total = product if total is None else total + product
        acc_ref[model] = total
        low += size


def first_kernel(pos_ref, part_ref, he_ref, ha_ref, out_ref):
    half_sums(pos_ref[0], part_ref, (he_ref, ha_ref), out_ref)


def second_kernel(
    pos_ref, part_ref, he_ref, ha_ref, first_ref, live_ref, ids_ref, _, out_ref, acc_ref
):
    beams, width = ids_ref.shape[0], he_ref.shape[0]
    half_sums(1 - pos_ref[0], part_ref, (he_ref, ha_ref), acc_ref)
    hits = ids_ref[...] == pos_ref[1] + lax.broadcasted_iota(jnp.int32, (1, width), 1)
    live = live_ref[...] == 1
    half = width // 2
    tiles = (beams // 8, 8, 128)
    upper = lax.broadcasted_iota(jnp.int32, tiles, 1) < 4
    for model in range(2):
        logits = first_ref[model] + acc_ref[model]
        pick = jnp.sum(jnp.where(hits, logits, 0.0), axis=1, keepdims=True)
        pick = jnp.broadcast_to(pick, (beams, 128 - half))
        held = jnp.where(live, logits, masked_floor)
        left = jnp.concatenate([held[:, :half], pick], axis=1).reshape(tiles)
        right = jnp.concatenate([held[:, half:], pick], axis=1).reshape(tiles)
        low_owner = jnp.where(upper, left, pltpu.roll(right, 4, 1))
        high_owner = jnp.where(upper, pltpu.roll(left, 4, 1), right)
        lanes = slice(128 * model, 128 * model + 128)
        for tile in range(tiles[0]):
            owner = 4 * (tile // 2) + tile % 2
            out_ref[owner, :, lanes] = low_owner[tile]
            out_ref[owner + 2, :, lanes] = high_owner[tile]


def lanes_of(columns, shape):
    lane = lax.broadcasted_iota(jnp.int32, shape, len(shape) - 1)
    result = jnp.zeros(shape, jnp.float32)
    for i, column in enumerate(columns):
        result = jnp.where(lane == i, column, result)
    return result


def lane_at(values, i):
    lane = lax.broadcasted_iota(jnp.int32, values.shape, values.ndim - 1)
    return jnp.sum(jnp.where(lane == i, values, 0.0), axis=-1, keepdims=True)


def total_rows(values):
    return jnp.sum(values, axis=1, keepdims=True)


def insert(levels, entry):
    for i, level in enumerate(levels):
        above = entry[0] > level[0]
        levels[i] = tuple(jnp.where(above, new, old) for new, old in zip(entry, level))
        entry = tuple(jnp.where(above, old, new) for new, old in zip(entry, level))


def remove_top(levels, top):
    hit = levels[0][0] == top
    payload = [total_rows(jnp.where(hit, field, 0.0)) for field in levels[0][1:]]
    count = total_rows(jnp.where(hit, 1.0, 0.0))
    last = tuple(jnp.full_like(f, masked_floor) for f in levels[0])
    lower = levels[1:] + [last]
    return payload, count, [
        tuple(jnp.where(hit, new, old) for new, old in zip(low, level))
        for low, level in zip(lower, levels)
    ]


def stats_kernel(width, table_ref, gap_ref, out_ref):
    sources, own = table_ref.shape[0], table_ref.shape[1] // 2
    shape = (2 * own, 128)
    real = lax.broadcasted_iota(jnp.int32, shape, 1) < width // 2
    columns = []
    for model in range(2):
        parts = [table_ref[i, :, 128 * model:128 * model + 128] for i in range(sources)]
        peak = functools.reduce(jnp.maximum, parts)
        peak = jnp.max(jnp.where(real, peak, masked_floor), axis=1, keepdims=True)
        peak = jnp.maximum(peak[:own], peak[own:])
        both = jnp.concatenate([peak, peak])
        total = functools.reduce(jnp.add, [jnp.exp(part - both) for part in parts])
        total = total_rows(jnp.where(real, total, 0.0))
        pick = lane_at(functools.reduce(jnp.add, parts), width // 2)
        columns.append((peak, total[:own] + total[own:], pick[:own]))
    (pe, te, ce), (pa, ta, ca) = columns
    least = pe - gap_ref[...].astype(jnp.float32) * 0.1
    least = jnp.concatenate([least, least])
    floor = jnp.full(shape, masked_floor, jnp.float32)
    near, rest = [(floor,) * 2] * TOP, [(floor,) * 3] * TOP
    count = jnp.zeros(shape, jnp.float32)
    for i in range(sources):
        e, a = table_ref[i, :, 0:128], table_ref[i, :, 128:256]
        live = real & (e > dead_below)
        is_near = live & (e >= least)
        count += jnp.where(is_near, 1.0, 0.0)
        insert(near, (jnp.where(is_near, e, masked_floor), a))
        insert(rest, (jnp.where(live & (e < least), 3.0 * e - a, masked_floor), e, a))
    missing = total_rows(count)
    picked = []
    for _ in range(NEAR):
        top = jnp.max(near[0][0], axis=1, keepdims=True)
        (a,), hits, near = remove_top(near, top)
        found = top > dead_below
        picked.append((jnp.where(found, top, masked_floor), a))
        missing -= jnp.where(found & (hits == 1.0), 1.0, 0.0)
    for _ in range(TOP):
        top = jnp.max(rest[0][0], axis=1, keepdims=True)
        (e, a), hits, rest = remove_top(rest, top)
        found = top > dead_below
        picked.append((jnp.where(found, e, masked_floor), a))
        missing += jnp.where(found & (hits > 1.0), 1.0, 0.0)
    zeros = [jnp.zeros_like(missing)]
    lanes = zeros * FIRST + [e for e, _ in picked]
    lanes += zeros * (64 + FIRST - len(lanes)) + [a for _, a in picked]
    lanes = lanes_of(lanes, shape)
    stats = lanes_of([pe, pa, te, ta, ce, ca, missing[:own] + missing[own:]], (own, 128))
    stats += lanes[:own] + pltpu.roll(lanes, len(picked), 1)[own:]
    for plane in range(out_ref.shape[0]):
        out_ref[plane] = stats


def best_of(levels):
    tops, counts, seen = [], [], 0.0
    for _ in range(TOP):
        top = jnp.max(levels[0], axis=1, keepdims=True)
        hit = levels[0] == top
        seen = seen + total_rows(jnp.where(hit, 1.0, 0.0))
        tops.append(top)
        counts.append(seen)
        lower = levels[1:] + [jnp.full_like(levels[0], -jnp.inf)]
        levels = [jnp.where(hit, low, level) for level, low in zip(levels, lower)]
    found = []
    for i in range(TOP):
        value = tops[-1]
        for top, seen in reversed(list(zip(tops, counts))):
            value = jnp.where(seen > i, top, value)
        found.append(value)
    return found


def sorted_levels(parts):
    levels = [jnp.full_like(parts[0], -jnp.inf)] * TOP
    for part in parts:
        for i in range(TOP):
            levels[i], part = jnp.maximum(levels[i], part), jnp.minimum(levels[i], part)
    return levels


def row_from(column):
    shape = (column.shape[0], column.shape[0])
    here = lax.broadcasted_iota(jnp.int32, shape, 0) == lax.broadcasted_iota(jnp.int32, shape, 1)
    return jnp.sum(jnp.where(here, column, 0.0), axis=0, keepdims=True)


def totals_of(stats_ref, gap_ref, copies=1):
    stats = stats_ref[...]
    peak_e, peak_a, sum_e, sum_a = [lane_at(stats, i) for i in range(4)]

    def total_of(peaks, sums):
        peak = jnp.max(peaks, axis=0)
        return peak, peak + jnp.log(jnp.sum(sums * jnp.exp(peaks - peak[None]), axis=0))

    peak_e, log_total_e = total_of(peak_e, sum_e)
    peak_a, log_total_a = total_of(peak_a, sum_a)
    cut = peak_e - log_total_e - gap_ref[...].astype(jnp.float32) * 0.1
    shift_e, shift_a, cuts = [
        jnp.concatenate([x] * copies) if copies > 1 else x for x in (log_total_e, log_total_a, cut)
    ]

    def score(logits_e, logits_a):
        logprob_e = logits_e - shift_e
        logprob_a = logits_a - shift_a
        return logprob_e - logprob_a - penalty_slope * jnp.maximum(cuts - logprob_e, 0.0)

    return [peak_e - log_total_e, peak_a - log_total_a], score


def finish_kernel(stats_ref, gap_ref, top_ref, peaks_ref, chosen_ref, lacking_ref):
    peaks, score = totals_of(stats_ref, gap_ref)
    stats = stats_ref[...]
    for i, peak in enumerate(peaks):
        peaks_ref[i:i + 1, :] = row_from(peak)
    picks = [jnp.sum(lane_at(stats, i), axis=0) for i in (4, 5)]
    chosen_ref[...] = row_from(score(*picks))
    lane = lax.broadcasted_iota(jnp.int32, stats.shape[1:], 1)
    is_candidate = (lane >= FIRST) & (lane < FIRST + 2 * (NEAR + TOP))
    parts, lacking = [], jnp.zeros(stats.shape[1:], jnp.float32)
    for plane in range(stats.shape[0]):
        e, a = stats[plane], pltpu.roll(stats[plane], 64, 1)
        value = jnp.where(e > dead_below, score(e, a), masked_floor)
        parts.append(jnp.where(is_candidate, value, -jnp.inf))
        lacking = jnp.maximum(lacking, jnp.where(lane == 6, e, 0.0))
    top_ref[...] = lanes_of(best_of(sorted_levels(parts)), top_ref.shape)
    lacking_ref[0] = jnp.where(jnp.max(lacking) > 0.0, 1, 0).astype(jnp.int32)


def score_kernel(width, table_ref, stats_ref, gap_ref, best_ref):
    _, score = totals_of(stats_ref, gap_ref, 2)
    own = table_ref.shape[1] // 2
    real = lax.broadcasted_iota(jnp.int32, (2 * own, 128), 1) < width // 2
    parts = []
    for source in range(table_ref.shape[0]):
        e, a = table_ref[source, :, 0:128], table_ref[source, :, 128:256]
        parts.append(jnp.where(real & (e > dead_below), score(e, a), masked_floor))
    found = best_of(sorted_levels(parts))
    found = [value[:own] for value in found] + [value[own:] for value in found]
    best = lanes_of(found, best_ref.shape[1:])
    for plane in range(best_ref.shape[0]):
        best_ref[plane] = best


def merge_kernel(parts_ref, out_ref):
    shape = parts_ref.shape[1:]
    real = lax.broadcasted_iota(jnp.int32, shape, 1) < 2 * TOP
    parts = [jnp.where(real, parts_ref[i], -jnp.inf) for i in range(parts_ref.shape[0])]
    out_ref[...] = lanes_of(best_of(sorted_levels(parts)), out_ref.shape)


def per_device(
    expert_hidden,
    expert_gain,
    expert_head,
    amateur_hidden,
    amateur_gain,
    amateur_head,
    live_mask,
    token_ids,
    plaus_level,
):
    own, depth_e = expert_hidden.shape
    depth_a = amateur_hidden.shape[1]
    width = expert_head.shape[0]
    rows, planes = lax.axis_size("rows"), lax.axis_size("vocab")
    beams = own * rows
    quarter = (depth_e + depth_a) // 4
    row, plane = lax.axis_index("rows"), lax.axis_index("vocab")
    position = jnp.stack([row % NC, (row * planes + plane) * width]).astype(jnp.int32)
    ids = token_ids.reshape(rows // 4, 2, 2, own).swapaxes(1, 2).reshape(beams, 1)
    gap = lax.dynamic_slice_in_dim(plaus_level, row * own, own, 0).reshape(own, 1)

    norm_inputs = (
        expert_hidden, expert_gain.reshape(-1, 128), amateur_hidden, amateur_gain.reshape(-1, 128)
    )
    blocks = pl.pallas_call(
        norm_kernel,
        out_shape=jax.ShapeDtypeStruct((rows, 2 * own, quarter), jnp.bfloat16),
        in_specs=[HBM] * 4,
        out_specs=HBM,
        scratch_shapes=[pltpu.VMEM(x.shape, x.dtype) for x in norm_inputs] + [
            pltpu.VMEM((NC, 2 * own, quarter), jnp.bfloat16),
            pltpu.SemaphoreType.DMA((4,)),
            pltpu.SemaphoreType.DMA((rows,)),
        ],
        compiler_params=WIDE_PARAMS,
        name="norms",
    )(*norm_inputs)
    half = lax.all_to_all(blocks, "rows", 0, 0, tiled=True).reshape(2 * beams, quarter)
    other_half = lax.ppermute(half, "rows", [(r, r ^ 1) for r in range(rows)])
    cost = pl.CostEstimate(
        flops=4 * beams * width * 2 * quarter, bytes_accessed=4 * beams * quarter, transcendentals=0
    )
    first = pl.pallas_call(
        first_kernel,
        out_shape=jax.ShapeDtypeStruct((2, beams, width), jnp.float32),
        in_specs=[SMEM] + [VMEM] * 3,
        out_specs=VMEM,
        compiler_params=PARAMS,
        cost_estimate=cost,
        name="first_half",
    )(position, half, expert_head, amateur_head)
    table = pl.pallas_call(
        second_kernel,
        out_shape=jax.ShapeDtypeStruct((rows, 2 * own, 256), jnp.float32),
        in_specs=[SMEM] + [VMEM] * 7,
        out_specs=VMEM,
        scratch_shapes=[pltpu.VMEM((2, beams, width), jnp.float32)],
        compiler_params=PARAMS,
        cost_estimate=cost,
        name="second_half",
    )(position, other_half, expert_head, amateur_head, first, live_mask.reshape(1, -1), ids, gap)
    table = lax.all_to_all(table, "rows", 0, 0, tiled=True)

    small = jax.ShapeDtypeStruct((planes, own, 128), jnp.float32)
    best_shape = jax.ShapeDtypeStruct((own, TOP), jnp.float32)
    stats = pl.pallas_call(
        functools.partial(stats_kernel, width),
        out_shape=small,
        in_specs=[VMEM] * 2,
        out_specs=VMEM,
        compiler_params=PARAMS,
        name="stats",
    )(table, gap)
    stats = lax.all_to_all(stats, "vocab", 0, 0, tiled=True)
    top, peaks, chosen, lacking = pl.pallas_call(
        finish_kernel,
        out_shape=(
            best_shape,
            jax.ShapeDtypeStruct((2, own), jnp.float32),
            jax.ShapeDtypeStruct((1, own), jnp.float32),
            jax.ShapeDtypeStruct((1,), jnp.int32),
        ),
        in_specs=[VMEM] * 2,
        out_specs=(VMEM, VMEM, VMEM, SMEM),
        compiler_params=PARAMS,
        name="finish",
    )(stats, gap)

    def with_every_entry(table, stats, gap, _):
        best = pl.pallas_call(
            functools.partial(score_kernel, width),
            out_shape=small,
            in_specs=[VMEM] * 3,
            out_specs=VMEM,
            compiler_params=PARAMS,
            name="scores",
        )(table, stats, gap)
        best = lax.all_to_all(best, "vocab", 0, 0, tiled=True)
        return pl.pallas_call(
            merge_kernel,
            out_shape=best_shape,
            in_specs=[VMEM],
            out_specs=VMEM,
            compiler_params=PARAMS,
            name="merge",
        )(best)

    top = lax.cond(lacking[0] > 0, with_every_entry, lambda *args: args[-1], table, stats, gap, top)
    return top, peaks.T, chosen.reshape(own)


def solution(mesh):
    in_specs = (
        P("rows", None),
        P(),
        P(("rows", "vocab"), None),
        P("rows", None),
        P(),
        P(("rows", "vocab"), None),
        P(("rows", "vocab")),
        P(),
        P(),
    )
    out_specs = (P("rows", None), P("rows", None), P("rows"))
    return jax.shard_map(
        per_device, mesh=mesh, in_specs=in_specs, out_specs=out_specs, check_vma=False
    )
```

```python
import functools

import jax
import jax.numpy as jnp
from jax import lax
from jax.experimental import pallas as pl
from jax.experimental.pallas import tpu as pltpu
from jax.sharding import PartitionSpec as P

TOP = 4
NEAR = 20
FIRST = 16
NC = 2

masked_floor = -1e30
dead_below = -5e29
penalty_slope = 2.0
norm_epsilon = 1e-06

VMEM = pl.BlockSpec(memory_space=pltpu.VMEM)
HBM = pl.BlockSpec(memory_space=pltpu.HBM)
SMEM = pl.BlockSpec(memory_space=pltpu.SMEM)
WIDE_PARAMS = pltpu.CompilerParams(vmem_limit_bytes=60 * 1024 * 1024)
PARAMS = pltpu.CompilerParams(vmem_limit_bytes=16 * 1024 * 1024)


def norm_kernel(*refs):
    inputs, out_ref, held, block_ref, sems, out_sems = refs[:4], refs[4], refs[5:9], *refs[9:]
    copies = [pltpu.make_async_copy(inputs[i], held[i], sems.at[i]) for i in range(4)]
    for copy in copies:
        copy.start()
    quarters = []
    for model in range(2):
        copies[2 * model].wait()
        copies[2 * model + 1].wait()
        values = held[2 * model][...].astype(jnp.float32)
        gain = held[2 * model + 1][...].astype(jnp.float32)
        mean = jnp.mean(values * values, axis=-1, keepdims=True)
        values = values * lax.rsqrt(mean + norm_epsilon)
        chunks = [
            values[:, 128 * i:128 * i + 128] * gain[i:i + 1, :] for i in range(values.shape[1] // 128)
        ]
        each = len(chunks) // 4
        quarters.append([chunks[each * q:each * q + each] for q in range(4)])
    sent = []
    for core in range(NC):
        rows = [quarters[0][2 * core + p] + quarters[1][2 * core + p] for p in range(2)]
        for i, pair in enumerate(zip(*rows)):
            block_ref[core, :, 128 * i:128 * i + 128] = jnp.concatenate(pair).astype(jnp.bfloat16)
        for dest in range(core, out_ref.shape[0], NC):
            sent.append(pltpu.make_async_copy(block_ref.at[core], out_ref.at[dest], out_sems.at[dest]))
            sent[-1].start()
    for copy in sent:
        copy.wait()


def quarters_apart(part):
    groups = part.reshape(part.shape[0] // 32, 2, 16, part.shape[1])
    even, odd = groups[:, 0], groups[:, 1]
    first = lax.broadcasted_iota(jnp.int32, even.shape, 1) % 8 < 4
    down = pltpu.roll(odd, 4, 1)
    up = pltpu.roll(even, 12, 1)
    apart = jnp.where(first, even, down), jnp.where(first, up, odd)
    return [x.reshape(part.shape[0] // 2, part.shape[1]) for x in apart]


def half_sums(core, part_ref, head_refs, acc_ref):
    low = 0
    for model, head in enumerate(head_refs):
        size = head.shape[1] // 4
        total = None
        for p, rows in enumerate(quarters_apart(part_ref[:, low:low + size])):
            columns = pl.ds(pl.multiple_of((2 * core + p) * size, 128), size)
            product = lax.dot_general(
                rows, head[:, columns], (((1,), (1,)), ((), ())), preferred_element_type=jnp.float32
            )
            total = product if total is None else total + product
        acc_ref[model] = total
        low += size


def first_kernel(pos_ref, part_ref, he_ref, ha_ref, out_ref):
    half_sums(pos_ref[0], part_ref, (he_ref, ha_ref), out_ref)


def second_kernel(
    pos_ref, part_ref, he_ref, ha_ref, first_ref, live_ref, ids_ref, _, out_ref, acc_ref
):
    beams, width = ids_ref.shape[0], he_ref.shape[0]
    half_sums(1 - pos_ref[0], part_ref, (he_ref, ha_ref), acc_ref)
    hits = ids_ref[...] == pos_ref[1] + lax.broadcasted_iota(jnp.int32, (1, width), 1)
    live = live_ref[...] == 1
    half = width // 2
    tiles = (beams // 8, 8, 128)
    upper = lax.broadcasted_iota(jnp.int32, tiles, 1) < 4
    for model in range(2):
        logits = first_ref[model] + acc_ref[model]
        pick = jnp.sum(jnp.where(hits, logits, 0.0), axis=1, keepdims=True)
        pick = jnp.broadcast_to(pick, (beams, 128 - half))
        held = jnp.where(live, logits, masked_floor)
        left = jnp.concatenate([held[:, :half], pick], axis=1).reshape(tiles)
        right = jnp.concatenate([held[:, half:], pick], axis=1).reshape(tiles)
        low_owner = jnp.where(upper, left, pltpu.roll(right, 4, 1))
        high_owner = jnp.where(upper, pltpu.roll(left, 4, 1), right)
        lanes = slice(128 * model, 128 * model + 128)
        for tile in range(tiles[0]):
            owner = 4 * (tile // 2) + tile % 2
            out_ref[owner, :, lanes] = low_owner[tile]
            out_ref[owner + 2, :, lanes] = high_owner[tile]


def lanes_of(columns, shape):
    lane = lax.broadcasted_iota(jnp.int32, shape, len(shape) - 1)
    result = jnp.zeros(shape, jnp.float32)
    for i, column in enumerate(columns):
        result = jnp.where(lane == i, column, result)
    return result


def lane_at(values, i):
    lane = lax.broadcasted_iota(jnp.int32, values.shape, values.ndim - 1)
    return jnp.sum(jnp.where(lane == i, values, 0.0), axis=-1, keepdims=True)


def total_rows(values):
    return jnp.sum(values, axis=1, keepdims=True)


def insert(levels, entry):
    for i, level in enumerate(levels):
        above = entry[0] > level[0]
        levels[i] = tuple(jnp.where(above, new, old) for new, old in zip(entry, level))
        entry = tuple(jnp.where(above, old, new) for new, old in zip(entry, level))


def remove_top(levels, top):
    hit = levels[0][0] == top
    payload = [total_rows(jnp.where(hit, field, 0.0)) for field in levels[0][1:]]
    count = total_rows(jnp.where(hit, 1.0, 0.0))
    last = tuple(jnp.full_like(f, masked_floor) for f in levels[0])
    lower = levels[1:] + [last]
    return payload, count, [
        tuple(jnp.where(hit, new, old) for new, old in zip(low, level))
        for low, level in zip(lower, levels)
    ]


def stats_kernel(width, table_ref, gap_ref, out_ref):
    sources, own = table_ref.shape[0], table_ref.shape[1] // 2
    shape = (2 * own, 128)
    real = lax.broadcasted_iota(jnp.int32, shape, 1) < width // 2
    columns = []
    for model in range(2):
        parts = [table_ref[i, :, 128 * model:128 * model + 128] for i in range(sources)]
        peak = functools.reduce(jnp.maximum, parts)
        peak = jnp.max(jnp.where(real, peak, masked_floor), axis=1, keepdims=True)
        peak = jnp.maximum(peak[:own], peak[own:])
        both = jnp.concatenate([peak, peak])
        total = functools.reduce(jnp.add, [jnp.exp(part - both) for part in parts])
        total = total_rows(jnp.where(real, total, 0.0))
        pick = lane_at(functools.reduce(jnp.add, parts), width // 2)
        columns.append((peak, total[:own] + total[own:], pick[:own]))
    (pe, te, ce), (pa, ta, ca) = columns
    least = pe - gap_ref[...].astype(jnp.float32) * 0.1
    least = jnp.concatenate([least, least])
    floor = jnp.full(shape, masked_floor, jnp.float32)
    near, rest = [(floor,) * 2] * TOP, [(floor,) * 3] * TOP
    count = jnp.zeros(shape, jnp.float32)
    for i in range(sources):
        e, a = table_ref[i, :, 0:128], table_ref[i, :, 128:256]
        live = real & (e > dead_below)
        is_near = live & (e >= least)
        count += jnp.where(is_near, 1.0, 0.0)
        insert(near, (jnp.where(is_near, e, masked_floor), a))
        insert(rest, (jnp.where(live & (e < least), 3.0 * e - a, masked_floor), e, a))
    missing = total_rows(count)
    picked = []
    for _ in range(NEAR):
        top = jnp.max(near[0][0], axis=1, keepdims=True)
        (a,), hits, near = remove_top(near, top)
        found = top > dead_below
        picked.append((jnp.where(found, top, masked_floor), a))
        missing -= jnp.where(found & (hits == 1.0), 1.0, 0.0)
    for _ in range(TOP):
        top = jnp.max(rest[0][0], axis=1, keepdims=True)
        (e, a), hits, rest = remove_top(rest, top)
        found = top > dead_below
        picked.append((jnp.where(found, e, masked_floor), a))
        missing += jnp.where(found & (hits > 1.0), 1.0, 0.0)
    zeros = [jnp.zeros_like(missing)]
    lanes = zeros * FIRST + [e for e, _ in picked]
    lanes += zeros * (64 + FIRST - len(lanes)) + [a for _, a in picked]
    lanes = lanes_of(lanes, shape)
    stats = lanes_of([pe, pa, te, ta, ce, ca, missing[:own] + missing[own:]], (own, 128))
    stats += lanes[:own] + pltpu.roll(lanes, len(picked), 1)[own:]
    for plane in range(out_ref.shape[0]):
        out_ref[plane] = stats


def best_of(levels):
    tops, counts, seen = [], [], 0.0
    for _ in range(TOP):
        top = jnp.max(levels[0], axis=1, keepdims=True)
        hit = levels[0] == top
        seen = seen + total_rows(jnp.where(hit, 1.0, 0.0))
        tops.append(top)
        counts.append(seen)
        lower = levels[1:] + [jnp.full_like(levels[0], -jnp.inf)]
        levels = [jnp.where(hit, low, level) for level, low in zip(levels, lower)]
    found = []
    for i in range(TOP):
        value = tops[-1]
        for top, seen in reversed(list(zip(tops, counts))):
            value = jnp.where(seen > i, top, value)
        found.append(value)
    return found


def sorted_levels(parts):
    levels = [jnp.full_like(parts[0], -jnp.inf)] * TOP
    for part in parts:
        for i in range(TOP):
            levels[i], part = jnp.maximum(levels[i], part), jnp.minimum(levels[i], part)
    return levels


def row_from(column):
    shape = (column.shape[0], column.shape[0])
    here = lax.broadcasted_iota(jnp.int32, shape, 0) == lax.broadcasted_iota(jnp.int32, shape, 1)
    return jnp.sum(jnp.where(here, column, 0.0), axis=0, keepdims=True)


def totals_of(stats_ref, gap_ref, copies=1):
    stats = stats_ref[...]
    peak_e, peak_a, sum_e, sum_a = [lane_at(stats, i) for i in range(4)]

    def total_of(peaks, sums):
        peak = jnp.max(peaks, axis=0)
        return peak, peak + jnp.log(jnp.sum(sums * jnp.exp(peaks - peak[None]), axis=0))

    peak_e, log_total_e = total_of(peak_e, sum_e)
    peak_a, log_total_a = total_of(peak_a, sum_a)
    cut = peak_e - log_total_e - gap_ref[...].astype(jnp.float32) * 0.1
    shift_e, shift_a, cuts = [
        jnp.concatenate([x] * copies) if copies > 1 else x for x in (log_total_e, log_total_a, cut)
    ]

    def score(logits_e, logits_a):
        logprob_e = logits_e - shift_e
        logprob_a = logits_a - shift_a
        return logprob_e - logprob_a - penalty_slope * jnp.maximum(cuts - logprob_e, 0.0)

    return [peak_e - log_total_e, peak_a - log_total_a], score


def finish_kernel(stats_ref, gap_ref, top_ref, peaks_ref, chosen_ref, lacking_ref):
    peaks, score = totals_of(stats_ref, gap_ref)
    stats = stats_ref[...]
    for i, peak in enumerate(peaks):
        peaks_ref[i:i + 1, :] = row_from(peak)
    picks = [jnp.sum(lane_at(stats, i), axis=0) for i in (4, 5)]
    chosen_ref[...] = row_from(score(*picks))
    lane = lax.broadcasted_iota(jnp.int32, stats.shape[1:], 1)
    is_candidate = (lane >= FIRST) & (lane < FIRST + 2 * (NEAR + TOP))
    parts, lacking = [], jnp.zeros(stats.shape[1:], jnp.float32)
    for plane in range(stats.shape[0]):
        e, a = stats[plane], pltpu.roll(stats[plane], 64, 1)
        value = jnp.where(e > dead_below, score(e, a), masked_floor)
        parts.append(jnp.where(is_candidate, value, -jnp.inf))
        lacking = jnp.maximum(lacking, jnp.where(lane == 6, e, 0.0))
    top_ref[...] = lanes_of(best_of(sorted_levels(parts)), top_ref.shape)
    lacking_ref[0] = jnp.where(jnp.max(lacking) > 0.0, 1, 0).astype(jnp.int32)


def score_kernel(width, table_ref, stats_ref, gap_ref, best_ref):
    _, score = totals_of(stats_ref, gap_ref, 2)
    own = table_ref.shape[1] // 2
    real = lax.broadcasted_iota(jnp.int32, (2 * own, 128), 1) < width // 2
    parts = []
    for source in range(table_ref.shape[0]):
        e, a = table_ref[source, :, 0:128], table_ref[source, :, 128:256]
        parts.append(jnp.where(real & (e > dead_below), score(e, a), masked_floor))
    found = best_of(sorted_levels(parts))
    found = [value[:own] for value in found] + [value[own:] for value in found]
    best = lanes_of(found, best_ref.shape[1:])
    for plane in range(best_ref.shape[0]):
        best_ref[plane] = best


def merge_kernel(parts_ref, out_ref):
    shape = parts_ref.shape[1:]
    real = lax.broadcasted_iota(jnp.int32, shape, 1) < 2 * TOP
    parts = [jnp.where(real, parts_ref[i], -jnp.inf) for i in range(parts_ref.shape[0])]
    out_ref[...] = lanes_of(best_of(sorted_levels(parts)), out_ref.shape)


def per_device(
    expert_hidden,
    expert_gain,
    expert_head,
    amateur_hidden,
    amateur_gain,
    amateur_head,
    live_mask,
    token_ids,
    plaus_level,
):
    own, depth_e = expert_hidden.shape
    depth_a = amateur_hidden.shape[1]
    width = expert_head.shape[0]
    rows, planes = lax.axis_size("rows"), lax.axis_size("vocab")
    beams = own * rows
    quarter = (depth_e + depth_a) // 4
    row, plane = lax.axis_index("rows"), lax.axis_index("vocab")
    position = jnp.stack([row % NC, (row * planes + plane) * width]).astype(jnp.int32)
    ids = token_ids.reshape(rows // 4, 2, 2, own).swapaxes(1, 2).reshape(beams, 1)
    gap = lax.dynamic_slice_in_dim(plaus_level, row * own, own, 0).reshape(own, 1)

    norm_inputs = (
        expert_hidden, expert_gain.reshape(-1, 128), amateur_hidden, amateur_gain.reshape(-1, 128)
    )
    blocks = pl.pallas_call(
        norm_kernel,
        out_shape=jax.ShapeDtypeStruct((rows, 2 * own, quarter), jnp.bfloat16),
        in_specs=[HBM] * 4,
        out_specs=HBM,
        scratch_shapes=[pltpu.VMEM(x.shape, x.dtype) for x in norm_inputs] + [
            pltpu.VMEM((NC, 2 * own, quarter), jnp.bfloat16),
            pltpu.SemaphoreType.DMA((4,)),
            pltpu.SemaphoreType.DMA((rows,)),
        ],
        compiler_params=WIDE_PARAMS,
        name="norms",
    )(*norm_inputs)
    blocks, expert_head, amateur_head = lax.optimization_barrier(
        (blocks, expert_head, amateur_head)
    )
    half = lax.all_to_all(blocks, "rows", 0, 0, tiled=True).reshape(2 * beams, quarter)
    other_half = lax.ppermute(half, "rows", [(r, r ^ 1) for r in range(rows)])
    cost = pl.CostEstimate(
        flops=4 * beams * width * 2 * quarter, bytes_accessed=4 * beams * quarter, transcendentals=0
    )
    first = pl.pallas_call(
        first_kernel,
        out_shape=jax.ShapeDtypeStruct((2, beams, width), jnp.float32),
        in_specs=[SMEM] + [VMEM] * 3,
        out_specs=VMEM,
        compiler_params=PARAMS,
        cost_estimate=cost,
        name="first_half",
    )(position, half, expert_head, amateur_head)
    table = pl.pallas_call(
        second_kernel,
        out_shape=jax.ShapeDtypeStruct((rows, 2 * own, 256), jnp.float32),
        in_specs=[SMEM] + [VMEM] * 7,
        out_specs=VMEM,
        scratch_shapes=[pltpu.VMEM((2, beams, width), jnp.float32)],
        compiler_params=PARAMS,
        cost_estimate=cost,
        name="second_half",
    )(position, other_half, expert_head, amateur_head, first, live_mask.reshape(1, -1), ids, gap)
    table = lax.all_to_all(table, "rows", 0, 0, tiled=True)

    small = jax.ShapeDtypeStruct((planes, own, 128), jnp.float32)
    best_shape = jax.ShapeDtypeStruct((own, TOP), jnp.float32)
    stats = pl.pallas_call(
        functools.partial(stats_kernel, width),
        out_shape=small,
        in_specs=[VMEM] * 2,
        out_specs=VMEM,
        compiler_params=PARAMS,
        name="stats",
    )(table, gap)
    stats = lax.all_to_all(stats, "vocab", 0, 0, tiled=True)
    top, peaks, chosen, lacking = pl.pallas_call(
        finish_kernel,
        out_shape=(
            best_shape,
            jax.ShapeDtypeStruct((2, own), jnp.float32),
            jax.ShapeDtypeStruct((1, own), jnp.float32),
            jax.ShapeDtypeStruct((1,), jnp.int32),
        ),
        in_specs=[VMEM] * 2,
        out_specs=(VMEM, VMEM, VMEM, SMEM),
        compiler_params=PARAMS,
        name="finish",
    )(stats, gap)

    def with_every_entry(table, stats, gap, _):
        best = pl.pallas_call(
            functools.partial(score_kernel, width),
            out_shape=small,
            in_specs=[VMEM] * 3,
            out_specs=VMEM,
            compiler_params=PARAMS,
            name="scores",
        )(table, stats, gap)
        best = lax.all_to_all(best, "vocab", 0, 0, tiled=True)
        return pl.pallas_call(
            merge_kernel,
            out_shape=best_shape,
            in_specs=[VMEM],
            out_specs=VMEM,
            compiler_params=PARAMS,
            name="merge",
        )(best)

    top = lax.cond(lacking[0] > 0, with_every_entry, lambda *args: args[-1], table, stats, gap, top)
    return top, peaks.T, chosen.reshape(own)


def solution(mesh):
    in_specs = (
        P("rows", None),
        P(),
        P(("rows", "vocab"), None),
        P("rows", None),
        P(),
        P(("rows", "vocab"), None),
        P(("rows", "vocab")),
        P(),
        P(),
    )
    out_specs = (P("rows", None), P("rows", None), P("rows"))
    return jax.shard_map(
        per_device, mesh=mesh, in_specs=in_specs, out_specs=out_specs, check_vma=False
    )
```

```python
import functools

import jax
import jax.numpy as jnp
from jax import lax
from jax.experimental import pallas as pl
from jax.experimental.pallas import tpu as pltpu
from jax.sharding import PartitionSpec as P

TOP = 4
NEAR = 20
FIRST = 16
NC = 2

masked_floor = -1e30
dead_below = -5e29
penalty_slope = 2.0
norm_epsilon = 1e-06

VMEM = pl.BlockSpec(memory_space=pltpu.VMEM)
HBM = pl.BlockSpec(memory_space=pltpu.HBM)
SMEM = pl.BlockSpec(memory_space=pltpu.SMEM)
WIDE_PARAMS = pltpu.CompilerParams(vmem_limit_bytes=60 * 1024 * 1024)
PARAMS = pltpu.CompilerParams(vmem_limit_bytes=16 * 1024 * 1024)


def norm_kernel(*refs):
    inputs, out_ref, held, block_ref, sems, out_sems = refs[:4], refs[4], refs[5:9], *refs[9:]
    copies = [pltpu.make_async_copy(inputs[i], held[i], sems.at[i]) for i in range(4)]
    for copy in copies:
        copy.start()
    quarters = []
    for model in range(2):
        copies[2 * model].wait()
        copies[2 * model + 1].wait()
        values = held[2 * model][...].astype(jnp.float32)
        gain = held[2 * model + 1][...].astype(jnp.float32)
        mean = jnp.mean(values * values, axis=-1, keepdims=True)
        values = values * lax.rsqrt(mean + norm_epsilon)
        chunks = [
            values[:, 128 * i:128 * i + 128] * gain[i:i + 1, :] for i in range(values.shape[1] // 128)
        ]
        each = len(chunks) // 4
        quarters.append([chunks[each * q:each * q + each] for q in range(4)])
    sent = []
    for core in range(NC):
        rows = [quarters[0][2 * core + p] + quarters[1][2 * core + p] for p in range(2)]
        for i, pair in enumerate(zip(*rows)):
            block_ref[core, :, 128 * i:128 * i + 128] = jnp.concatenate(pair).astype(jnp.bfloat16)
        for dest in range(core, out_ref.shape[0], NC):
            sent.append(pltpu.make_async_copy(block_ref.at[core], out_ref.at[dest], out_sems.at[dest]))
            sent[-1].start()
    for copy in sent:
        copy.wait()


def quarters_apart(part):
    groups = part.reshape(part.shape[0] // 32, 2, 16, part.shape[1])
    even, odd = groups[:, 0], groups[:, 1]
    first = lax.broadcasted_iota(jnp.int32, even.shape, 1) % 8 < 4
    down = pltpu.roll(odd, 4, 1)
    up = pltpu.roll(even, 12, 1)
    apart = jnp.where(first, even, down), jnp.where(first, up, odd)
    return [x.reshape(part.shape[0] // 2, part.shape[1]) for x in apart]


def half_sums(core, part_ref, head_refs, acc_ref):
    low = 0
    for model, head in enumerate(head_refs):
        size = head.shape[1] // 4
        total = None
        for p, rows in enumerate(quarters_apart(part_ref[:, low:low + size])):
            columns = pl.ds(pl.multiple_of((2 * core + p) * size, 128), size)
            product = lax.dot_general(
                rows, head[:, columns], (((1,), (1,)), ((), ())), preferred_element_type=jnp.float32
            )
            total = product if total is None else total + product
        acc_ref[model] = total
        low += size


def first_kernel(pos_ref, part_ref, he_ref, ha_ref, out_ref):
    half_sums(pos_ref[0], part_ref, (he_ref, ha_ref), out_ref)


def second_kernel(
    pos_ref, part_ref, he_ref, ha_ref, first_ref, live_ref, ids_ref, _, out_ref, acc_ref
):
    beams, width = ids_ref.shape[0], he_ref.shape[0]
    half_sums(1 - pos_ref[0], part_ref, (he_ref, ha_ref), acc_ref)
    hits = ids_ref[...] == pos_ref[1] + lax.broadcasted_iota(jnp.int32, (1, width), 1)
    live = live_ref[...] == 1
    half = width // 2
    tiles = (beams // 8, 8, 128)
    upper = lax.broadcasted_iota(jnp.int32, tiles, 1) < 4
    for model in range(2):
        logits = first_ref[model] + acc_ref[model]
        pick = jnp.sum(jnp.where(hits, logits, 0.0), axis=1, keepdims=True)
        pick = jnp.broadcast_to(pick, (beams, 128 - half))
        held = jnp.where(live, logits, masked_floor)
        left = jnp.concatenate([held[:, :half], pick], axis=1).reshape(tiles)
        right = jnp.concatenate([held[:, half:], pick], axis=1).reshape(tiles)
        low_owner = jnp.where(upper, left, pltpu.roll(right, 4, 1))
        high_owner = jnp.where(upper, pltpu.roll(left, 4, 1), right)
        lanes = slice(128 * model, 128 * model + 128)
        for tile in range(tiles[0]):
            owner = 4 * (tile // 2) + tile % 2
            out_ref[owner, :, lanes] = low_owner[tile]
            out_ref[owner + 2, :, lanes] = high_owner[tile]


def lanes_of(columns, shape):
    lane = lax.broadcasted_iota(jnp.int32, shape, len(shape) - 1)
    result = jnp.zeros(shape, jnp.float32)
    for i, column in enumerate(columns):
        result = jnp.where(lane == i, column, result)
    return result


def lane_at(values, i):
    lane = lax.broadcasted_iota(jnp.int32, values.shape, values.ndim - 1)
    return jnp.sum(jnp.where(lane == i, values, 0.0), axis=-1, keepdims=True)


def total_rows(values):
    return jnp.sum(values, axis=1, keepdims=True)


def insert(levels, entry):
    for i, level in enumerate(levels):
        above = entry[0] > level[0]
        levels[i] = tuple(jnp.where(above, new, old) for new, old in zip(entry, level))
        entry = tuple(jnp.where(above, old, new) for new, old in zip(entry, level))


def remove_top(levels, top):
    hit = levels[0][0] == top
    payload = [total_rows(jnp.where(hit, field, 0.0)) for field in levels[0][1:]]
    count = total_rows(jnp.where(hit, 1.0, 0.0))
    last = tuple(jnp.full_like(f, masked_floor) for f in levels[0])
    lower = levels[1:] + [last]
    return payload, count, [
        tuple(jnp.where(hit, new, old) for new, old in zip(low, level))
        for low, level in zip(lower, levels)
    ]


def stats_kernel(width, table_ref, gap_ref, out_ref):
    sources, own = table_ref.shape[0], table_ref.shape[1] // 2
    shape = (2 * own, 128)
    real = lax.broadcasted_iota(jnp.int32, shape, 1) < width // 2
    columns = []
    for model in range(2):
        parts = [table_ref[i, :, 128 * model:128 * model + 128] for i in range(sources)]
        peak = functools.reduce(jnp.maximum, parts)
        peak = jnp.max(jnp.where(real, peak, masked_floor), axis=1, keepdims=True)
        peak = jnp.maximum(peak[:own], peak[own:])
        both = jnp.concatenate([peak, peak])
        total = functools.reduce(jnp.add, [jnp.exp(part - both) for part in parts])
        total = total_rows(jnp.where(real, total, 0.0))
        pick = lane_at(functools.reduce(jnp.add, parts), width // 2)
        columns.append((peak, total[:own] + total[own:], pick[:own]))
    (pe, te, ce), (pa, ta, ca) = columns
    least = pe - gap_ref[...].astype(jnp.float32) * 0.1
    least = jnp.concatenate([least, least])
    floor = jnp.full(shape, masked_floor, jnp.float32)
    near, rest = [(floor,) * 2] * TOP, [(floor,) * 3] * TOP
    count = jnp.zeros(shape, jnp.float32)
    for i in range(sources):
        e, a = table_ref[i, :, 0:128], table_ref[i, :, 128:256]
        live = real & (e > dead_below)
        is_near = live & (e >= least)
        count += jnp.where(is_near, 1.0, 0.0)
        insert(near, (jnp.where(is_near, e, masked_floor), a))
        insert(rest, (jnp.where(live & (e < least), 3.0 * e - a, masked_floor), e, a))
    missing = total_rows(count)
    picked = []
    for _ in range(NEAR):
        top = jnp.max(near[0][0], axis=1, keepdims=True)
        (a,), hits, near = remove_top(near, top)
        found = top > dead_below
        picked.append((jnp.where(found, top, masked_floor), a))
        missing -= jnp.where(found & (hits == 1.0), 1.0, 0.0)
    for _ in range(TOP):
        top = jnp.max(rest[0][0], axis=1, keepdims=True)
        (e, a), hits, rest = remove_top(rest, top)
        found = top > dead_below
        picked.append((jnp.where(found, e, masked_floor), a))
        missing += jnp.where(found & (hits > 1.0), 1.0, 0.0)
    zeros = [jnp.zeros_like(missing)]
    lanes = zeros * FIRST + [e for e, _ in picked]
    lanes += zeros * (64 + FIRST - len(lanes)) + [a for _, a in picked]
    lanes = lanes_of(lanes, shape)
    stats = lanes_of([pe, pa, te, ta, ce, ca, missing[:own] + missing[own:]], (own, 128))
    stats += lanes[:own] + pltpu.roll(lanes, len(picked), 1)[own:]
    for plane in range(out_ref.shape[0]):
        out_ref[plane] = stats


def best_of(levels):
    tops, counts, seen = [], [], 0.0
    for _ in range(TOP):
        top = jnp.max(levels[0], axis=1, keepdims=True)
        hit = levels[0] == top
        seen = seen + total_rows(jnp.where(hit, 1.0, 0.0))
        tops.append(top)
        counts.append(seen)
        lower = levels[1:] + [jnp.full_like(levels[0], -jnp.inf)]
        levels = [jnp.where(hit, low, level) for level, low in zip(levels, lower)]
    found = []
    for i in range(TOP):
        value = tops[-1]
        for top, seen in reversed(list(zip(tops, counts))):
            value = jnp.where(seen > i, top, value)
        found.append(value)
    return found


def sorted_levels(parts):
    levels = [jnp.full_like(parts[0], -jnp.inf)] * TOP
    for part in parts:
        for i in range(TOP):
            levels[i], part = jnp.maximum(levels[i], part), jnp.minimum(levels[i], part)
    return levels


def row_from(column):
    shape = (column.shape[0], column.shape[0])
    here = lax.broadcasted_iota(jnp.int32, shape, 0) == lax.broadcasted_iota(jnp.int32, shape, 1)
    return jnp.sum(jnp.where(here, column, 0.0), axis=0, keepdims=True)


def totals_of(stats_ref, gap_ref, copies=1):
    stats = stats_ref[...]
    peak_e, peak_a, sum_e, sum_a = [lane_at(stats, i) for i in range(4)]

    def total_of(peaks, sums):
        peak = jnp.max(peaks, axis=0)
        return peak, peak + jnp.log(jnp.sum(sums * jnp.exp(peaks - peak[None]), axis=0))

    peak_e, log_total_e = total_of(peak_e, sum_e)
    peak_a, log_total_a = total_of(peak_a, sum_a)
    cut = peak_e - log_total_e - gap_ref[...].astype(jnp.float32) * 0.1
    shift_e, shift_a, cuts = [
        jnp.concatenate([x] * copies) if copies > 1 else x for x in (log_total_e, log_total_a, cut)
    ]

    def score(logits_e, logits_a):
        logprob_e = logits_e - shift_e
        logprob_a = logits_a - shift_a
        return logprob_e - logprob_a - penalty_slope * jnp.maximum(cuts - logprob_e, 0.0)

    return [peak_e - log_total_e, peak_a - log_total_a], score


def finish_kernel(stats_ref, gap_ref, top_ref, peaks_ref, chosen_ref, lacking_ref):
    peaks, score = totals_of(stats_ref, gap_ref)
    stats = stats_ref[...]
    for i, peak in enumerate(peaks):
        peaks_ref[i:i + 1, :] = row_from(peak)
    picks = [jnp.sum(lane_at(stats, i), axis=0) for i in (4, 5)]
    chosen_ref[...] = row_from(score(*picks))
    lane = lax.broadcasted_iota(jnp.int32, stats.shape[1:], 1)
    is_candidate = (lane >= FIRST) & (lane < FIRST + 2 * (NEAR + TOP))
    parts, lacking = [], jnp.zeros(stats.shape[1:], jnp.float32)
    for plane in range(stats.shape[0]):
        e, a = stats[plane], pltpu.roll(stats[plane], 64, 1)
        value = jnp.where(e > dead_below, score(e, a), masked_floor)
        parts.append(jnp.where(is_candidate, value, -jnp.inf))
        lacking = jnp.maximum(lacking, jnp.where(lane == 6, e, 0.0))
    top_ref[...] = lanes_of(best_of(sorted_levels(parts)), top_ref.shape)
    lacking_ref[0] = jnp.where(jnp.max(lacking) > 0.0, 1, 0).astype(jnp.int32)


def score_kernel(width, table_ref, stats_ref, gap_ref, best_ref):
    _, score = totals_of(stats_ref, gap_ref, 2)
    own = table_ref.shape[1] // 2
    real = lax.broadcasted_iota(jnp.int32, (2 * own, 128), 1) < width // 2
    parts = []
    for source in range(table_ref.shape[0]):
        e, a = table_ref[source, :, 0:128], table_ref[source, :, 128:256]
        parts.append(jnp.where(real & (e > dead_below), score(e, a), masked_floor))
    found = best_of(sorted_levels(parts))
    found = [value[:own] for value in found] + [value[own:] for value in found]
    best = lanes_of(found, best_ref.shape[1:])
    for plane in range(best_ref.shape[0]):
        best_ref[plane] = best


def merge_kernel(parts_ref, out_ref):
    shape = parts_ref.shape[1:]
    real = lax.broadcasted_iota(jnp.int32, shape, 1) < 2 * TOP
    parts = [jnp.where(real, parts_ref[i], -jnp.inf) for i in range(parts_ref.shape[0])]
    out_ref[...] = lanes_of(best_of(sorted_levels(parts)), out_ref.shape)


def per_device(
    expert_hidden,
    expert_gain,
    expert_head,
    amateur_hidden,
    amateur_gain,
    amateur_head,
    live_mask,
    token_ids,
    plaus_level,
):
    own, depth_e = expert_hidden.shape
    depth_a = amateur_hidden.shape[1]
    width = expert_head.shape[0]
    rows, planes = lax.axis_size("rows"), lax.axis_size("vocab")
    beams = own * rows
    quarter = (depth_e + depth_a) // 4
    row, plane = lax.axis_index("rows"), lax.axis_index("vocab")
    position = jnp.stack([row % NC, (row * planes + plane) * width]).astype(jnp.int32)
    ids = token_ids.reshape(rows // 4, 2, 2, own).swapaxes(1, 2).reshape(beams, 1)
    gap = lax.dynamic_slice_in_dim(plaus_level, row * own, own, 0).reshape(own, 1)

    norm_inputs = (
        expert_hidden, expert_gain.reshape(-1, 128), amateur_hidden, amateur_gain.reshape(-1, 128)
    )
    blocks = pl.pallas_call(
        norm_kernel,
        out_shape=jax.ShapeDtypeStruct((rows, 2 * own, quarter), jnp.bfloat16),
        in_specs=[HBM] * 4,
        out_specs=HBM,
        scratch_shapes=[pltpu.VMEM(x.shape, x.dtype) for x in norm_inputs] + [
            pltpu.VMEM((NC, 2 * own, quarter), jnp.bfloat16),
            pltpu.SemaphoreType.DMA((4,)),
            pltpu.SemaphoreType.DMA((rows,)),
        ],
        compiler_params=WIDE_PARAMS,
        name="norms",
    )(*norm_inputs)
    blocks, expert_head, amateur_head = lax.optimization_barrier(
        (blocks, expert_head, amateur_head)
    )
    half = lax.all_to_all(blocks, "rows", 0, 0, tiled=True).reshape(2 * beams, quarter)
    other_half = lax.ppermute(half, "rows", [(r, r ^ 1) for r in range(rows)])
    cost = pl.CostEstimate(
        flops=4 * beams * width * 2 * quarter, bytes_accessed=4 * beams * quarter, transcendentals=0
    )
    first = pl.pallas_call(
        first_kernel,
        out_shape=jax.ShapeDtypeStruct((2, beams, width), jnp.float32),
        in_specs=[SMEM] + [VMEM] * 3,
        out_specs=VMEM,
        compiler_params=PARAMS,
        cost_estimate=cost,
        name="first_half",
    )(position, half, expert_head, amateur_head)
    table = pl.pallas_call(
        second_kernel,
        out_shape=jax.ShapeDtypeStruct((rows, 2 * own, 256), jnp.float32),
        in_specs=[SMEM] + [VMEM] * 7,
        out_specs=VMEM,
        scratch_shapes=[pltpu.VMEM((2, beams, width), jnp.float32)],
        compiler_params=PARAMS,
        cost_estimate=cost,
        name="second_half",
    )(position, other_half, expert_head, amateur_head, first, live_mask.reshape(1, -1), ids, gap)
    table = lax.all_to_all(table, "rows", 0, 0, tiled=True)

    small = jax.ShapeDtypeStruct((planes, own, 128), jnp.float32)
    best_shape = jax.ShapeDtypeStruct((own, TOP), jnp.float32)
    stats = pl.pallas_call(
        functools.partial(stats_kernel, width),
        out_shape=small,
        in_specs=[VMEM] * 2,
        out_specs=VMEM,
        compiler_params=PARAMS,
        name="stats",
    )(table, gap)
    around = [[(planes // 2 + z) % planes for z in range(planes)]]
    stats = lax.all_to_all(stats, "vocab", 0, 0, tiled=True, axis_index_groups=around)
    top, peaks, chosen, lacking = pl.pallas_call(
        finish_kernel,
        out_shape=(
            best_shape,
            jax.ShapeDtypeStruct((2, own), jnp.float32),
            jax.ShapeDtypeStruct((1, own), jnp.float32),
            jax.ShapeDtypeStruct((1,), jnp.int32),
        ),
        in_specs=[VMEM] * 2,
        out_specs=(VMEM, VMEM, VMEM, SMEM),
        compiler_params=PARAMS,
        name="finish",
    )(stats, gap)

    def with_every_entry(table, stats, gap, _):
        best = pl.pallas_call(
            functools.partial(score_kernel, width),
            out_shape=small,
            in_specs=[VMEM] * 3,
            out_specs=VMEM,
            compiler_params=PARAMS,
            name="scores",
        )(table, stats, gap)
        best = lax.all_to_all(best, "vocab", 0, 0, tiled=True)
        return pl.pallas_call(
            merge_kernel,
            out_shape=best_shape,
            in_specs=[VMEM],
            out_specs=VMEM,
            compiler_params=PARAMS,
            name="merge",
        )(best)

    top = lax.cond(lacking[0] > 0, with_every_entry, lambda *args: args[-1], table, stats, gap, top)
    return top, peaks.T, chosen.reshape(own)


def solution(mesh):
    in_specs = (
        P("rows", None),
        P(),
        P(("rows", "vocab"), None),
        P("rows", None),
        P(),
        P(("rows", "vocab"), None),
        P(("rows", "vocab")),
        P(),
        P(),
    )
    out_specs = (P("rows", None), P("rows", None), P("rows"))
    return jax.shard_map(
        per_device, mesh=mesh, in_specs=in_specs, out_specs=out_specs, check_vma=False
    )
```

```python
import functools

import jax
import jax.numpy as jnp
from jax import lax
from jax.experimental import pallas as pl
from jax.experimental.pallas import tpu as pltpu
from jax.sharding import PartitionSpec as P

TOP = 4
NEAR = 20
FIRST = 16
NC = 2

masked_floor = -1e30
dead_below = -5e29
penalty_slope = 2.0
norm_epsilon = 1e-06

VMEM = pl.BlockSpec(memory_space=pltpu.VMEM)
HBM = pl.BlockSpec(memory_space=pltpu.HBM)
SMEM = pl.BlockSpec(memory_space=pltpu.SMEM)
WIDE_PARAMS = pltpu.CompilerParams(vmem_limit_bytes=60 * 1024 * 1024)
PARAMS = pltpu.CompilerParams(vmem_limit_bytes=16 * 1024 * 1024)


def norm_kernel(*refs):
    inputs, out_ref, held, block_ref, sems, out_sems = refs[:4], refs[4], refs[5:9], *refs[9:]
    copies = [pltpu.make_async_copy(inputs[i], held[i], sems.at[i]) for i in range(4)]
    for copy in copies:
        copy.start()
    quarters = []
    for model in range(2):
        copies[2 * model].wait()
        copies[2 * model + 1].wait()
        values = held[2 * model][...].astype(jnp.float32)
        gain = held[2 * model + 1][...].astype(jnp.float32)
        mean = jnp.mean(values * values, axis=-1, keepdims=True)
        values = values * lax.rsqrt(mean + norm_epsilon)
        chunks = [
            values[:, 128 * i:128 * i + 128] * gain[i:i + 1, :] for i in range(values.shape[1] // 128)
        ]
        each = len(chunks) // 4
        quarters.append([chunks[each * q:each * q + each] for q in range(4)])
    sent = []
    for core in range(NC):
        rows = [quarters[0][2 * core + p] + quarters[1][2 * core + p] for p in range(2)]
        for i, pair in enumerate(zip(*rows)):
            block_ref[core, :, 128 * i:128 * i + 128] = jnp.concatenate(pair).astype(jnp.bfloat16)
        for dest in range(core, out_ref.shape[0], NC):
            sent.append(pltpu.make_async_copy(block_ref.at[core], out_ref.at[dest], out_sems.at[dest]))
            sent[-1].start()
    for copy in sent:
        copy.wait()


def quarters_apart(part):
    groups = part.reshape(part.shape[0] // 32, 2, 16, part.shape[1])
    even, odd = groups[:, 0], groups[:, 1]
    first = lax.broadcasted_iota(jnp.int32, even.shape, 1) % 8 < 4
    down = pltpu.roll(odd, 4, 1)
    up = pltpu.roll(even, 12, 1)
    apart = jnp.where(first, even, down), jnp.where(first, up, odd)
    return [x.reshape(part.shape[0] // 2, part.shape[1]) for x in apart]


def half_sums(core, part_ref, head_refs, acc_ref):
    low = 0
    for model, head in enumerate(head_refs):
        size = head.shape[1] // 4
        total = None
        for p, rows in enumerate(quarters_apart(part_ref[:, low:low + size])):
            columns = pl.ds(pl.multiple_of((2 * core + p) * size, 128), size)
            product = lax.dot_general(
                rows, head[:, columns], (((1,), (1,)), ((), ())), preferred_element_type=jnp.float32
            )
            total = product if total is None else total + product
        acc_ref[model] = total
        low += size


def first_kernel(pos_ref, part_ref, he_ref, ha_ref, out_ref):
    half_sums(pos_ref[0], part_ref, (he_ref, ha_ref), out_ref)


def second_kernel(
    pos_ref, part_ref, he_ref, ha_ref, first_ref, live_ref, ids_ref, _, out_ref, acc_ref
):
    beams, width = ids_ref.shape[0], he_ref.shape[0]
    half_sums(1 - pos_ref[0], part_ref, (he_ref, ha_ref), acc_ref)
    hits = ids_ref[...] == pos_ref[1] + lax.broadcasted_iota(jnp.int32, (1, width), 1)
    live = live_ref[...] == 1
    half = width // 2
    tiles = (beams // 8, 8, 128)
    upper = lax.broadcasted_iota(jnp.int32, tiles, 1) < 4
    for model in range(2):
        logits = first_ref[model] + acc_ref[model]
        pick = jnp.sum(jnp.where(hits, logits, 0.0), axis=1, keepdims=True)
        pick = jnp.broadcast_to(pick, (beams, 128 - half))
        held = jnp.where(live, logits, masked_floor)
        left = jnp.concatenate([held[:, :half], pick], axis=1).reshape(tiles)
        right = jnp.concatenate([held[:, half:], pick], axis=1).reshape(tiles)
        low_owner = jnp.where(upper, left, pltpu.roll(right, 4, 1))
        high_owner = jnp.where(upper, pltpu.roll(left, 4, 1), right)
        lanes = slice(128 * model, 128 * model + 128)
        for tile in range(tiles[0]):
            owner = 4 * (tile // 2) + tile % 2
            out_ref[owner, :, lanes] = low_owner[tile]
            out_ref[owner + 2, :, lanes] = high_owner[tile]


def lanes_of(columns, shape):
    lane = lax.broadcasted_iota(jnp.int32, shape, len(shape) - 1)
    result = jnp.zeros(shape, jnp.float32)
    for i, column in enumerate(columns):
        result = jnp.where(lane == i, column, result)
    return result


def lane_at(values, i):
    lane = lax.broadcasted_iota(jnp.int32, values.shape, values.ndim - 1)
    return jnp.sum(jnp.where(lane == i, values, 0.0), axis=-1, keepdims=True)


def total_rows(values):
    return jnp.sum(values, axis=1, keepdims=True)


def insert(levels, entry):
    for i, level in enumerate(levels):
        above = entry[0] > level[0]
        levels[i] = tuple(jnp.where(above, new, old) for new, old in zip(entry, level))
        entry = tuple(jnp.where(above, old, new) for new, old in zip(entry, level))


def remove_top(levels, top):
    hit = levels[0][0] == top
    payload = [total_rows(jnp.where(hit, field, 0.0)) for field in levels[0][1:]]
    count = total_rows(jnp.where(hit, 1.0, 0.0))
    last = tuple(jnp.full_like(f, masked_floor) for f in levels[0])
    lower = levels[1:] + [last]
    return payload, count, [
        tuple(jnp.where(hit, new, old) for new, old in zip(low, level))
        for low, level in zip(lower, levels)
    ]


def stats_kernel(width, table_ref, gap_ref, out_ref):
    sources, own = table_ref.shape[0], table_ref.shape[1] // 2
    shape = (2 * own, 128)
    real = lax.broadcasted_iota(jnp.int32, shape, 1) < width // 2
    columns = []
    for model in range(2):
        parts = [table_ref[i, :, 128 * model:128 * model + 128] for i in range(sources)]
        peak = functools.reduce(jnp.maximum, parts)
        peak = jnp.max(jnp.where(real, peak, masked_floor), axis=1, keepdims=True)
        peak = jnp.maximum(peak[:own], peak[own:])
        both = jnp.concatenate([peak, peak])
        total = functools.reduce(jnp.add, [jnp.exp(part - both) for part in parts])
        total = total_rows(jnp.where(real, total, 0.0))
        pick = lane_at(functools.reduce(jnp.add, parts), width // 2)
        columns.append((peak, total[:own] + total[own:], pick[:own]))
    (pe, te, ce), (pa, ta, ca) = columns
    least = pe - gap_ref[...].astype(jnp.float32) * 0.1
    least = jnp.concatenate([least, least])
    floor = jnp.full(shape, masked_floor, jnp.float32)
    near, rest = [(floor,) * 2] * TOP, [(floor,) * 3] * TOP
    count = jnp.zeros(shape, jnp.float32)
    for i in range(sources):
        e, a = table_ref[i, :, 0:128], table_ref[i, :, 128:256]
        live = real & (e > dead_below)
        is_near = live & (e >= least)
        count += jnp.where(is_near, 1.0, 0.0)
        insert(near, (jnp.where(is_near, e, masked_floor), a))
        insert(rest, (jnp.where(live & (e < least), 3.0 * e - a, masked_floor), e, a))
    missing = total_rows(count)
    picked = []
    for _ in range(NEAR):
        top = jnp.max(near[0][0], axis=1, keepdims=True)
        (a,), hits, near = remove_top(near, top)
        found = top > dead_below
        picked.append((jnp.where(found, top, masked_floor), a))
        missing -= jnp.where(found & (hits == 1.0), 1.0, 0.0)
    for _ in range(TOP):
        top = jnp.max(rest[0][0], axis=1, keepdims=True)
        (e, a), hits, rest = remove_top(rest, top)
        found = top > dead_below
        picked.append((jnp.where(found, e, masked_floor), a))
        missing += jnp.where(found & (hits > 1.0), 1.0, 0.0)
    zeros = [jnp.zeros_like(missing)]
    lanes = zeros * FIRST + [e for e, _ in picked]
    lanes += zeros * (64 + FIRST - len(lanes)) + [a for _, a in picked]
    lanes = lanes_of(lanes, shape)
    stats = lanes_of([pe, pa, te, ta, ce, ca, missing[:own] + missing[own:]], (own, 128))
    stats += lanes[:own] + pltpu.roll(lanes, len(picked), 1)[own:]
    for plane in range(out_ref.shape[0]):
        out_ref[plane] = stats


def best_of(levels):
    tops, counts, seen = [], [], 0.0
    for _ in range(TOP):
        top = jnp.max(levels[0], axis=1, keepdims=True)
        hit = levels[0] == top
        seen = seen + total_rows(jnp.where(hit, 1.0, 0.0))
        tops.append(top)
        counts.append(seen)
        lower = levels[1:] + [jnp.full_like(levels[0], -jnp.inf)]
        levels = [jnp.where(hit, low, level) for level, low in zip(levels, lower)]
    found = []
    for i in range(TOP):
        value = tops[-1]
        for top, seen in reversed(list(zip(tops, counts))):
            value = jnp.where(seen > i, top, value)
        found.append(value)
    return found


def sorted_levels(parts):
    levels = [jnp.full_like(parts[0], -jnp.inf)] * TOP
    for part in parts:
        for i in range(TOP):
            levels[i], part = jnp.maximum(levels[i], part), jnp.minimum(levels[i], part)
    return levels


def row_from(column):
    shape = (column.shape[0], column.shape[0])
    here = lax.broadcasted_iota(jnp.int32, shape, 0) == lax.broadcasted_iota(jnp.int32, shape, 1)
    return jnp.sum(jnp.where(here, column, 0.0), axis=0, keepdims=True)


def totals_of(stats_ref, gap_ref, copies=1):
    stats = stats_ref[...]
    peak_e, peak_a, sum_e, sum_a = [lane_at(stats, i) for i in range(4)]

    def total_of(peaks, sums):
        peak = jnp.max(peaks, axis=0)
        return peak, peak + jnp.log(jnp.sum(sums * jnp.exp(peaks - peak[None]), axis=0))

    peak_e, log_total_e = total_of(peak_e, sum_e)
    peak_a, log_total_a = total_of(peak_a, sum_a)
    cut = peak_e - log_total_e - gap_ref[...].astype(jnp.float32) * 0.1
    shift_e, shift_a, cuts = [
        jnp.concatenate([x] * copies) if copies > 1 else x for x in (log_total_e, log_total_a, cut)
    ]

    def score(logits_e, logits_a):
        logprob_e = logits_e - shift_e
        logprob_a = logits_a - shift_a
        return logprob_e - logprob_a - penalty_slope * jnp.maximum(cuts - logprob_e, 0.0)

    return [peak_e - log_total_e, peak_a - log_total_a], score


def finish_kernel(stats_ref, gap_ref, top_ref, peaks_ref, chosen_ref, lacking_ref):
    peaks, score = totals_of(stats_ref, gap_ref)
    stats = stats_ref[...]
    for i, peak in enumerate(peaks):
        peaks_ref[i:i + 1, :] = row_from(peak)
    picks = [jnp.sum(lane_at(stats, i), axis=0) for i in (4, 5)]
    chosen_ref[...] = row_from(score(*picks))
    lane = lax.broadcasted_iota(jnp.int32, stats.shape[1:], 1)
    is_candidate = (lane >= FIRST) & (lane < FIRST + 2 * (NEAR + TOP))
    parts, lacking = [], jnp.zeros(stats.shape[1:], jnp.float32)
    for plane in range(stats.shape[0]):
        e, a = stats[plane], pltpu.roll(stats[plane], 64, 1)
        value = jnp.where(e > dead_below, score(e, a), masked_floor)
        parts.append(jnp.where(is_candidate, value, -jnp.inf))
        lacking = jnp.maximum(lacking, jnp.where(lane == 6, e, 0.0))
    top_ref[...] = lanes_of(best_of(sorted_levels(parts)), top_ref.shape)
    lacking_ref[0] = jnp.where(jnp.max(lacking) > 0.0, 1, 0).astype(jnp.int32)


def score_kernel(width, table_ref, stats_ref, gap_ref, best_ref):
    _, score = totals_of(stats_ref, gap_ref, 2)
    own = table_ref.shape[1] // 2
    real = lax.broadcasted_iota(jnp.int32, (2 * own, 128), 1) < width // 2
    parts = []
    for source in range(table_ref.shape[0]):
        e, a = table_ref[source, :, 0:128], table_ref[source, :, 128:256]
        parts.append(jnp.where(real & (e > dead_below), score(e, a), masked_floor))
    found = best_of(sorted_levels(parts))
    found = [value[:own] for value in found] + [value[own:] for value in found]
    best = lanes_of(found, best_ref.shape[1:])
    for plane in range(best_ref.shape[0]):
        best_ref[plane] = best


def merge_kernel(parts_ref, out_ref):
    shape = parts_ref.shape[1:]
    real = lax.broadcasted_iota(jnp.int32, shape, 1) < 2 * TOP
    parts = [jnp.where(real, parts_ref[i], -jnp.inf) for i in range(parts_ref.shape[0])]
    out_ref[...] = lanes_of(best_of(sorted_levels(parts)), out_ref.shape)


def per_device(
    expert_hidden,
    expert_gain,
    expert_head,
    amateur_hidden,
    amateur_gain,
    amateur_head,
    live_mask,
    token_ids,
    plaus_level,
):
    own, depth_e = expert_hidden.shape
    depth_a = amateur_hidden.shape[1]
    width = expert_head.shape[0]
    rows, planes = lax.axis_size("rows"), lax.axis_size("vocab")
    beams = own * rows
    quarter = (depth_e + depth_a) // 4
    row, plane = lax.axis_index("rows"), lax.axis_index("vocab")
    position = jnp.stack([row % NC, (row * planes + plane) * width]).astype(jnp.int32)
    middle = rows // 2 + rows // 8
    order = [(middle + r) % rows for r in range(rows)]
    ids = jnp.roll(token_ids, -middle * own)
    ids = ids.reshape(rows // 4, 2, 2, own).swapaxes(1, 2).reshape(beams, 1)
    gap = lax.dynamic_slice_in_dim(plaus_level, row * own, own, 0).reshape(own, 1)

    norm_inputs = (
        expert_hidden, expert_gain.reshape(-1, 128), amateur_hidden, amateur_gain.reshape(-1, 128)
    )
    blocks = pl.pallas_call(
        norm_kernel,
        out_shape=jax.ShapeDtypeStruct((rows, 2 * own, quarter), jnp.bfloat16),
        in_specs=[HBM] * 4,
        out_specs=HBM,
        scratch_shapes=[pltpu.VMEM(x.shape, x.dtype) for x in norm_inputs] + [
            pltpu.VMEM((NC, 2 * own, quarter), jnp.bfloat16),
            pltpu.SemaphoreType.DMA((4,)),
            pltpu.SemaphoreType.DMA((rows,)),
        ],
        compiler_params=WIDE_PARAMS,
        name="norms",
    )(*norm_inputs)
    blocks, expert_head, amateur_head = lax.optimization_barrier(
        (blocks, expert_head, amateur_head)
    )
    half = lax.all_to_all(blocks, "rows", 0, 0, tiled=True, axis_index_groups=[order]).reshape(2 * beams, quarter)
    other_half = lax.ppermute(half, "rows", [(r, r ^ 1) for r in range(rows)])
    cost = pl.CostEstimate(
        flops=4 * beams * width * 2 * quarter, bytes_accessed=4 * beams * quarter, transcendentals=0
    )
    first = pl.pallas_call(
        first_kernel,
        out_shape=jax.ShapeDtypeStruct((2, beams, width), jnp.float32),
        in_specs=[SMEM] + [VMEM] * 3,
        out_specs=VMEM,
        compiler_params=PARAMS,
        cost_estimate=cost,
        name="first_half",
    )(position, half, expert_head, amateur_head)
    table = pl.pallas_call(
        second_kernel,
        out_shape=jax.ShapeDtypeStruct((rows, 2 * own, 256), jnp.float32),
        in_specs=[SMEM] + [VMEM] * 7,
        out_specs=VMEM,
        scratch_shapes=[pltpu.VMEM((2, beams, width), jnp.float32)],
        compiler_params=PARAMS,
        cost_estimate=cost,
        name="second_half",
    )(position, other_half, expert_head, amateur_head, first, live_mask.reshape(1, -1), ids, gap)
    table = lax.all_to_all(table, "rows", 0, 0, tiled=True, axis_index_groups=[order])

    small = jax.ShapeDtypeStruct((planes, own, 128), jnp.float32)
    best_shape = jax.ShapeDtypeStruct((own, TOP), jnp.float32)
    stats = pl.pallas_call(
        functools.partial(stats_kernel, width),
        out_shape=small,
        in_specs=[VMEM] * 2,
        out_specs=VMEM,
        compiler_params=PARAMS,
        name="stats",
    )(table, gap)
    around = [[(planes // 2 + z) % planes for z in range(planes)]]
    stats = lax.all_to_all(stats, "vocab", 0, 0, tiled=True, axis_index_groups=around)
    top, peaks, chosen, lacking = pl.pallas_call(
        finish_kernel,
        out_shape=(
            best_shape,
            jax.ShapeDtypeStruct((2, own), jnp.float32),
            jax.ShapeDtypeStruct((1, own), jnp.float32),
            jax.ShapeDtypeStruct((1,), jnp.int32),
        ),
        in_specs=[VMEM] * 2,
        out_specs=(VMEM, VMEM, VMEM, SMEM),
        compiler_params=PARAMS,
        name="finish",
    )(stats, gap)

    def with_every_entry(table, stats, gap, _):
        best = pl.pallas_call(
            functools.partial(score_kernel, width),
            out_shape=small,
            in_specs=[VMEM] * 3,
            out_specs=VMEM,
            compiler_params=PARAMS,
            name="scores",
        )(table, stats, gap)
        best = lax.all_to_all(best, "vocab", 0, 0, tiled=True)
        return pl.pallas_call(
            merge_kernel,
            out_shape=best_shape,
            in_specs=[VMEM],
            out_specs=VMEM,
            compiler_params=PARAMS,
            name="merge",
        )(best)

    top = lax.cond(lacking[0] > 0, with_every_entry, lambda *args: args[-1], table, stats, gap, top)
    return top, peaks.T, chosen.reshape(own)


def solution(mesh):
    in_specs = (
        P("rows", None),
        P(),
        P(("rows", "vocab"), None),
        P("rows", None),
        P(),
        P(("rows", "vocab"), None),
        P(("rows", "vocab")),
        P(),
        P(),
    )
    out_specs = (P("rows", None), P("rows", None), P("rows"))
    return jax.shard_map(
        per_device, mesh=mesh, in_specs=in_specs, out_specs=out_specs, check_vma=False
    )
```

```python
import functools

import jax
import jax.numpy as jnp
from jax import lax
from jax.experimental import pallas as pl
from jax.experimental.pallas import tpu as pltpu
from jax.sharding import PartitionSpec as P

TOP = 4
NEAR = 20
FIRST = 16
NC = 2

masked_floor = -1e30
dead_below = -5e29
penalty_slope = 2.0
norm_epsilon = 1e-06

VMEM = pl.BlockSpec(memory_space=pltpu.VMEM)
HBM = pl.BlockSpec(memory_space=pltpu.HBM)
SMEM = pl.BlockSpec(memory_space=pltpu.SMEM)
WIDE_PARAMS = pltpu.CompilerParams(vmem_limit_bytes=60 * 1024 * 1024)
PARAMS = pltpu.CompilerParams(vmem_limit_bytes=16 * 1024 * 1024)


def norm_kernel(*refs):
    inputs, out_ref, held, block_ref, sems, out_sems = refs[:4], refs[4], refs[5:9], *refs[9:]
    copies = [pltpu.make_async_copy(inputs[i], held[i], sems.at[i]) for i in range(4)]
    for copy in copies:
        copy.start()
    quarters = []
    for model in range(2):
        copies[2 * model].wait()
        copies[2 * model + 1].wait()
        values = held[2 * model][...].astype(jnp.float32)
        gain = held[2 * model + 1][...].astype(jnp.float32)
        mean = jnp.mean(values * values, axis=-1, keepdims=True)
        values = values * lax.rsqrt(mean + norm_epsilon)
        chunks = [
            values[:, 128 * i:128 * i + 128] * gain[i:i + 1, :] for i in range(values.shape[1] // 128)
        ]
        each = len(chunks) // 4
        quarters.append([chunks[each * q:each * q + each] for q in range(4)])
    sent = []
    for core in range(NC):
        rows = [quarters[0][2 * core + p] + quarters[1][2 * core + p] for p in range(2)]
        for i, pair in enumerate(zip(*rows)):
            block_ref[core, :, 128 * i:128 * i + 128] = jnp.concatenate(pair).astype(jnp.bfloat16)
        for dest in range(core, out_ref.shape[0], NC):
            sent.append(pltpu.make_async_copy(block_ref.at[core], out_ref.at[dest], out_sems.at[dest]))
            sent[-1].start()
    for copy in sent:
        copy.wait()


def quarters_apart(part):
    groups = part.reshape(part.shape[0] // 32, 2, 16, part.shape[1])
    even, odd = groups[:, 0], groups[:, 1]
    first = lax.broadcasted_iota(jnp.int32, even.shape, 1) % 8 < 4
    down = pltpu.roll(odd, 4, 1)
    up = pltpu.roll(even, 12, 1)
    apart = jnp.where(first, even, down), jnp.where(first, up, odd)
    return [x.reshape(part.shape[0] // 2, part.shape[1]) for x in apart]


def half_sums(core, part, head, low):
    size = head.shape[1] // 4
    total = None
    for p, rows in enumerate(quarters_apart(part[:, low:low + size])):
        columns = pl.ds(pl.multiple_of((2 * core + p) * size, 128), size)
        product = lax.dot_general(
            rows, head[:, columns], (((1,), (1,)), ((), ())), preferred_element_type=jnp.float32
        )
        total = product if total is None else total + product
    return total


def first_kernel(pos_ref, part_ref, he_ref, out_ref, rest_ref):
    out_ref[...] = half_sums(pos_ref[0], part_ref, he_ref, 0)
    rest_ref[...] = part_ref[:, he_ref.shape[1] // 4:]


def second_kernel(
    pos_ref, part_ref, he_ref, ha_ref, first_ref, rest_ref, live_ref, ids_ref, _, out_ref, acc_ref
):
    beams, width = ids_ref.shape[0], he_ref.shape[0]
    mine, other = pos_ref[0], 1 - pos_ref[0]
    acc_ref[0] = first_ref[...] + half_sums(other, part_ref, he_ref, 0)
    acc_ref[1] = half_sums(mine, rest_ref, ha_ref, 0)
    acc_ref[1] += half_sums(other, part_ref, ha_ref, he_ref.shape[1] // 4)
    hits = ids_ref[...] == pos_ref[1] + lax.broadcasted_iota(jnp.int32, (1, width), 1)
    live = live_ref[...] == 1
    half = width // 2
    tiles = (beams // 8, 8, 128)
    upper = lax.broadcasted_iota(jnp.int32, tiles, 1) < 4
    for model in range(2):
        logits = acc_ref[model]
        pick = jnp.sum(jnp.where(hits, logits, 0.0), axis=1, keepdims=True)
        pick = jnp.broadcast_to(pick, (beams, 128 - half))
        held = jnp.where(live, logits, masked_floor)
        left = jnp.concatenate([held[:, :half], pick], axis=1).reshape(tiles)
        right = jnp.concatenate([held[:, half:], pick], axis=1).reshape(tiles)
        low_owner = jnp.where(upper, left, pltpu.roll(right, 4, 1))
        high_owner = jnp.where(upper, pltpu.roll(left, 4, 1), right)
        lanes = slice(128 * model, 128 * model + 128)
        for tile in range(tiles[0]):
            owner = 4 * (tile // 2) + tile % 2
            out_ref[owner, :, lanes] = low_owner[tile]
            out_ref[owner + 2, :, lanes] = high_owner[tile]


def lanes_of(columns, shape):
    lane = lax.broadcasted_iota(jnp.int32, shape, len(shape) - 1)
    result = jnp.zeros(shape, jnp.float32)
    for i, column in enumerate(columns):
        result = jnp.where(lane == i, column, result)
    return result


def lane_at(values, i):
    lane = lax.broadcasted_iota(jnp.int32, values.shape, values.ndim - 1)
    return jnp.sum(jnp.where(lane == i, values, 0.0), axis=-1, keepdims=True)


def total_rows(values):
    return jnp.sum(values, axis=1, keepdims=True)


def insert(levels, entry):
    for i, level in enumerate(levels):
        above = entry[0] > level[0]
        levels[i] = tuple(jnp.where(above, new, old) for new, old in zip(entry, level))
        entry = tuple(jnp.where(above, old, new) for new, old in zip(entry, level))


def remove_top(levels, top):
    hit = levels[0][0] == top
    payload = [total_rows(jnp.where(hit, field, 0.0)) for field in levels[0][1:]]
    count = total_rows(jnp.where(hit, 1.0, 0.0))
    last = tuple(jnp.full_like(f, masked_floor) for f in levels[0])
    lower = levels[1:] + [last]
    return payload, count, [
        tuple(jnp.where(hit, new, old) for new, old in zip(low, level))
        for low, level in zip(lower, levels)
    ]


def stats_kernel(width, table_ref, gap_ref, out_ref):
    sources, own = table_ref.shape[0], table_ref.shape[1] // 2
    shape = (2 * own, 128)
    real = lax.broadcasted_iota(jnp.int32, shape, 1) < width // 2
    columns = []
    for model in range(2):
        parts = [table_ref[i, :, 128 * model:128 * model + 128] for i in range(sources)]
        peak = functools.reduce(jnp.maximum, parts)
        peak = jnp.max(jnp.where(real, peak, masked_floor), axis=1, keepdims=True)
        peak = jnp.maximum(peak[:own], peak[own:])
        both = jnp.concatenate([peak, peak])
        total = functools.reduce(jnp.add, [jnp.exp(part - both) for part in parts])
        total = total_rows(jnp.where(real, total, 0.0))
        pick = lane_at(functools.reduce(jnp.add, parts), width // 2)
        columns.append((peak, total[:own] + total[own:], pick[:own]))
    (pe, te, ce), (pa, ta, ca) = columns
    least = pe - gap_ref[...].astype(jnp.float32) * 0.1
    least = jnp.concatenate([least, least])
    floor = jnp.full(shape, masked_floor, jnp.float32)
    near, rest = [(floor,) * 2] * TOP, [(floor,) * 3] * TOP
    count = jnp.zeros(shape, jnp.float32)
    for i in range(sources):
        e, a = table_ref[i, :, 0:128], table_ref[i, :, 128:256]
        live = real & (e > dead_below)
        is_near = live & (e >= least)
        count += jnp.where(is_near, 1.0, 0.0)
        insert(near, (jnp.where(is_near, e, masked_floor), a))
        insert(rest, (jnp.where(live & (e < least), 3.0 * e - a, masked_floor), e, a))
    missing = total_rows(count)
    picked = []
    for _ in range(NEAR):
        top = jnp.max(near[0][0], axis=1, keepdims=True)
        (a,), hits, near = remove_top(near, top)
        found = top > dead_below
        picked.append((jnp.where(found, top, masked_floor), a))
        missing -= jnp.where(found & (hits == 1.0), 1.0, 0.0)
    for _ in range(TOP):
        top = jnp.max(rest[0][0], axis=1, keepdims=True)
        (e, a), hits, rest = remove_top(rest, top)
        found = top > dead_below
        picked.append((jnp.where(found, e, masked_floor), a))
        missing += jnp.where(found & (hits > 1.0), 1.0, 0.0)
    zeros = [jnp.zeros_like(missing)]
    lanes = zeros * FIRST + [e for e, _ in picked]
    lanes += zeros * (64 + FIRST - len(lanes)) + [a for _, a in picked]
    lanes = lanes_of(lanes, shape)
    stats = lanes_of([pe, pa, te, ta, ce, ca, missing[:own] + missing[own:]], (own, 128))
    stats += lanes[:own] + pltpu.roll(lanes, len(picked), 1)[own:]
    for plane in range(out_ref.shape[0]):
        out_ref[plane] = stats


def best_of(levels):
    tops, counts, seen = [], [], 0.0
    for _ in range(TOP):
        top = jnp.max(levels[0], axis=1, keepdims=True)
        hit = levels[0] == top
        seen = seen + total_rows(jnp.where(hit, 1.0, 0.0))
        tops.append(top)
        counts.append(seen)
        lower = levels[1:] + [jnp.full_like(levels[0], -jnp.inf)]
        levels = [jnp.where(hit, low, level) for level, low in zip(levels, lower)]
    found = []
    for i in range(TOP):
        value = tops[-1]
        for top, seen in reversed(list(zip(tops, counts))):
            value = jnp.where(seen > i, top, value)
        found.append(value)
    return found


def sorted_levels(parts):
    levels = [jnp.full_like(parts[0], -jnp.inf)] * TOP
    for part in parts:
        for i in range(TOP):
            levels[i], part = jnp.maximum(levels[i], part), jnp.minimum(levels[i], part)
    return levels


def row_from(column):
    shape = (column.shape[0], column.shape[0])
    here = lax.broadcasted_iota(jnp.int32, shape, 0) == lax.broadcasted_iota(jnp.int32, shape, 1)
    return jnp.sum(jnp.where(here, column, 0.0), axis=0, keepdims=True)


def totals_of(stats_ref, gap_ref, copies=1):
    stats = stats_ref[...]
    peak_e, peak_a, sum_e, sum_a = [lane_at(stats, i) for i in range(4)]

    def total_of(peaks, sums):
        peak = jnp.max(peaks, axis=0)
        return peak, peak + jnp.log(jnp.sum(sums * jnp.exp(peaks - peak[None]), axis=0))

    peak_e, log_total_e = total_of(peak_e, sum_e)
    peak_a, log_total_a = total_of(peak_a, sum_a)
    cut = peak_e - log_total_e - gap_ref[...].astype(jnp.float32) * 0.1
    shift_e, shift_a, cuts = [
        jnp.concatenate([x] * copies) if copies > 1 else x for x in (log_total_e, log_total_a, cut)
    ]

    def score(logits_e, logits_a):
        logprob_e = logits_e - shift_e
        logprob_a = logits_a - shift_a
        return logprob_e - logprob_a - penalty_slope * jnp.maximum(cuts - logprob_e, 0.0)

    return [peak_e - log_total_e, peak_a - log_total_a], score


def finish_kernel(stats_ref, gap_ref, top_ref, peaks_ref, chosen_ref, lacking_ref):
    peaks, score = totals_of(stats_ref, gap_ref)
    stats = stats_ref[...]
    for i, peak in enumerate(peaks):
        peaks_ref[i:i + 1, :] = row_from(peak)
    picks = [jnp.sum(lane_at(stats, i), axis=0) for i in (4, 5)]
    chosen_ref[...] = row_from(score(*picks))
    lane = lax.broadcasted_iota(jnp.int32, stats.shape[1:], 1)
    is_candidate = (lane >= FIRST) & (lane < FIRST + 2 * (NEAR + TOP))
    parts, lacking = [], jnp.zeros(stats.shape[1:], jnp.float32)
    for plane in range(stats.shape[0]):
        e, a = stats[plane], pltpu.roll(stats[plane], 64, 1)
        value = jnp.where(e > dead_below, score(e, a), masked_floor)
        parts.append(jnp.where(is_candidate, value, -jnp.inf))
        lacking = jnp.maximum(lacking, jnp.where(lane == 6, e, 0.0))
    top_ref[...] = lanes_of(best_of(sorted_levels(parts)), top_ref.shape)
    lacking_ref[0] = jnp.where(jnp.max(lacking) > 0.0, 1, 0).astype(jnp.int32)


def score_kernel(width, table_ref, stats_ref, gap_ref, best_ref):
    _, score = totals_of(stats_ref, gap_ref, 2)
    own = table_ref.shape[1] // 2
    real = lax.broadcasted_iota(jnp.int32, (2 * own, 128), 1) < width // 2
    parts = []
    for source in range(table_ref.shape[0]):
        e, a = table_ref[source, :, 0:128], table_ref[source, :, 128:256]
        parts.append(jnp.where(real & (e > dead_below), score(e, a), masked_floor))
    found = best_of(sorted_levels(parts))
    found = [value[:own] for value in found] + [value[own:] for value in found]
    best = lanes_of(found, best_ref.shape[1:])
    for plane in range(best_ref.shape[0]):
        best_ref[plane] = best


def merge_kernel(parts_ref, out_ref):
    shape = parts_ref.shape[1:]
    real = lax.broadcasted_iota(jnp.int32, shape, 1) < 2 * TOP
    parts = [jnp.where(real, parts_ref[i], -jnp.inf) for i in range(parts_ref.shape[0])]
    out_ref[...] = lanes_of(best_of(sorted_levels(parts)), out_ref.shape)


def per_device(
    expert_hidden,
    expert_gain,
    expert_head,
    amateur_hidden,
    amateur_gain,
    amateur_head,
    live_mask,
    token_ids,
    plaus_level,
):
    own, depth_e = expert_hidden.shape
    depth_a = amateur_hidden.shape[1]
    width = expert_head.shape[0]
    rows, planes = lax.axis_size("rows"), lax.axis_size("vocab")
    beams = own * rows
    quarter = (depth_e + depth_a) // 4
    row, plane = lax.axis_index("rows"), lax.axis_index("vocab")
    position = jnp.stack([row % NC, (row * planes + plane) * width]).astype(jnp.int32)
    middle = rows // 2 + rows // 8
    order = [(middle + r) % rows for r in range(rows)]
    ids = jnp.roll(token_ids, -middle * own)
    ids = ids.reshape(rows // 4, 2, 2, own).swapaxes(1, 2).reshape(beams, 1)
    gap = lax.dynamic_slice_in_dim(plaus_level, row * own, own, 0).reshape(own, 1)

    norm_inputs = (
        expert_hidden, expert_gain.reshape(-1, 128), amateur_hidden, amateur_gain.reshape(-1, 128)
    )
    blocks = pl.pallas_call(
        norm_kernel,
        out_shape=jax.ShapeDtypeStruct((rows, 2 * own, quarter), jnp.bfloat16),
        in_specs=[HBM] * 4,
        out_specs=HBM,
        scratch_shapes=[pltpu.VMEM(x.shape, x.dtype) for x in norm_inputs] + [
            pltpu.VMEM((NC, 2 * own, quarter), jnp.bfloat16),
            pltpu.SemaphoreType.DMA((4,)),
            pltpu.SemaphoreType.DMA((rows,)),
        ],
        compiler_params=WIDE_PARAMS,
        name="norms",
    )(*norm_inputs)
    blocks, expert_head, amateur_head = lax.optimization_barrier(
        (blocks, expert_head, amateur_head)
    )
    half = lax.all_to_all(blocks, "rows", 0, 0, tiled=True, axis_index_groups=[order]).reshape(2 * beams, quarter)
    other_half = lax.ppermute(half, "rows", [(r, r ^ 1) for r in range(rows)])
    cost = pl.CostEstimate(
        flops=4 * beams * width * 2 * quarter, bytes_accessed=4 * beams * quarter, transcendentals=0
    )
    first, rest = pl.pallas_call(
        first_kernel,
        out_shape=(
            jax.ShapeDtypeStruct((beams, width), jnp.float32),
            jax.ShapeDtypeStruct((2 * beams, depth_a // 4), jnp.bfloat16),
        ),
        in_specs=[SMEM] + [VMEM] * 2,
        out_specs=(VMEM, VMEM),
        compiler_params=PARAMS,
        cost_estimate=cost,
        name="first_half",
    )(position, half, expert_head)
    table = pl.pallas_call(
        second_kernel,
        out_shape=jax.ShapeDtypeStruct((rows, 2 * own, 256), jnp.float32),
        in_specs=[SMEM] + [VMEM] * 8,
        out_specs=VMEM,
        scratch_shapes=[pltpu.VMEM((2, beams, width), jnp.float32)],
        compiler_params=PARAMS,
        cost_estimate=cost,
        name="second_half",
    )(position, other_half, expert_head, amateur_head, first, rest, live_mask.reshape(1, -1), ids, gap)
    table = lax.all_to_all(table, "rows", 0, 0, tiled=True, axis_index_groups=[order])

    small = jax.ShapeDtypeStruct((planes, own, 128), jnp.float32)
    best_shape = jax.ShapeDtypeStruct((own, TOP), jnp.float32)
    stats = pl.pallas_call(
        functools.partial(stats_kernel, width),
        out_shape=small,
        in_specs=[VMEM] * 2,
        out_specs=VMEM,
        compiler_params=PARAMS,
        name="stats",
    )(table, gap)
    around = [[(planes // 2 + z) % planes for z in range(planes)]]
    stats = lax.all_to_all(stats, "vocab", 0, 0, tiled=True, axis_index_groups=around)
    top, peaks, chosen, lacking = pl.pallas_call(
        finish_kernel,
        out_shape=(
            best_shape,
            jax.ShapeDtypeStruct((2, own), jnp.float32),
            jax.ShapeDtypeStruct((1, own), jnp.float32),
            jax.ShapeDtypeStruct((1,), jnp.int32),
        ),
        in_specs=[VMEM] * 2,
        out_specs=(VMEM, VMEM, VMEM, SMEM),
        compiler_params=PARAMS,
        name="finish",
    )(stats, gap)

    def with_every_entry(table, stats, gap, _):
        best = pl.pallas_call(
            functools.partial(score_kernel, width),
            out_shape=small,
            in_specs=[VMEM] * 3,
            out_specs=VMEM,
            compiler_params=PARAMS,
            name="scores",
        )(table, stats, gap)
        best = lax.all_to_all(best, "vocab", 0, 0, tiled=True)
        return pl.pallas_call(
            merge_kernel,
            out_shape=best_shape,
            in_specs=[VMEM],
            out_specs=VMEM,
            compiler_params=PARAMS,
            name="merge",
        )(best)

    top = lax.cond(lacking[0] > 0, with_every_entry, lambda *args: args[-1], table, stats, gap, top)
    return top, peaks.T, chosen.reshape(own)


def solution(mesh):
    in_specs = (
        P("rows", None),
        P(),
        P(("rows", "vocab"), None),
        P("rows", None),
        P(),
        P(("rows", "vocab"), None),
        P(("rows", "vocab")),
        P(),
        P(),
    )
    out_specs = (P("rows", None), P("rows", None), P("rows"))
    return jax.shard_map(
        per_device, mesh=mesh, in_specs=in_specs, out_specs=out_specs, check_vma=False
    )
```
